32 devices in a mesh: expert: 8 (over y, x, core), tensor: 4 (over z).
Axes of the slice: x: 2, y: 2, z: 4, core: 2. Of those that a mesh axis runs over, the one named last changes fastest.
Arguments:
- patches: bfloat16 [2, 32, 196, 768], P(None, ('expert', 'tensor')), may hold values from -6 to 6
- cotangent: bfloat16 [2, 32, 196, 768], P(None, ('expert', 'tensor')), may hold values from -6 to 6
- expert_ids: int32 [2, 32, 196, 2], P(None, ('expert', 'tensor')), may hold values from 0 to 7, as said below
- slots: int32 [2, 32, 196, 2], P(None, ('expert', 'tensor')), may hold values from 0 to 52, as said below
- attn_weights: float32 [768, 3072], P(('expert', 'tensor'))
- attn_first: float32 [768, 3072], P(('expert', 'tensor')), may hold values from -768 to 768
- attn_second: float32 [768, 3072], P(('expert', 'tensor')), may hold values from 6272 to 50176
- router_weights: float32 [768, 8], P(('expert', 'tensor')), may hold values from -0.15625 to 0.15625
- router_first: float32 [768, 8], P(('expert', 'tensor')), may hold values from -2048 to 2048
- router_second: float32 [768, 8], P(('expert', 'tensor')), may hold values from 50176 to 451584
- norm_params: float32 [4, 768], P(None, ('expert', 'tensor'))
- norm_first: float32 [4, 768], P(None, ('expert', 'tensor')), may hold values from -2560 to 2560
- norm_second: float32 [4, 768], P(None, ('expert', 'tensor')), may hold values from 100352 to 802816
- w_in: float32 [8, 768, 3072], P('expert', None, 'tensor'), may hold values from -0.21875 to 0.21875
- w_in_first: float32 [8, 768, 3072], P('expert', None, 'tensor'), may hold values from -256 to 256
- w_in_second: float32 [8, 768, 3072], P('expert', None, 'tensor'), may hold values from 2131.5 to 8538.25
- w_in_stat: float32 [8, 8, 384, 384], P('expert', 'tensor'), as said below
- w_in_basis: float32 [8, 8, 384, 384], P('expert', 'tensor'), as said below
- w_out: float32 [8, 3072, 768], P('expert', 'tensor'), may hold values from -2.5 to 2.5
- w_out_first: float32 [8, 3072, 768], P('expert', 'tensor'), may hold values from -28 to 28
- w_out_second: float32 [8, 3072, 768], P('expert', 'tensor'), may hold values from 24.5 to 98
- w_out_stat: float32 [8, 8, 384, 384], P('expert', 'tensor'), as said below
- w_out_basis: float32 [8, 8, 384, 384], P('expert', 'tensor'), as said below
- b_in: float32 [8, 3072], P('expert', 'tensor'), may hold values from -0.625 to 0.625
- b_in_first: float32 [8, 3072], P('expert', 'tensor'), may hold values from -256 to 256
- b_in_second: float32 [8, 3072], P('expert', 'tensor'), may hold values from 2131.5 to 8538.25
- b_out: float32 [8, 768], P('expert', 'tensor'), may hold values from -8 to 8
- b_out_first: float32 [8, 768], P('expert', 'tensor'), may hold values from -48 to 48
- b_out_second: float32 [8, 768], P('expert', 'tensor'), may hold values from 58.8 to 235.2
Outputs:
- block_output: bfloat16 [2, 32, 196, 768], P(None, ('expert', 'tensor'))
- input_grad: float32 [2, 32, 196, 768], P(None, ('expert', 'tensor'))
- attn_first_new: float32 [768, 3072], P(('expert', 'tensor'))
- attn_second_new: float32 [768, 3072], P(('expert', 'tensor'))
- attn_new: float32 [768, 3072], P(('expert', 'tensor'))
- attn_copy: bfloat16 [768, 3072], P(('expert', 'tensor'))
- router_first_new: float32 [768, 8], P(('expert', 'tensor'))
- router_second_new: float32 [768, 8], P(('expert', 'tensor'))
- router_new: float32 [768, 8], P(('expert', 'tensor'))
- router_copy: bfloat16 [768, 8], P(('expert', 'tensor'))
- norm_first_new: float32 [4, 768], P(None, ('expert', 'tensor'))
- norm_second_new: float32 [4, 768], P(None, ('expert', 'tensor'))
- norm_new: float32 [4, 768], P(None, ('expert', 'tensor'))
- w_in_first_new: float32 [8, 768, 3072], P('expert', None, 'tensor')
- w_in_second_new: float32 [8, 768, 3072], P('expert', None, 'tensor')
- w_in_new: float32 [8, 768, 3072], P('expert', None, 'tensor')
- w_in_copy: bfloat16 [8, 768, 3072], P('expert', None, 'tensor')
- w_in_stat_new: float32 [8, 8, 384, 384], P('expert', 'tensor')
- w_in_basis_new: float32 [8, 8, 384, 384], P('expert', 'tensor')
- w_out_first_new: float32 [8, 3072, 768], P('expert', 'tensor')
- w_out_second_new: float32 [8, 3072, 768], P('expert', 'tensor')
- w_out_new: float32 [8, 3072, 768], P('expert', 'tensor')
- w_out_copy: bfloat16 [8, 3072, 768], P('expert', 'tensor')
- w_out_stat_new: float32 [8, 8, 384, 384], P('expert', 'tensor')
- w_out_basis_new: float32 [8, 8, 384, 384], P('expert', 'tensor')
- b_in_first_new: float32 [8, 3072], P('expert', 'tensor')
- b_in_second_new: float32 [8, 3072], P('expert', 'tensor')
- b_in_new: float32 [8, 3072], P('expert', 'tensor')
- b_out_first_new: float32 [8, 768], P('expert', 'tensor')
- b_out_second_new: float32 [8, 768], P('expert', 'tensor')
- b_out_new: float32 [8, 768], P('expert', 'tensor')
The draws below stay inside these ranges and needn't reach their ends.
Inputs may be any that keep to these rules, and one draw needn't show every extreme that they name: `expert_ids`: the 2 experts of a token are distinct. Within one device block (the 196 tokens of one device in one micro-batch) the pairs that name one expert take slots 0, 1, 2 and so on in a priority order in which all first choices come before all second choices; a pair whose turn comes after the expert's 52 slots are taken has slot 52 and is dropped. In every micro-batch some expert has all 52 slots taken in every device block. `w_in_basis`: each 384 x 384 block is orthogonal. `w_out_basis`: each 384 x 384 block is orthogonal. `w_in_stat`: each block is symmetric and positive definite. `w_out_stat`: each block is symmetric and positive definite.
All inputs are finite; a program needn't handle non-finite values.
Results may differ from the reference program's by a relative error of at most 0.038.
Values may be sent and summed in bfloat16 or wider, within the bound.
No kernel may reach another device: no remote copies, remote signals or barrier semaphores. Data moves between devices by JAX's collectives and lax.ppermute only.
A program may use at most 256 MiB of HBM per device.

```python
import math
from functools import partial
import jax
import jax.numpy as jnp
from jax import lax

D = 768
HEADS = 12
HEAD_DIM = 64
FF = 3072
SEQ = 196
TOPK = 2
IMG_DEV = 1
MB = 2
STEP = 10
BLK = 384
EXPERTS = 8
TOK_DEV = 196
IMAGES = 32
CS = 52
PAIRS_EXP = 3136
TOKENS_ALL = 12544
N_EXPERT = 8
N_TENSOR = 4


def route_tables(key):
    folded = jax.random.fold_in(key, 11)
    subkeys = jax.random.split(folded, 6)
    block_count = MB * IMAGES // IMG_DEV
    grid_shape = (block_count, TOK_DEV)
    first_pick = jnp.minimum(jax.random.randint(subkeys[0], grid_shape, 0, EXPERTS), jax.random.randint(subkeys[1], grid_shape, 0, EXPERTS))
    offset = jax.random.randint(subkeys[2], grid_shape, 1, EXPERTS)
    second_pick = (first_pick + offset) % EXPERTS
    labels = jax.random.permutation(subkeys[3], EXPERTS)
    first_label = labels[first_pick]
    second_label = labels[second_pick]
    scores = jax.random.randint(subkeys[4], grid_shape, 0, 1 << 20) * TOK_DEV + jnp.arange(TOK_DEV)[None, :]
    priority = jnp.argsort(jnp.argsort(scores, axis=-1), axis=-1)
    favoured = jax.random.randint(subkeys[5], (MB,), 0, EXPERTS)
    favoured_rows = jnp.repeat(favoured, block_count // MB)[:, None]
    forced = priority <= CS
    first_final = jnp.where(forced, favoured_rows, first_label)
    second_final = jnp.where(forced & (second_label == favoured_rows), first_label, second_label)
    chosen = jnp.stack([first_final, second_final], axis=-1)
    order_key = jnp.stack([priority, priority + TOK_DEV], axis=-1).reshape(block_count, 2 * TOK_DEV)
    flat_chosen = chosen.reshape(block_count, 2 * TOK_DEV)
    sequence = jnp.argsort(order_key, axis=-1)
    sorted_chosen = jnp.take_along_axis(flat_chosen, sequence, axis=-1)
    onehot = (sorted_chosen[:, :, None] == jnp.arange(EXPERTS)[None, None, :]).astype(jnp.int32)
    earlier = jnp.cumsum(onehot, axis=1) - onehot
    sorted_rank = jnp.sum(earlier * onehot, axis=-1)
    slot_rank = jnp.zeros_like(sorted_rank).at[jnp.arange(block_count)[:, None], sequence].set(sorted_rank)
    slot_values = jnp.minimum(slot_rank, CS)
    shape_out = (MB, IMAGES, SEQ, TOPK)
    return (chosen.reshape(shape_out).astype(jnp.int32), slot_values.reshape(shape_out).astype(jnp.int32))


def draw_expert_ids(key, part):
    return route_tables(key)[0]


def draw_slots(key, part):
    return route_tables(key)[1]


def draw_attn_weights(key, part):
    column_scale = jnp.where(jnp.arange(4 * D) < 3 * D, (2.0 / D) ** 0.5, (8.0 / D) ** 0.5)
    subkey = jax.random.fold_in(key, 5)
    entries = jax.random.normal(subkey, (D, 4 * D), jnp.float32)
    return entries * column_scale[None, :]


def draw_norm_params(key, part):
    gain_key, shift_key = jax.random.split(jax.random.fold_in(key, 3))
    gain_rows = jax.random.uniform(gain_key, (4, D), jnp.float32, 0.6, 1.4)
    shift_rows = 0.2 * jax.random.normal(shift_key, (4, D), jnp.float32)
    return jnp.where((jnp.arange(4) % 2 == 0)[:, None], gain_rows, shift_rows)


def stat_draw(key, salt, scale_value):
    diag_key, off_key = jax.random.split(jax.random.fold_in(key, salt))
    shape_full = (EXPERTS, FF // BLK, BLK, BLK)
    diagonal = jnp.exp(jax.random.uniform(diag_key, shape_full[:3], jnp.float32, math.log(1.5), math.log(6.0)))
    entries = jax.random.normal(off_key, shape_full, jnp.float32)
    symmetric = (entries + jnp.swapaxes(entries, -1, -2)) * 0.7071
    eye_mask = jnp.eye(BLK, dtype=bool)
    off_part = jnp.where(eye_mask, 0.0, symmetric) * (3.25 / (5.0 * BLK ** 0.5))
    return scale_value * (jnp.where(eye_mask, diagonal[..., None], 0.0) + off_part)


def draw_w_in_stat(key, part):
    return stat_draw(key, 9, 174.0 * D * D * PAIRS_EXP / FF / EXPERTS ** 2)


def draw_w_out_stat(key, part):
    return stat_draw(key, 19, 0.49 * D * PAIRS_EXP / EXPERTS ** 2)


def basis_draw(key, salt):
    row_key, col_key, sign_key = jax.random.split(jax.random.fold_in(key, salt), 3)
    batch_shape = (EXPERTS, FF // BLK, BLK)
    row_order = jnp.argsort(jax.random.randint(row_key, batch_shape, 0, 1 << 20) * BLK + jnp.arange(BLK), axis=-1)
    col_order = jnp.argsort(jax.random.randint(col_key, batch_shape, 0, 1 << 20) * BLK + jnp.arange(BLK), axis=-1)
    sign_flip = jnp.where(jax.random.randint(sign_key, batch_shape, 0, 2) == 0, -1.0, 1.0)
    frequency = col_order.astype(jnp.float32)[..., None, :]
    position = row_order.astype(jnp.float32)[..., :, None]
    cosines = jnp.cos(math.pi * (2.0 * position + 1.0) * frequency / (2.0 * BLK))
    row_scale = jnp.where(frequency == 0.0, (1.0 / BLK) ** 0.5, (2.0 / BLK) ** 0.5)
    return cosines * row_scale * sign_flip[..., None, :]


def draw_w_in_basis(key, part):
    return basis_draw(key, 13)


def draw_w_out_basis(key, part):
    return basis_draw(key, 17)


def strengthened(values, stream_key, source, target, blocks, factor):
    def block_of(axis_at):
        return (jnp.arange(values.shape[axis_at]) // (values.shape[axis_at] // blocks)).reshape((-1,) + (1,) * (values.ndim - 1 - axis_at))

    near = jax.random.permutation(stream_key, blocks)[block_of(target)]
    other_side = (block_of(target) + blocks // 2) % blocks
    return jnp.where((block_of(source) == near) | (block_of(source) == other_side), factor * values, values)


def shard_levels(own_key, shape, shards, least, top_value):
    level, own = 1.0, jax.random.fold_in(own_key, 6)
    for dim, shards_of in shards:
        draws = jnp.exp(jax.random.uniform(jax.random.fold_in(own, dim), (shards_of,), jnp.float32, least / len(shards), top_value / len(shards)))
        level = level * jnp.repeat(draws, shape[dim] // shards_of).reshape([-1 if axis == dim else 1 for axis in range(len(shape))])
    return level


def noise(own_key, shape, width, reach, cuts=(), held_as=jnp.bfloat16):
    values = jax.random.normal(own_key, shape, jnp.float32) * width
    if len(cuts) > 0:
        values = shard_levels(own_key, shape, cuts, -0.22, 0.18) * values
    return jnp.clip(values, min=-reach, max=reach).astype(held_as)


def gaussian_with(own_key, extent, scale, reach, cuts, heavy, kind=jnp.bfloat16):
    values = scale * jax.random.normal(own_key, extent, jnp.float32)
    if cuts:
        values = values * shard_levels(own_key, extent, cuts, -0.22, 0.18)
    return jnp.clip(strengthened(values, jax.random.fold_in(own_key, 3), *heavy), -reach, reach).astype(kind)


def setup_inputs(seed: int = 0) -> dict:
    arg_keys = jax.random.split(jax.random.key(seed), 30)
    patches = gaussian_with(arg_keys[0], (MB, IMAGES, SEQ, D), 1.0, 6.0, ((1, 32),), (1, 3, 32, 2.75))
    cotangent = noise(arg_keys[1], (MB, IMAGES, SEQ, D), 1.0, 6.0, ((1, 32),))
    expert_ids = draw_expert_ids(jax.random.fold_in(arg_keys[29], 71), 0)
    slots = draw_slots(jax.random.fold_in(arg_keys[29], 71), 0)
    attn_weights = draw_attn_weights(jax.random.fold_in(arg_keys[29], 71), 0)
    attn_first = noise(arg_keys[5], (D, 4 * D), (1.2 * TOKENS_ALL ** 0.5), 768.0, ((0, 32),), jnp.float32)
    attn_second = jnp.clip(jnp.exp(math.log(50176.0) - 2.0794415 * jax.random.uniform(arg_keys[6], (D, 4 * D), jnp.float32) ** shard_levels(arg_keys[6], (D, 4 * D), ((0, 32),), -0.2, 0.2)), 6272.0, 50176.0)
    router_weights = noise(arg_keys[7], (D, EXPERTS), (0.7 / D ** 0.5), 0.15625, ((0, 32),), jnp.float32)
    router_first = noise(arg_keys[8], (D, EXPERTS), (3 * TOKENS_ALL ** 0.5), 2048.0, ((0, 32),), jnp.float32)
    router_second = jnp.clip(jnp.exp(math.log(451584.0) - 2.1972246 * jax.random.uniform(arg_keys[9], (D, EXPERTS), jnp.float32) ** shard_levels(arg_keys[9], (D, EXPERTS), ((0, 32),), -0.2, 0.2)), 50176.0, 451584.0)
    norm_params = draw_norm_params(jax.random.fold_in(arg_keys[29], 71), 0)
    norm_first = noise(arg_keys[11], (4, D), (4 * TOKENS_ALL ** 0.5), 2560.0, ((1, 32),), jnp.float32)
    norm_second = jnp.clip(jnp.exp(math.log(802816.0) - 2.0794415 * jax.random.uniform(arg_keys[12], (4, D), jnp.float32) ** shard_levels(arg_keys[12], (4, D), ((1, 32),), -0.2, 0.2)), 100352.0, 802816.0)
    w_in = noise(arg_keys[13], (EXPERTS, D, FF), D ** -0.5, 0.21875, ((0, 8), (2, 4)), jnp.float32)
    w_in_first = noise(arg_keys[14], (EXPERTS, D, FF), (13.2 * (D * PAIRS_EXP / FF) ** 0.5 / EXPERTS), 256.0, ((0, 8), (2, 4)), jnp.float32)
    w_in_second = jnp.clip(jnp.exp(math.log(8538.25) - 1.3877301 * jax.random.uniform(arg_keys[15], (EXPERTS, D, FF), jnp.float32) ** shard_levels(arg_keys[15], (EXPERTS, D, FF), ((0, 8), (2, 4)), -0.2, 0.2)), 2131.5, 8538.25)
    w_in_stat = draw_w_in_stat(jax.random.fold_in(arg_keys[29], 71), 0)
    w_in_basis = draw_w_in_basis(jax.random.fold_in(arg_keys[29], 71), 0)
    w_out = noise(arg_keys[18], (EXPERTS, FF, D), (24 / FF ** 0.5), 2.5, ((0, 8), (1, 4)), jnp.float32)
    w_out_first = noise(arg_keys[19], (EXPERTS, FF, D), (0.7 * PAIRS_EXP ** 0.5 / EXPERTS), 28.0, ((0, 8), (1, 4)), jnp.float32)
    w_out_second = jnp.clip(jnp.exp(math.log(98.0) - 1.3862944 * jax.random.uniform(arg_keys[20], (EXPERTS, FF, D), jnp.float32) ** shard_levels(arg_keys[20], (EXPERTS, FF, D), ((0, 8), (1, 4)), -0.2, 0.2)), 24.5, 98.0)
    w_out_stat = draw_w_out_stat(jax.random.fold_in(arg_keys[29], 71), 0)
    w_out_basis = draw_w_out_basis(jax.random.fold_in(arg_keys[29], 71), 0)
    b_in = noise(arg_keys[23], (EXPERTS, FF), 0.1, 0.625, ((0, 8), (1, 4)), jnp.float32)
    b_in_first = noise(arg_keys[24], (EXPERTS, FF), (13.2 * (D * PAIRS_EXP / FF) ** 0.5 / EXPERTS), 256.0, ((0, 8), (1, 4)), jnp.float32)
    b_in_second = jnp.clip(jnp.exp(math.log(8538.25) - 1.3877301 * jax.random.uniform(arg_keys[25], (EXPERTS, FF), jnp.float32) ** shard_levels(arg_keys[25], (EXPERTS, FF), ((0, 8), (1, 4)), -0.2, 0.2)), 2131.5, 8538.25)
    b_out = noise(arg_keys[26], (EXPERTS, D), 1.5, 8.0, ((0, 8), (1, 4)), jnp.float32)
    b_out_first = noise(arg_keys[27], (EXPERTS, D), (1.1 * PAIRS_EXP ** 0.5 / EXPERTS), 48.0, ((0, 8), (1, 4)), jnp.float32)
    b_out_second = jnp.clip(jnp.exp(math.log(235.2) - 1.3862944 * jax.random.uniform(arg_keys[28], (EXPERTS, D), jnp.float32) ** shard_levels(arg_keys[28], (EXPERTS, D), ((0, 8), (1, 4)), -0.2, 0.2)), 58.8, 235.2)
    return {"patches": patches, "cotangent": cotangent, "expert_ids": expert_ids, "slots": slots, "attn_weights": attn_weights, "attn_first": attn_first, "attn_second": attn_second, "router_weights": router_weights, "router_first": router_first, "router_second": router_second, "norm_params": norm_params, "norm_first": norm_first, "norm_second": norm_second, "w_in": w_in, "w_in_first": w_in_first, "w_in_second": w_in_second, "w_in_stat": w_in_stat, "w_in_basis": w_in_basis, "w_out": w_out, "w_out_first": w_out_first, "w_out_second": w_out_second, "w_out_stat": w_out_stat, "w_out_basis": w_out_basis, "b_in": b_in, "b_in_first": b_in_first, "b_in_second": b_in_second, "b_out": b_out, "b_out_first": b_out_first, "b_out_second": b_out_second}


MATMUL_ACCURACY = lax.Precision.HIGHEST
NORM_EPS = 1e-06
BETA_FIRST = 0.5
BETA_SECOND = 0.5
STAT_DECAY = 0.5
ADAM_EPS = 1e-08
DECAY_RATE = 0.1
RATE_DENSE = 0.05
RATE_NORMS = 0.4
RATE_INPUT = 0.04
RATE_OUTPUT = 0.4
RATE_BIASES = 0.05
RATE_OFFSETS = 1.0

@jax.custom_vjp
def reduced_value(v):
    return lax.optimization_barrier(v.astype(jnp.bfloat16)).astype(jnp.float32)

@jax.custom_vjp
def low_back(v):
    return v

def low_keep(v):
    return (reduced_value(v), None)

def low_pass(kept, grad):
    return (grad,)

def back_keep(v):
    return (v, None)

def back_low(kept, grad):
    return (reduced_value(grad),)
reduced_value.defvjp(low_keep, low_pass)
low_back.defvjp(back_keep, back_low)

def layer_norm(values, gain_row, shift_row):
    centre = lax.optimization_barrier(jnp.mean(values, axis=-1, keepdims=True))
    centred = values - centre
    spread = lax.optimization_barrier(jnp.mean(centred * centred, axis=-1, keepdims=True))
    return centred * lax.rsqrt(spread + NORM_EPS) * gain_row + shift_row

def exact_gelu(values):
    return jax.nn.gelu(values, approximate=False)

def moment_step(gradient, first_moment, second_moment):
    first_new = BETA_FIRST * first_moment + (1.0 - BETA_FIRST) * gradient
    second_new = BETA_SECOND * second_moment + (1.0 - BETA_SECOND) * gradient * gradient
    normed_step = first_new / (1.0 - BETA_FIRST ** STEP) / (jnp.sqrt(second_new / (1.0 - BETA_SECOND ** STEP)) + ADAM_EPS)
    return (first_new, second_new, normed_step)

def adam_update(weight, gradient, first_moment, second_moment, step_rate, weight_decay):
    first_new, second_new, normed_step = moment_step(gradient, first_moment, second_moment)
    return (first_new, second_new, weight - step_rate * (normed_step + weight_decay * weight))

def renew_basis(statistic, rotation):
    stretched = jnp.einsum('...kj,...jl->...kl', statistic, rotation, precision=MATMUL_ACCURACY)
    gram_matrix = jnp.einsum('...kl,...km->...lm', stretched, stretched, precision=MATMUL_ACCURACY)
    factor = jnp.linalg.cholesky(gram_matrix)
    solved = jax.scipy.linalg.solve_triangular(factor, jnp.swapaxes(stretched, -1, -2), lower=True)
    return jnp.swapaxes(solved, -1, -2)

def soap_right(weight, gradient, first_moment, second_moment, statistic, rotation, step_rate):
    leading, rows_count, unit_count = gradient.shape
    blocked = gradient.reshape(leading, rows_count, unit_count // BLK, BLK)
    turned = jnp.einsum('edbk,ebkj->edbj', blocked, rotation, precision=MATMUL_ACCURACY).reshape(gradient.shape)
    first_new, second_new, normed_step = moment_step(turned, first_moment, second_moment)
    returned_step = jnp.einsum('edbj,ebkj->edbk', normed_step.reshape(blocked.shape), rotation, precision=MATMUL_ACCURACY).reshape(gradient.shape)
    weight_new = weight - step_rate * (returned_step + DECAY_RATE * weight)
    stat_new = STAT_DECAY * statistic + (1.0 - STAT_DECAY) * jnp.einsum('edbk,edbj->ebkj', blocked, blocked, precision=MATMUL_ACCURACY)
    return (first_new, second_new, weight_new, stat_new, renew_basis(stat_new, rotation))

def soap_left(weight, gradient, first_moment, second_moment, statistic, rotation, step_rate):
    leading, unit_count, cols_count = gradient.shape
    blocked = gradient.reshape(leading, unit_count // BLK, BLK, cols_count)
    turned = jnp.einsum('ebkj,ebkd->ebjd', rotation, blocked, precision=MATMUL_ACCURACY).reshape(gradient.shape)
    first_new, second_new, normed_step = moment_step(turned, first_moment, second_moment)
    returned_step = jnp.einsum('ebkj,ebjd->ebkd', rotation, normed_step.reshape(blocked.shape), precision=MATMUL_ACCURACY).reshape(gradient.shape)
    weight_new = weight - step_rate * (returned_step + DECAY_RATE * weight)
    stat_new = STAT_DECAY * statistic + (1.0 - STAT_DECAY) * jnp.einsum('ebkd,ebjd->ebkj', blocked, blocked, precision=MATMUL_ACCURACY)
    return (first_new, second_new, weight_new, stat_new, renew_basis(stat_new, rotation))

def attention_block(block, attn_low, norm_low):
    group_count = block.shape[0]
    normed = reduced_value(layer_norm(block, norm_low[0], norm_low[1]))
    projected = jnp.einsum('gsd,dc->gsc', normed, attn_low[:, :3 * D], precision=MATMUL_ACCURACY)
    joined = reduced_value(low_back(projected)).reshape(group_count, SEQ, 3, HEADS, HEAD_DIM)
    scores = jnp.einsum('gshd,gthd->ghst', joined[:, :, 0], joined[:, :, 1], precision=MATMUL_ACCURACY) * HEAD_DIM ** (-0.5)
    weights = reduced_value(jax.nn.softmax(low_back(scores), axis=-1))
    mixed = jnp.einsum('ghst,gthd->gshd', weights, joined[:, :, 2], precision=MATMUL_ACCURACY).reshape(group_count, SEQ, D)
    mixed = reduced_value(low_back(mixed))
    branch = jnp.einsum('gsd,de->gse', mixed, attn_low[:, 3 * D:], precision=MATMUL_ACCURACY)
    return block + low_back(branch)

def expert_block(operands):
    rows_in, first_low, second_low, bias_first_reduced, bias_second_low = operands
    row_count = rows_in.shape[0]
    portion_units = FF // N_TENSOR
    replicas = low_back(jnp.broadcast_to(rows_in, (N_TENSOR, row_count, D)))
    first_pieces = first_low.reshape(D, N_TENSOR, portion_units).transpose(1, 0, 2)
    preactivation = jnp.einsum('nhp,npi->nhi', replicas, first_pieces, precision=MATMUL_ACCURACY) + bias_first_reduced.reshape(N_TENSOR, 1, portion_units)
    hidden_units = reduced_value(exact_gelu(low_back(preactivation)))
    second_pieces = second_low.reshape(N_TENSOR, portion_units, D)
    owner_mask = jnp.arange(D)[None, :] // (D // N_TENSOR) == jnp.arange(N_TENSOR)[:, None]
    bias_pieces = jnp.where(owner_mask, bias_second_low[None, :], 0.0)
    partial_sums = reduced_value(jnp.einsum('ixg,igy->ixy', hidden_units, second_pieces, precision=MATMUL_ACCURACY) + bias_pieces[:, None, :])
    return reduced_value(low_back(lax.optimization_barrier(jnp.sum(partial_sums, axis=0))))

def mixture(middle, router_low, norm_low, first_low, second_low, bias_first_reduced, bias_second_low, chosen, placed):
    token_count = middle.shape[0]
    device_count = N_EXPERT * N_TENSOR
    normed = reduced_value(layer_norm(middle, norm_low[2], norm_low[3]))
    logits = low_back(jnp.dot(normed, router_low, precision=MATMUL_ACCURACY))
    router_probs = jax.nn.softmax(logits, axis=-1)
    gate_values = jnp.take_along_axis(router_probs, chosen, axis=-1)
    device = (jnp.arange(token_count) // TOK_DEV).astype(jnp.int32)
    target = ((chosen * device_count + device[:, None]) * (CS + 1) + placed).reshape(-1)
    pair_rows = low_back(jnp.broadcast_to(normed[:, None, :], (token_count, TOPK, D))).reshape(token_count * TOPK, D)
    buffer = jnp.zeros((EXPERTS * device_count * (CS + 1), D), jnp.float32).at[target].add(pair_rows)
    buffer = buffer.reshape(EXPERTS, device_count, CS + 1, D)[:, :, :CS].reshape(EXPERTS, device_count * CS, D)
    results = lax.map(jax.checkpoint(expert_block), (buffer, first_low, second_low, bias_first_reduced, bias_second_low))
    padded = jnp.pad(results.reshape(EXPERTS, device_count, CS, D), ((0, 0), (0, 0), (0, 1), (0, 0))).reshape(-1, D)
    returned = padded[target].reshape(token_count, TOPK, D)
    return middle + lax.optimization_barrier(jnp.sum(gate_values[:, :, None] * returned, axis=1))

def forward(params, inputs, chosen, placed):
    attn_param, router_param, norm_param, first_param, second_param, bias_first_param, bias_second_param = params
    attn_low = reduced_value(attn_param)
    norm_low = reduced_value(norm_param)
    image_group = math.gcd(IMAGES, 16)
    blocks = inputs.reshape(IMAGES // image_group, image_group, SEQ, D)
    middle = lax.map(jax.checkpoint(partial(attention_block, attn_low=attn_low, norm_low=norm_low)), blocks)
    middle = middle.reshape(IMAGES * SEQ, D)
    final = mixture(middle, reduced_value(router_param), norm_low, reduced_value(first_param), reduced_value(second_param), reduced_value(bias_first_param), reduced_value(bias_second_param), chosen, placed)
    return final.reshape(IMAGES, SEQ, D)

def reference(patches, cotangent, expert_ids, slots, attn_weights, attn_first, attn_second, router_weights, router_first, router_second, norm_params, norm_first, norm_second, w_in, w_in_first, w_in_second, w_in_stat, w_in_basis, w_out, w_out_first, w_out_second, w_out_stat, w_out_basis, b_in, b_in_first, b_in_second, b_out, b_out_first, b_out_second):
    params = (attn_weights, router_weights, norm_params, w_in, w_out, b_in, b_out)
    totals = jax.tree.map(jnp.zeros_like, params)
    outputs_list = []
    grads_list = []
    for micro_step in range(MB):
        chosen = expert_ids[micro_step].reshape(IMAGES * SEQ, TOPK)
        placed = slots[micro_step].reshape(IMAGES * SEQ, TOPK)
        inputs = patches[micro_step].astype(jnp.float32)
        result, pullback = jax.vjp(partial(forward, chosen=chosen, placed=placed), params, inputs)
        param_grads, input_grads = pullback(cotangent[micro_step].astype(jnp.float32))
        totals = jax.tree.map(jnp.add, totals, param_grads)
        outputs_list.append(result.astype(jnp.bfloat16))
        grads_list.append(input_grads)
    grad_attn, grad_router, grad_norm, grad_win, grad_wout, grad_bin, grad_bout = totals
    attn_first_new, attn_second_new, attn_new = adam_update(attn_weights, grad_attn, attn_first, attn_second, RATE_DENSE, DECAY_RATE)
    router_first_new, router_second_new, router_new = adam_update(router_weights, grad_router, router_first, router_second, RATE_DENSE, DECAY_RATE)
    norm_first_new, norm_second_new, norm_new = adam_update(norm_params, grad_norm, norm_first, norm_second, RATE_NORMS, 0.0)
    win_first_new, win_second_new, win_new, win_stat_new, win_basis_new = soap_right(w_in, grad_win, w_in_first, w_in_second, w_in_stat, w_in_basis, RATE_INPUT)
    wout_first_new, wout_second_new, wout_new, wout_stat_new, wout_basis_new = soap_left(w_out, grad_wout, w_out_first, w_out_second, w_out_stat, w_out_basis, RATE_OUTPUT)
    bin_first_new, bin_second_new, bin_new = adam_update(b_in, grad_bin, b_in_first, b_in_second, RATE_BIASES, 0.0)
    bout_first_new, bout_second_new, bout_new = adam_update(b_out, grad_bout, b_out_first, b_out_second, RATE_OFFSETS, 0.0)
    return (jnp.stack(outputs_list, axis=0), jnp.stack(grads_list, axis=0), attn_first_new, attn_second_new, attn_new, attn_new.astype(jnp.bfloat16), router_first_new, router_second_new, router_new, router_new.astype(jnp.bfloat16), norm_first_new, norm_second_new, norm_new, win_first_new, win_second_new, win_new, win_new.astype(jnp.bfloat16), win_stat_new, win_basis_new, wout_first_new, wout_second_new, wout_new, wout_new.astype(jnp.bfloat16), wout_stat_new, wout_basis_new, bin_first_new, bin_second_new, bin_new, bout_first_new, bout_second_new, bout_new)
```

```python
from functools import partial

import jax
import jax.numpy as jnp
from jax import lax
from jax.experimental import pallas as pl
from jax.experimental.pallas import tpu as pltpu
from jax.sharding import PartitionSpec as P

D = 768
HEADS = 12
HEAD_DIM = 64
SEQ = 196
TOPK = 2
MB = 2
STEP = 10
BLK = 384


MATMUL_ACCURACY = lax.Precision.HIGHEST
NORM_EPS = 1e-06
BETA_FIRST = 0.5
BETA_SECOND = 0.5
STAT_DECAY = 0.5
ADAM_EPS = 1e-08
DECAY_RATE = 0.1
RATE_DENSE = 0.05
RATE_NORMS = 0.4
RATE_INPUT = 0.04
RATE_OUTPUT = 0.4
RATE_BIASES = 0.05
RATE_OFFSETS = 1.0


def column_sum(left_side, right_side):
    return lax.dot_general(
        left_side, right_side, (((0,), (0,)), ((), ())), preferred_element_type=jnp.float32
    )


def row_product(left_side, right_side):
    return lax.dot_general(
        left_side, right_side, (((1,), (1,)), ((), ())), preferred_element_type=jnp.float32
    )


def moment_step(gradient, first_moment, second_moment):
    first_new = BETA_FIRST * first_moment + (1.0 - BETA_FIRST) * gradient
    second_new = BETA_SECOND * second_moment + (1.0 - BETA_SECOND) * gradient * gradient
    normed_step = (
        first_new
        / (1.0 - BETA_FIRST**STEP)
        / (jnp.sqrt(second_new / (1.0 - BETA_SECOND**STEP)) + ADAM_EPS)
    )
    return (first_new, second_new, normed_step)


def adam_update(weight, gradient, first_moment, second_moment, step_rate, weight_decay):
    first_new, second_new, normed_step = moment_step(gradient, first_moment, second_moment)
    return (first_new, second_new, weight - step_rate * (normed_step + weight_decay * weight))


EXPERT = "expert"
TENSOR = "tensor"
BOTH = (EXPERT, TENSOR)
VMEM_LIMIT = 56 * 2**20
SUB = 64


def mm(left, right):
    return jnp.dot(left, right, preferred_element_type=jnp.float32, precision=MATMUL_ACCURACY)


def mt(left, right):
    return lax.dot_general(
        left,
        right,
        (((1,), (1,)), ((), ())),
        preferred_element_type=jnp.float32,
        precision=MATMUL_ACCURACY,
    )


def tm(left, right):
    return lax.dot_general(
        left,
        right,
        (((0,), (0,)), ((), ())),
        preferred_element_type=jnp.float32,
        precision=MATMUL_ACCURACY,
    )


def factor_inverse(mats):
    n=SUB; B=jnp.broadcast_to; w=(8,2*n)
    lane=lax.broadcasted_iota(jnp.int32,w,1); sub=lax.broadcasted_iota(jnp.int32,w,0)
    X=[]
    for m in mats:
        tiles=[]
        for i in range(n//8):
            eye=jnp.where(lane==sub+8*i+n,1.0,0.0)
            tiles.append(jnp.concatenate([m[8*i:8*i+8,:],eye[:,n:]],axis=1))
        X.append(tiles)
    outs=[[] for _ in mats]
    for r in range(n//8):
        for m,tiles in enumerate(X):
            T=tiles[r]
            cols=[[B(tiles[t][:,8*r+k:8*r+k+1],w) for k in range(8)] for t in range(r,n//8)]
            a=[[B(cols[0][j][i:i+1,:],w) for j in range(i+1)] for i in range(8)]
            rows=[B(T[i:i+1,:],w) for i in range(8)]
            inv=[None]*8; l=[[None]*8 for _ in range(8)]
            for k in range(8):
                inv[k]=1.0/a[k][k]
                for i in range(k+1,8): l[i][k]=a[i][k]*inv[k]
                for i in range(k+1,8):
                    for j in range(k+1,i+1):
                        a[i][j]=a[i][j]-l[i][k]*a[j][k]
                for i in range(k+1,8): rows[i]=rows[i]-l[i][k]*rows[k]
            o=jnp.zeros(w,jnp.float32)
            for k in range(8): o=jnp.where(sub==k,rows[k]*lax.rsqrt(a[k][k]),o)
            outs[m].append(o[:,n:])
            if r+1<n//8:
                wv=[rows[k]*inv[k] for k in range(8)]
                for k in range(6,-1,-1):
                    for j in range(k+1,8): wv[k]=wv[k]-l[j][k]*wv[j]
                for t in range(r+1,n//8):
                    c=cols[t-r]
                    acc=c[0]*wv[0]
                    for k in range(1,8): acc=acc+c[k]*wv[k]
                    tiles[t]=tiles[t]-acc
    return [jnp.concatenate(o,axis=0) for o in outs]
def renew_kernel(z_ref,q_ref,m_ref):
    nb=z_ref.shape[0]; n=z_ref.shape[1]; kb=n//128; h=SUB
    for b in range(nb):
        z=z_ref[b]
        m_ref[b]=tm(z,z)
    for k in range(kb):
        o=128*k; sl=slice(o,o+128)
        d11=[m_ref[b,o:o+h,o:o+h] for b in range(nb)]
        i1=factor_inverse(d11)
        l21=[mt(m_ref[b,o+h:o+128,o:o+h],i1[b]) for b in range(nb)]
        d22=[m_ref[b,o+h:o+128,o+h:o+128]-mt(l21[b],l21[b]) for b in range(nb)]
        i2=factor_inverse(d22)
        inv=[]
        for b in range(nb):
            low=-mm(mm(i2[b],l21[b]),i1[b])
            inv.append(jnp.concatenate([jnp.concatenate([i1[b],jnp.zeros((h,h),jnp.float32)],1),jnp.concatenate([low,i2[b]],1)],0))
        for b in range(nb):
            q=z_ref[b,:,sl]
            for j in range(k):
                q=q-mt(q_ref[b,:,128*j:128*j+128],m_ref[b,sl,128*j:128*j+128])
            q_ref[b,:,sl]=mt(q,inv[b])
            if k+1<kb:
                p=mt(m_ref[b,o+128:,sl],inv[b])
                m_ref[b,o+128:,sl]=p
                m_ref[b,o+128:,o+128:]=m_ref[b,o+128:,o+128:]-mt(p,p)
def renew(z):
    return pl.pallas_call(renew_kernel,out_shape=jax.ShapeDtypeStruct(z.shape,z.dtype),
      in_specs=[pl.BlockSpec(memory_space=pltpu.VMEM)],out_specs=pl.BlockSpec(memory_space=pltpu.VMEM),
      scratch_shapes=[pltpu.VMEM(z.shape,jnp.float32)],
      compiler_params=pltpu.CompilerParams(vmem_limit_bytes=32*2**20))(z)


def low(values):
    return values.astype(jnp.bfloat16)


def wide(values):
    return values.astype(jnp.float32)


def dot(left, right):
    return jnp.dot(left, right, preferred_element_type=jnp.float32)


def vmem_call(kernel, **options):
    return pl.pallas_call(
        kernel, compiler_params=pltpu.CompilerParams(vmem_limit_bytes=VMEM_LIMIT), **options
    )


def full_block(shape):
    return pl.BlockSpec(shape, lambda *_: (0,) * len(shape))


def norm_parts(values):
    centred = values - jnp.mean(values, axis=-1, keepdims=True)
    scale = lax.rsqrt(jnp.mean(centred * centred, axis=-1, keepdims=True) + NORM_EPS)
    return centred * scale, scale


def norm_backward(grads, normed, scale, gain):
    inner = grads * gain
    return scale * (
        inner
        - jnp.mean(inner, axis=-1, keepdims=True)
        - normed * jnp.mean(inner * normed, axis=-1, keepdims=True)
    )


def route_mask(target, slot_total):
    slot_index = lax.broadcasted_iota(jnp.int32, (target.shape[0], slot_total), 1)
    hit = (slot_index == target[:, :1]) | (slot_index == target[:, 1:2])
    return jnp.where(hit, 1.0, 0.0)


def masked_softmax(logits, count):
    lanes = lax.broadcasted_iota(jnp.int32, logits.shape, 1)
    inside = lanes < count
    peak = jnp.max(jnp.where(inside, logits, -jnp.inf), axis=-1, keepdims=True)
    raised = jnp.where(inside, jnp.exp(jnp.where(inside, logits - peak, 0.0)), 0.0)
    return raised / jnp.sum(raised, axis=-1, keepdims=True)


def softmax_rows(scores):
    raised = jnp.exp(scores - jnp.max(scores, axis=-1, keepdims=True))
    return raised / jnp.sum(raised, axis=-1, keepdims=True)


def dispatch_kernel(target_ref, rows_ref, out_ref):
    experts, copies, steps, padded, _ = out_ref.shape
    for step in range(steps):
        routing = low(route_mask(target_ref[step], experts * padded))
        rows = column_sum(routing, rows_ref[step, 0])
        rows = low(rows.reshape(experts, padded, D))
        for copy in range(copies):
            out_ref[:, copy, step] = rows


def attention_kernel(
    experts, x_ref, target_ref, a_ref, out_ref, qkv_ref, mixed_ref, middle_ref, probs_ref
):
    copies, padded = (out_ref.shape[2], out_ref.shape[3])
    inputs = wide(x_ref[0, 0])
    extra = a_ref[:, 4 * D :]
    vectors = wide(extra).T
    gains = [vectors[experts + i : experts + i + 1] for i in range(4)]
    normed, _ = norm_parts(inputs)
    normed_low = low(normed * gains[0] + gains[1])
    qkv_ref[0] = low(dot(normed_low, a_ref[:, : 3 * D]))
    lanes = lax.broadcasted_iota(jnp.int32, (SEQ, 2 * HEAD_DIM), 1)
    for pair in range(HEADS // 2):
        start = 2 * HEAD_DIM * pair
        query = qkv_ref[0, :, start : start + 2 * HEAD_DIM]
        keys = qkv_ref[0, :, D + start : D + start + 2 * HEAD_DIM]
        values = qkv_ref[0, :, 2 * D + start : 2 * D + start + 2 * HEAD_DIM]
        both = []
        for side in range(2):
            here = (lanes < HEAD_DIM) if side == 0 else (lanes >= HEAD_DIM)
            scores = row_product(jnp.where(here, query, 0), keys) * HEAD_DIM ** (-0.5)
            both.append(dot(low(softmax_rows(scores)), values))
        mixed_ref[0, :, start : start + 2 * HEAD_DIM] = low(
            jnp.where(lanes < HEAD_DIM, both[0], both[1])
        )
    middle = inputs + dot(mixed_ref[0], a_ref[:, 3 * D : 4 * D])
    middle_ref[0] = middle
    normed, _ = norm_parts(middle)
    moe_low = low(normed * gains[2] + gains[3])
    probs_ref[0] = masked_softmax(dot(moe_low, extra), experts)
    routing = low(route_mask(target_ref[0], experts * padded))
    rows = low(column_sum(routing, moe_low).reshape(experts, padded, D))
    for copy in range(copies):
        out_ref[0, :, copy] = rows


def attention_backward_kernel(
    experts,
    x_ref,
    up_ref,
    target_ref,
    back_ref,
    qkv_ref,
    mixed_ref,
    middle_ref,
    probs_ref,
    a_ref,
    *refs,
):
    out_ref, grad_ref, normed_ref, joined_ref, branch_ref, moe_ref, logit_ref, vector_ref = refs[-8:]
    copies, padded = (back_ref.shape[1], back_ref.shape[3])
    slot_total = experts * padded
    extra = a_ref[:, 4 * D :]
    vectors = wide(extra).T
    gains = [vectors[experts + i : experts + i + 1] for i in range(4)]
    inputs = wide(x_ref[0, 0])
    upstream_low = up_ref[0, 0]
    upstream = wide(upstream_low)
    middle = middle_ref[0]
    probs = probs_ref[0]

    def collected(kind):
        total = wide(back_ref[:, 0, kind])
        for copy in range(1, copies):
            total = total + wide(back_ref[:, copy, kind])
        return low(total.reshape(slot_total, D))

    coming = collected(0)
    grad_coming = collected(1)
    routing = route_mask(target_ref[0], slot_total)
    member = jnp.where(
        lax.broadcasted_iota(jnp.int32, (probs.shape[1], slot_total), 1) // padded
        == lax.broadcasted_iota(jnp.int32, (probs.shape[1], slot_total), 0),
        1.0,
        0.0,
    )
    member_low = low(member)
    probs_high = low(probs)
    slot_gate = routing * (dot(probs_high, member_low) + dot(low(probs - wide(probs_high)), member_low))
    gate_high = low(slot_gate)
    final = middle + dot(gate_high, coming) + dot(low(slot_gate - wide(gate_high)), coming)
    out_ref[0, 0] = low(final)
    slot_grads = routing * row_product(upstream_low, coming)
    slot_high = low(slot_grads)
    prob_grads = row_product(slot_high, member_low) + row_product(
        low(slot_grads - wide(slot_high)), member_low
    )
    logit_low = low(
        probs * (prob_grads - jnp.sum(prob_grads * probs, axis=-1, keepdims=True))
    )
    logit_ref[...] = logit_low
    moe_grad = dot(low(routing), grad_coming) + row_product(logit_low, extra)
    normed, scale = norm_parts(middle)
    moe_ref[...] = low(normed * gains[2] + gains[3])
    vector_ref[2:3] = jnp.sum(moe_grad * normed, axis=0, keepdims=True)
    vector_ref[3:4] = jnp.sum(moe_grad, axis=0, keepdims=True)
    grad_middle = upstream + norm_backward(moe_grad, normed, scale, gains[2])
    branch_low = low(grad_middle)
    branch_ref[...] = branch_low
    grad_mixed = low(row_product(branch_low, a_ref[:, 3 * D : 4 * D]))
    lanes = lax.broadcasted_iota(jnp.int32, (SEQ, 2 * HEAD_DIM), 1)
    for pair in range(HEADS // 2):
        start = 2 * HEAD_DIM * pair
        stop = start + 2 * HEAD_DIM
        query = qkv_ref[0, :, start:stop]
        keys = qkv_ref[0, :, D + start : D + stop]
        values = qkv_ref[0, :, 2 * D + start : 2 * D + stop]
        grad_here = grad_mixed[:, start:stop]
        results = []
        for side in range(2):
            here = (lanes < HEAD_DIM) if side == 0 else (lanes >= HEAD_DIM)
            scores = row_product(jnp.where(here, query, 0), keys) * HEAD_DIM ** (-0.5)
            weights = softmax_rows(scores)
            grad_probs = row_product(jnp.where(here, grad_here, 0), values)
            grad_scores = low(
                weights
                * (grad_probs - jnp.sum(grad_probs * weights, axis=-1, keepdims=True))
            )
            results.append(
                (
                    dot(grad_scores, keys) * HEAD_DIM ** (-0.5),
                    column_sum(grad_scores, query) * HEAD_DIM ** (-0.5),
                    column_sum(low(weights), grad_here),
                )
            )
        for part in range(3):
            joined_ref[:, part * D + start : part * D + stop] = low(
                jnp.where(lanes < HEAD_DIM, results[0][part], results[1][part])
            )
    grad_normed = row_product(joined_ref[...], a_ref[:, : 3 * D])
    normed, scale = norm_parts(inputs)
    normed_ref[...] = low(normed * gains[0] + gains[1])
    vector_ref[4:8] = jnp.zeros((4, D), jnp.float32)
    vector_ref[0:1] = jnp.sum(grad_normed * normed, axis=0, keepdims=True)
    vector_ref[1:2] = jnp.sum(grad_normed, axis=0, keepdims=True)
    grad_ref[0, 0] = grad_middle + norm_backward(grad_normed, normed, scale, gains[0])


def weight_sums_kernel(experts, core_ref, mixed_ref, *refs):
    own_ref, other_ref = refs[-2:]
    steps = [refs[6 * i : 6 * i + 6] for i in range(MB)]
    held, block, _ = own_ref.shape
    first_core = core_ref[0] == 0

    def write(total, start):
        stop = start + total.shape[1]
        pairs = total.reshape(held, 2, block, total.shape[1])
        even, odd = (pairs[:, 0], pairs[:, 1])
        own_ref[:, :, start:stop] = jnp.where(first_core, even, odd)
        other_ref[:, :, start:stop] = low(jnp.where(first_core, odd, even))

    for part in range(3):
        total = sum(column_sum(s[0][...], s[1][:, part * D : part * D + D]) for s in steps)
        write(total, part * D)
    write(sum(column_sum(mixed_ref[i], s[2][...]) for i, s in enumerate(steps)), 3 * D)
    vectors = sum(s[5][...] for s in steps)
    vectors = jnp.concatenate(
        [
            jnp.zeros((experts, D), jnp.float32),
            vectors,
            jnp.zeros((128 - experts - vectors.shape[0], D), jnp.float32),
        ],
        axis=0,
    )
    write(sum(column_sum(s[3][...], s[4][...]) for s in steps) + vectors.T, 4 * D)


def gelu_parts(values):
    raised = jnp.exp(-0.5 * values * values)
    root = 1.0 / (1.0 + (0.3275911 * 0.5**0.5) * jnp.abs(values))
    tail = 1.061405429 * root - 1.453152027
    tail = tail * root + 1.421413741
    tail = tail * root - 0.284496736
    tail = tail * root + 0.254829592
    tail = 0.5 * tail * root * raised
    return jnp.where(values >= 0.0, 1.0 - tail, tail), raised * 0.3989422804014327


def hidden_kernel(
    experts,
    expert_ref,
    rows_ref,
    up_ref,
    router_ref,
    own_ref,
    peer_ref,
    bias_ref,
    hidden_own_ref,
    hidden_peer_ref,
    slope_own_ref,
    slope_peer_ref,
    grad_ref,
    sum_ref,
):
    count, padded = rows_ref.shape[:2]
    units = own_ref.shape[1]
    rows = low(wide(rows_ref[...]).reshape(count * padded, D))
    probs = masked_softmax(dot(rows, router_ref[...]), experts)
    lanes = lax.broadcasted_iota(jnp.int32, probs.shape, 1)
    gate = jnp.sum(jnp.where(lanes == expert_ref[0], probs, 0.0), axis=-1, keepdims=True)
    grad = low(gate * wide(up_ref[...]).reshape(count * padded, D))
    grad_ref[...] = grad
    partial = jnp.sum(wide(grad), axis=0, keepdims=True)

    @pl.when(pl.program_id(0) == 0)
    def _():
        sum_ref[...] = jnp.zeros_like(sum_ref)

    sum_ref[0:1] += partial
    for side, (weight, hidden_ref, slope_ref) in enumerate(
        ((own_ref, hidden_own_ref, slope_own_ref), (peer_ref, hidden_peer_ref, slope_peer_ref))
    ):
        values = dot(rows, weight[...]) + bias_ref[:, side * units : (side + 1) * units]
        area, density = gelu_parts(values)
        hidden_ref[...] = low(values * area)
        slope_ref[...] = low(area + values * density)


def result_kernel(
    hidden_own_ref,
    hidden_peer_ref,
    slope_own_ref,
    slope_peer_ref,
    grad_ref,
    out_own_ref,
    out_peer_ref,
    in_own_ref,
    in_peer_ref,
    bias_ref,
    back_ref,
    pre_own_ref,
    pre_peer_ref,
    sum_ref,
):
    count, _, padded, _ = back_ref.shape
    units = in_own_ref.shape[1]

    @pl.when(pl.program_id(0) == 0)
    def _():
        sum_ref[...] = jnp.zeros_like(sum_ref)

    out_term = (
        dot(hidden_own_ref[...], out_own_ref[...])
        + dot(hidden_peer_ref[...], out_peer_ref[...])
        + bias_ref[...]
    )
    back_ref[:, 0] = low(out_term.reshape(count, padded, D))
    grad_term = None
    for side, (slope, out_weight, in_weight, pre_ref) in enumerate(
        (
            (slope_own_ref, out_own_ref, in_own_ref, pre_own_ref),
            (slope_peer_ref, out_peer_ref, in_peer_ref, pre_peer_ref),
        )
    ):
        pre = low(row_product(grad_ref[...], out_weight[...]) * wide(slope[...]))
        pre_ref[...] = pre
        sum_ref[0:1, side * units : (side + 1) * units] += jnp.sum(
            wide(pre), axis=0, keepdims=True
        )
        term = row_product(pre, in_weight[...])
        grad_term = term if grad_term is None else grad_term + term
    back_ref[:, 1] = low(grad_term.reshape(count, padded, D))


def split(values):
    high = low(values)
    return high, low(values - wide(high))


def split_dot(left, right, dims):
    def one(a, b):
        return lax.dot_general(a, b, (dims, ((), ())), preferred_element_type=jnp.float32)

    return one(left[0], right[0]) + (one(left[0], right[1]) + one(left[1], right[0]))


def turn_kernel(
    along_rows,
    rate,
    own_ref,
    other_ref,
    weight_ref,
    first_ref,
    second_ref,
    stat_ref,
    basis_ref,
    first_out,
    second_out,
    weight_out,
    copy_out,
    stat_out,
    stretched_out,
):
    gradient = own_ref[...] + wide(other_ref[...])
    basis = basis_ref[0, 0]
    gradient_parts, basis_parts = (split(gradient), split(basis))
    if along_rows:
        turned = split_dot(basis_parts, gradient_parts, ((0,), (0,)))
        outer = mt(gradient, gradient)
    else:
        turned = split_dot(gradient_parts, basis_parts, ((1,), (0,)))
        outer = tm(gradient, gradient)
    first_new, second_new, step = moment_step(turned, first_ref[0], second_ref[0])
    first_out[0] = first_new
    second_out[0] = second_new
    step_parts = split(step)
    if along_rows:
        returned = split_dot(basis_parts, step_parts, ((1,), (0,)))
    else:
        returned = split_dot(step_parts, basis_parts, ((1,), (1,)))
    weight = weight_ref[0]
    weight_new = weight - rate * (returned + DECAY_RATE * weight)
    weight_out[0] = weight_new
    copy_out[0] = low(weight_new)
    stat_new = STAT_DECAY * stat_ref[0, 0] + (1.0 - STAT_DECAY) * outer
    stat_out[0, 0] = stat_new
    stretched_out[0] = mm(stat_new, basis)


def swap(values, axis, distance):
    size = lax.axis_size(axis)
    return lax.ppermute(values, axis, [(i, i ^ distance) for i in range(size)])


def ordered(bit, mine, other):
    return jnp.where(bit == 0, jnp.stack([mine, other]), jnp.stack([other, mine]))


def gather_rows(shard):
    experts, tensors = (lax.axis_size(EXPERT), lax.axis_size(TENSOR))
    expert, tensor = (lax.axis_index(EXPERT), lax.axis_index(TENSOR))
    block = shard[None]
    distance = 1
    while distance < tensors:
        other = swap(block, TENSOR, distance)
        block = ordered((tensor // distance) % 2, block, other).reshape(-1, *shard.shape)
        distance *= 2
    first_stage = block
    block = block[None]
    distance = 2
    while distance < experts // 4:
        other = swap(block, EXPERT, distance)
        block = ordered((expert // distance) % 2, block, other).reshape(-1, *block.shape[1:])
        distance *= 2
    near, far = (distance, 2 * distance)
    middle = tensors // 2
    from_near, from_far = (swap(block, EXPERT, near), swap(block, EXPERT, far))
    corner = jnp.concatenate(
        [swap(from_far[:, :middle], EXPERT, near), swap(from_near[:, middle:], EXPERT, far)],
        axis=1,
    )
    second_stage = corner
    pieces = (block, from_near, from_far, corner)
    crossed = [swap(piece, EXPERT, 1) for piece in pieces]
    near_bit, far_bit = ((expert // near) % 2, (expert // far) % 2)

    def arranged(four):
        return ordered(
            far_bit,
            ordered(near_bit, four[0], four[1]),
            ordered(near_bit, four[2], four[3]),
        ).reshape(-1, *block.shape[1:])

    whole = ordered(expert % 2, arranged(pieces), arranged(crossed))
    whole = jnp.moveaxis(whole, 0, 1)
    return whole.reshape(-1, shard.shape[1]), first_stage, second_stage


def scatter_sums(held, sending):
    experts, tensors = (lax.axis_size(EXPERT), lax.axis_size(TENSOR))
    expert, tensor = (lax.axis_index(EXPERT), lax.axis_index(TENSOR))
    columns = held.shape[2]

    def pick(values, index, axis=0):
        return lax.dynamic_index_in_dim(values, index, axis, False)

    held = held + wide(swap(sending, EXPERT, 1))
    near, far = (experts // 4, experts // 2)
    near_bit, far_bit = ((expert // near) % 2, (expert // far) % 2)
    held = held.reshape(4, experts // 8, tensors, -1, columns)
    place = 2 * far_bit + near_bit
    own, to_near, to_far, to_corner = (
        pick(held, place),
        pick(held, place ^ 1),
        pick(held, place ^ 2),
        pick(held, place ^ 3),
    )
    middle = tensors // 2
    passed_near = swap(low(to_corner[:, :middle]), EXPERT, near)
    passed_far = swap(low(to_corner[:, middle:]), EXPERT, far)
    to_far = jnp.concatenate([to_far[:, :middle] + wide(passed_near), to_far[:, middle:]], axis=1)
    to_near = jnp.concatenate([to_near[:, :middle], to_near[:, middle:] + wide(passed_far)], axis=1)
    held = (
        own
        + wide(swap(low(to_near), EXPERT, near))
        + wide(swap(low(to_far), EXPERT, far))
    )
    distance = experts // 8
    while distance >= 2:
        bit = (expert // distance) % 2
        halves = held.reshape(2, -1, *held.shape[1:])
        held = pick(halves, bit) + wide(swap(low(pick(halves, 1 - bit)), EXPERT, distance))
        distance //= 2
    held = held.reshape(tensors, -1, columns)
    distance = tensors // 2
    while distance >= 1:
        bit = (tensor // distance) % 2
        halves = held.reshape(2, -1, *held.shape[1:])
        held = pick(halves, bit) + wide(swap(low(pick(halves, 1 - bit)), TENSOR, distance))
        distance //= 2
    return held.reshape(-1, columns)


def soap(along_rows, rate, own, other, weight, first, second, statistic, rotation):
    blocks = statistic.shape[1]
    f32 = jnp.float32
    if along_rows:
        flat = pl.BlockSpec((BLK, D), lambda i: (i, 0))
        deep = pl.BlockSpec((1, BLK, D), lambda i: (0, i, 0))
    else:
        flat = pl.BlockSpec((D, BLK), lambda i: (0, i))
        deep = pl.BlockSpec((1, D, BLK), lambda i: (0, 0, i))
    square = pl.BlockSpec((1, 1, BLK, BLK), lambda i: (0, i, 0, 0))
    results = vmem_call(
        partial(turn_kernel, along_rows, rate),
        grid=(blocks,),
        in_specs=[flat, flat, deep, deep, deep, square, square],
        out_specs=[deep] * 4 + [square, pl.BlockSpec((1, BLK, BLK), lambda i: (i, 0, 0))],
        out_shape=[jax.ShapeDtypeStruct(weight.shape, f32)] * 3
        + [
            jax.ShapeDtypeStruct(weight.shape, jnp.bfloat16),
            jax.ShapeDtypeStruct(statistic.shape, f32),
            jax.ShapeDtypeStruct(statistic.shape[1:], f32),
        ],
    )(own, other, weight, first, second, statistic, rotation)
    return (*results[:5], renew(results[5])[None])


def per_device(
    patches,
    cotangent,
    expert_ids,
    slots,
    attn_weights,
    attn_first,
    attn_second,
    router_weights,
    router_first,
    router_second,
    norm_params,
    norm_first,
    norm_second,
    w_in,
    w_in_first,
    w_in_second,
    w_in_stat,
    w_in_basis,
    w_out,
    w_out_first,
    w_out_second,
    w_out_stat,
    w_out_basis,
    b_in,
    b_in_first,
    b_in_second,
    b_out,
    b_out_first,
    b_out_second,
):
    tokens_here = SEQ
    expert_total = router_weights.shape[1]
    capacity = (105 * TOPK * tokens_here + 100 * expert_total - 1) // (100 * expert_total)
    padded = 8 * ((capacity + 7) // 8)
    experts, tensors = (lax.axis_size(EXPERT), lax.axis_size(TENSOR))
    expert, tensor = (lax.axis_index(EXPERT), lax.axis_index(TENSOR))
    half = tensors // 2
    members = expert_total * half
    units = w_in.shape[2]
    shard_columns = b_out.shape[1]
    columns = 4 * D + 128
    bf16, f32 = (jnp.bfloat16, jnp.float32)
    shape = jax.ShapeDtypeStruct
    partner = [(i, (i + half) % tensors) for i in range(tensors)]
    groups = [
        [e * tensors + z for e in range(experts) for z in range(h * half, (h + 1) * half)]
        for h in range(2)
    ]

    def exchange(values):
        return lax.all_to_all(values, BOTH, 0, 0, axis_index_groups=groups, tiled=True)

    def across(values):
        return lax.ppermute(values, TENSOR, partner)

    packed = jnp.concatenate(
        [
            low(attn_weights),
            low(router_weights),
            low(norm_params).T,
            jnp.zeros((attn_weights.shape[0], 128 - expert_total - 4), bf16),
        ],
        axis=1,
    )
    gathered, first_stage, second_stage = gather_rows(packed)
    in_own, out_own = (low(w_in[0]), low(w_out[0]))
    sent_in, sent_out, _ = lax.optimization_barrier((in_own, out_own, first_stage))
    in_peer, out_peer = (across(sent_in), across(sent_out))
    b_in_low, b_out_low = (low(b_in), low(b_out))
    peer_bias = across(jnp.concatenate([b_in_low, b_out_low], axis=1))
    bias_in = wide(jnp.concatenate([b_in_low, peer_bias[:, :units]], axis=1))
    bias_out = jnp.zeros((1, D), f32)
    own_place = tensor * shard_columns
    peer_place = ((tensor + half) % tensors) * shard_columns
    bias_out = lax.dynamic_update_slice(bias_out, wide(b_out_low), (0, own_place))
    bias_out = lax.dynamic_update_slice(bias_out, wide(peer_bias[:, units:]), (0, peer_place))
    chosen = expert_ids.reshape(MB, tokens_here, TOPK)
    placed = slots.reshape(MB, tokens_here, TOPK)
    target = jnp.where(placed < capacity, chosen * padded + placed, -1)
    target_all = full_block(target.shape)
    up_sent = vmem_call(
        dispatch_kernel,
        grid=(1,),
        in_specs=[target_all, full_block(cotangent.shape)],
        out_specs=full_block((expert_total, half, MB, padded, D)),
        out_shape=shape((expert_total, half, MB, padded, D), bf16),
    )(target, cotangent)
    up_sent, _ = lax.optimization_barrier((up_sent, second_stage))
    up_all = exchange(up_sent.reshape(members, MB, padded, D))
    image = pl.BlockSpec((1, 1, SEQ, D), lambda i: (i, 0, 0, 0))

    def per_step(*tail):
        return pl.BlockSpec((1, *tail), lambda i: (i,) + (0,) * len(tail))

    sent, qkv, mixed, middle, probs = vmem_call(
        partial(attention_kernel, expert_total),
        grid=(MB,),
        in_specs=[image, per_step(SEQ, TOPK), full_block((D, columns))],
        out_specs=[
            per_step(expert_total, half, padded, D),
            per_step(SEQ, 3 * D),
            per_step(SEQ, D),
            per_step(SEQ, D),
            per_step(SEQ, 128),
        ],
        out_shape=[
            shape((MB, expert_total, half, padded, D), bf16),
            shape((MB, SEQ, 3 * D), bf16),
            shape((MB, SEQ, D), bf16),
            shape((MB, SEQ, D), f32),
            shape((MB, SEQ, 128), f32),
        ],
    )(patches, target, gathered)
    arrived = [exchange(sent[step].reshape(members, padded, D)) for step in range(MB)]
    count = max(
        n
        for n in range(1, members + 1)
        if members % n == 0 and n * padded <= 256 and (n * padded) % 16 == 0
    )
    tile = count * padded
    total_rows = members * padded
    tiles = members // count

    def rows_of(width):
        return pl.BlockSpec((tile, width), lambda i: (i, 0))

    expert_scalar = jnp.reshape(expert, (1,)).astype(jnp.int32)
    in_smem = pl.BlockSpec(memory_space=pltpu.SMEM)
    hidden = []
    for step in range(MB):
        hidden.append(
            vmem_call(
                partial(hidden_kernel, expert_total),
                grid=(tiles,),
                in_specs=[
                    in_smem,
                    pl.BlockSpec((count, padded, D), lambda i: (i, 0, 0)),
                    pl.BlockSpec((count, None, padded, D), lambda i, step=step: (i, step, 0, 0)),
                    pl.BlockSpec((D, 128), lambda i: (0, 4 * D // 128)),
                    full_block((D, units)),
                    full_block((D, units)),
                    full_block((1, 2 * units)),
                ],
                out_specs=[rows_of(units)] * 4 + [rows_of(D), full_block((8, D))],
                out_shape=[shape((total_rows, units), bf16)] * 4
                + [shape((total_rows, D), bf16), shape((8, D), f32)],
            )(expert_scalar, arrived[step], up_all, gathered, in_own, in_peer, bias_in)
        )
    sum_out = sum(column_sum(h[1], h[4]) for h in hidden)
    out_other = across(low(sum_out))
    sum_out_own = sum(column_sum(h[0], h[4]) for h in hidden)
    results = []
    for step in range(MB):
        results.append(
            vmem_call(
                result_kernel,
                grid=(tiles,),
                in_specs=[rows_of(units)] * 4
                + [
                    rows_of(D),
                    full_block((units, D)),
                    full_block((units, D)),
                    full_block((D, units)),
                    full_block((D, units)),
                    full_block((1, D)),
                ],
                out_specs=[
                    pl.BlockSpec((count, 2, padded, D), lambda i: (i, 0, 0, 0)),
                    rows_of(units),
                    rows_of(units),
                    full_block((8, 2 * units)),
                ],
                out_shape=[
                    shape((members, 2, padded, D), bf16),
                    shape((total_rows, units), bf16),
                    shape((total_rows, units), bf16),
                    shape((8, 2 * units), f32),
                ],
            )(*hidden[step][:5], out_own, out_peer, in_own, in_peer, bias_out)
        )
    returned = [exchange(r[0]) for r in results]
    flat_rows = [rows.reshape(total_rows, D) for rows in arrived]
    sum_in = sum(column_sum(rows, r[2]) for rows, r in zip(flat_rows, results))
    in_other = across(low(sum_in))
    sum_in_own = sum(column_sum(rows, r[1]) for rows, r in zip(flat_rows, results))
    sum_bin = sum(r[3][:1] for r in results)
    sum_bout = sum(h[5][:1] for h in hidden)
    bias_sums = jnp.concatenate(
        [
            sum_bin[:, units:],
            lax.dynamic_slice_in_dim(sum_bout, peer_place, shard_columns, 1),
        ],
        axis=1,
    )
    bias_other = across(bias_sums)
    grad_bin = sum_bin[:, :units] + bias_other[:, :units]
    grad_bout = (
        lax.dynamic_slice_in_dim(sum_bout, own_place, shard_columns, 1) + bias_other[:, units:]
    )
    backward = []
    for step in range(MB):
        first = step == 0
        here = pl.BlockSpec((1, 1, SEQ, D), lambda i, step=step: (step, 0, 0, 0))

        def of_step(*tail, step=step):
            return pl.BlockSpec((1, *tail), lambda i: (step,) + (0,) * len(tail))

        back = returned[step].reshape(expert_total, half, 2, padded, D)
        outs = [
            (shape(patches.shape, bf16), here),
            (shape(patches.shape, f32), here),
            (shape((SEQ, D), bf16), full_block((SEQ, D))),
            (shape((SEQ, 3 * D), bf16), full_block((SEQ, 3 * D))),
            (shape((SEQ, D), bf16), full_block((SEQ, D))),
            (shape((SEQ, D), bf16), full_block((SEQ, D))),
            (shape((SEQ, 128), bf16), full_block((SEQ, 128))),
            (shape((8, D), f32), full_block((8, D))),
        ]
        earlier = [] if first else list(backward[-1][:2])
        backward.append(
            vmem_call(
                partial(attention_backward_kernel, expert_total),
                grid=(1,),
                in_specs=[
                    here,
                    here,
                    of_step(SEQ, TOPK),
                    full_block(back.shape),
                    of_step(SEQ, 3 * D),
                    of_step(SEQ, D),
                    of_step(SEQ, D),
                    of_step(SEQ, 128),
                    full_block((D, columns)),
                ]
                + [pl.BlockSpec(memory_space=pl.ANY)] * len(earlier),
                out_specs=[o[1] for o in outs],
                out_shape=[o[0] for o in outs],
                input_output_aliases={} if first else {9: 0, 10: 1},
            )(patches, cotangent, target, back, qkv, mixed, middle, probs, gathered, *earlier)
        )
    core_scalar = jnp.reshape(expert % 2, (1,)).astype(jnp.int32)
    block_rows = tensors * attn_weights.shape[0]
    flat_steps = [value for b in backward for value in b[2:]]
    core_shape = (experts // 2, block_rows, columns)
    whole_vmem = pl.BlockSpec(memory_space=pltpu.VMEM)
    held, sending = vmem_call(
        partial(weight_sums_kernel, expert_total),
        in_specs=[in_smem] + [whole_vmem] * (1 + len(flat_steps)),
        out_specs=[whole_vmem] * 2,
        out_shape=[shape(core_shape, f32), shape(core_shape, bf16)],
    )(core_scalar, mixed, *flat_steps)
    mine = scatter_sums(held, sending)
    grad_attn = mine[:, : 4 * D]
    grad_router = mine[:, 4 * D : 4 * D + expert_total]
    grad_norm = mine[:, 4 * D + expert_total : 4 * D + expert_total + 4].T
    attn_first_new, attn_second_new, attn_new = adam_update(
        attn_weights, grad_attn, attn_first, attn_second, RATE_DENSE, DECAY_RATE
    )
    router_first_new, router_second_new, router_new = adam_update(
        router_weights, grad_router, router_first, router_second, RATE_DENSE, DECAY_RATE
    )
    norm_first_new, norm_second_new, norm_new = adam_update(
        norm_params, grad_norm, norm_first, norm_second, RATE_NORMS, 0.0
    )
    w_out_results = soap(
        True,
        RATE_OUTPUT,
        sum_out_own,
        out_other,
        w_out,
        w_out_first,
        w_out_second,
        w_out_stat,
        w_out_basis,
    )
    w_in_results = soap(
        False,
        RATE_INPUT,
        sum_in_own,
        in_other,
        w_in,
        w_in_first,
        w_in_second,
        w_in_stat,
        w_in_basis,
    )
    bin_first_new, bin_second_new, bin_new = adam_update(
        b_in, grad_bin, b_in_first, b_in_second, RATE_BIASES, 0.0
    )
    bout_first_new, bout_second_new, bout_new = adam_update(
        b_out, grad_bout, b_out_first, b_out_second, RATE_OFFSETS, 0.0
    )
    return (
        *backward[-1][:2],
        attn_first_new,
        attn_second_new,
        attn_new,
        low(attn_new),
        router_first_new,
        router_second_new,
        router_new,
        low(router_new),
        norm_first_new,
        norm_second_new,
        norm_new,
        *w_in_results,
        *w_out_results,
        bin_first_new,
        bin_second_new,
        bin_new,
        bout_first_new,
        bout_second_new,
        bout_new,
    )


def solution(mesh):
    tokens = P(None, BOTH, None, None)
    rows = P(BOTH, None)
    columns = P(None, BOTH)
    first_layer = P(EXPERT, None, TENSOR)
    second_layer = P(EXPERT, TENSOR, None)
    blocks = P(EXPERT, TENSOR, None, None)
    biases = P(EXPERT, TENSOR)
    in_specs = (
        (tokens,) * 4
        + (rows,) * 6
        + (columns,) * 3
        + (first_layer,) * 3
        + (blocks,) * 2
        + (second_layer,) * 3
        + (blocks,) * 2
        + (biases,) * 6
    )
    out_specs = (
        (tokens,) * 2
        + (rows,) * 8
        + (columns,) * 3
        + (first_layer,) * 4
        + (blocks,) * 2
        + (second_layer,) * 4
        + (blocks,) * 2
        + (biases,) * 6
    )
    return jax.shard_map(
        per_device, mesh=mesh, in_specs=in_specs, out_specs=out_specs, check_vma=False
    )
```

```python
from functools import partial

import jax
import jax.numpy as jnp
from jax import lax
from jax.experimental import pallas as pl
from jax.experimental.pallas import tpu as pltpu
from jax.sharding import PartitionSpec as P

D = 768
HEADS = 12
HEAD_DIM = 64
SEQ = 196
TOPK = 2
MB = 2
STEP = 10
BLK = 384


MATMUL_ACCURACY = lax.Precision.HIGHEST
NORM_EPS = 1e-06
BETA_FIRST = 0.5
BETA_SECOND = 0.5
STAT_DECAY = 0.5
ADAM_EPS = 1e-08
DECAY_RATE = 0.1
RATE_DENSE = 0.05
RATE_NORMS = 0.4
RATE_INPUT = 0.04
RATE_OUTPUT = 0.4
RATE_BIASES = 0.05
RATE_OFFSETS = 1.0


def column_sum(left_side, right_side):
    return lax.dot_general(
        left_side, right_side, (((0,), (0,)), ((), ())), preferred_element_type=jnp.float32
    )


def row_product(left_side, right_side):
    return lax.dot_general(
        left_side, right_side, (((1,), (1,)), ((), ())), preferred_element_type=jnp.float32
    )


def moment_step(gradient, first_moment, second_moment):
    first_new = BETA_FIRST * first_moment + (1.0 - BETA_FIRST) * gradient
    second_new = BETA_SECOND * second_moment + (1.0 - BETA_SECOND) * gradient * gradient
    normed_step = (
        first_new
        / (1.0 - BETA_FIRST**STEP)
        / (jnp.sqrt(second_new / (1.0 - BETA_SECOND**STEP)) + ADAM_EPS)
    )
    return (first_new, second_new, normed_step)


def adam_update(weight, gradient, first_moment, second_moment, step_rate, weight_decay):
    first_new, second_new, normed_step = moment_step(gradient, first_moment, second_moment)
    return (first_new, second_new, weight - step_rate * (normed_step + weight_decay * weight))


EXPERT = "expert"
TENSOR = "tensor"
BOTH = (EXPERT, TENSOR)
VMEM_LIMIT = 56 * 2**20
FLOPS_PER_US = 1.1e9
ROW_TILE = 512
SUB = 64


def mm(left, right):
    return jnp.dot(left, right, preferred_element_type=jnp.float32, precision=MATMUL_ACCURACY)


def mt(left, right):
    return lax.dot_general(
        left,
        right,
        (((1,), (1,)), ((), ())),
        preferred_element_type=jnp.float32,
        precision=MATMUL_ACCURACY,
    )


def tm(left, right):
    return lax.dot_general(
        left,
        right,
        (((0,), (0,)), ((), ())),
        preferred_element_type=jnp.float32,
        precision=MATMUL_ACCURACY,
    )


def factor_inverse(mats):
    n=SUB; B=jnp.broadcast_to; w=(8,2*n)
    lane=lax.broadcasted_iota(jnp.int32,w,1); sub=lax.broadcasted_iota(jnp.int32,w,0)
    X=[]
    for m in mats:
        tiles=[]
        for i in range(n//8):
            eye=jnp.where(lane==sub+8*i+n,1.0,0.0)
            tiles.append(jnp.concatenate([m[8*i:8*i+8,:],eye[:,n:]],axis=1))
        X.append(tiles)
    outs=[[] for _ in mats]
    for r in range(n//8):
        for m,tiles in enumerate(X):
            T=tiles[r]
            cols=[[B(tiles[t][:,8*r+k:8*r+k+1],w) for k in range(8)] for t in range(r,n//8)]
            a=[[B(cols[0][j][i:i+1,:],w) for j in range(i+1)] for i in range(8)]
            rows=[B(T[i:i+1,:],w) for i in range(8)]
            inv=[None]*8; l=[[None]*8 for _ in range(8)]
            for k in range(8):
                inv[k]=1.0/a[k][k]
                for i in range(k+1,8): l[i][k]=a[i][k]*inv[k]
                for i in range(k+1,8):
                    for j in range(k+1,i+1):
                        a[i][j]=a[i][j]-l[i][k]*a[j][k]
                for i in range(k+1,8): rows[i]=rows[i]-l[i][k]*rows[k]
            o=jnp.zeros(w,jnp.float32)
            for k in range(8): o=jnp.where(sub==k,rows[k]*lax.rsqrt(a[k][k]),o)
            outs[m].append(o[:,n:])
            if r+1<n//8:
                wv=[rows[k]*inv[k] for k in range(8)]
                for k in range(6,-1,-1):
                    for j in range(k+1,8): wv[k]=wv[k]-l[j][k]*wv[j]
                for t in range(r+1,n//8):
                    c=cols[t-r]
                    acc=c[0]*wv[0]
                    for k in range(1,8): acc=acc+c[k]*wv[k]
                    tiles[t]=tiles[t]-acc
    return [jnp.concatenate(o,axis=0) for o in outs]
def renew_kernel(skipped, *refs):
    refs=refs[skipped:]
    m_ref=refs[-1]
    zs=refs[:-2]
    nb=len(zs)
    qs=[refs[-2].at[0,i] for i in range(nb)]
    n=BLK; kb=n//128; h=SUB
    for b in range(nb):
        z=zs[b][...]
        m_ref[b]=tm(z,z)
    for k in range(kb):
        o=128*k; sl=slice(o,o+128)
        d11=[m_ref[b,o:o+h,o:o+h] for b in range(nb)]
        i1=factor_inverse(d11)
        l21=[mt(m_ref[b,o+h:o+128,o:o+h],i1[b]) for b in range(nb)]
        d22=[m_ref[b,o+h:o+128,o+h:o+128]-mt(l21[b],l21[b]) for b in range(nb)]
        i2=factor_inverse(d22)
        inv=[]
        for b in range(nb):
            low=-mm(mm(i2[b],l21[b]),i1[b])
            inv.append(jnp.concatenate([jnp.concatenate([i1[b],jnp.zeros((h,h),jnp.float32)],1),jnp.concatenate([low,i2[b]],1)],0))
        for b in range(nb):
            q=zs[b][:,sl]
            for j in range(k):
                q=q-mt(qs[b][:,128*j:128*j+128],m_ref[b,sl,128*j:128*j+128])
            qs[b][:,sl]=mt(q,inv[b])
            if k+1<kb:
                p=mt(m_ref[b,o+128:,sl],inv[b])
                m_ref[b,o+128:,sl]=p
                m_ref[b,o+128:,o+128:]=m_ref[b,o+128:,o+128:]-mt(p,p)
def renew(tokens, stretched):
    count=len(stretched)
    return vmem_call(
        partial(renew_kernel, len(tokens)),
        30,
        grid=(1,),
        out_shape=jax.ShapeDtypeStruct((1, count, BLK, BLK), jnp.float32),
        in_specs=[pl.BlockSpec(memory_space=pl.ANY)] * len(tokens)
        + [full_block((BLK, BLK))] * count,
        out_specs=full_block((1, count, BLK, BLK)),
        scratch_shapes=[pltpu.VMEM((count, BLK, BLK), jnp.float32)],
    )(*tokens, *stretched)


def low(values):
    return values.astype(jnp.bfloat16)


def wide(values):
    return values.astype(jnp.float32)


def dot(left, right):
    return jnp.dot(left, right, preferred_element_type=jnp.float32)


def vmem_call(kernel, microseconds, **options):
    cost = pl.CostEstimate(
        flops=int(microseconds * FLOPS_PER_US), bytes_accessed=0, transcendentals=0
    )
    return pl.pallas_call(
        kernel,
        compiler_params=pltpu.CompilerParams(vmem_limit_bytes=VMEM_LIMIT),
        cost_estimate=cost,
        **options,
    )


def full_block(shape):
    return pl.BlockSpec(shape, lambda *_: (0,) * len(shape))


def norm_parts(values):
    centred = values - jnp.mean(values, axis=-1, keepdims=True)
    scale = lax.rsqrt(jnp.mean(centred * centred, axis=-1, keepdims=True) + NORM_EPS)
    return centred * scale, scale


def norm_backward(grads, normed, scale, gain):
    inner = grads * gain
    return scale * (
        inner
        - jnp.mean(inner, axis=-1, keepdims=True)
        - normed * jnp.mean(inner * normed, axis=-1, keepdims=True)
    )


def route_mask(target, slot_total):
    slot_index = lax.broadcasted_iota(jnp.int32, (target.shape[0], slot_total), 1)
    hit = (slot_index == target[:, :1]) | (slot_index == target[:, 1:2])
    return jnp.where(hit, 1.0, 0.0)


def masked_softmax(logits, count):
    lanes = lax.broadcasted_iota(jnp.int32, logits.shape, 1)
    inside = lanes < count
    peak = jnp.max(jnp.where(inside, logits, -jnp.inf), axis=-1, keepdims=True)
    raised = jnp.where(inside, jnp.exp(jnp.where(inside, logits - peak, 0.0)), 0.0)
    return raised / jnp.sum(raised, axis=-1, keepdims=True)


def softmax_rows(scores):
    raised = jnp.exp(scores - jnp.max(scores, axis=-1, keepdims=True))
    return raised / jnp.sum(raised, axis=-1, keepdims=True)


def dispatch_kernel(target_ref, rows_ref, out_ref):
    experts, copies, steps, padded, _ = out_ref.shape
    for step in range(steps):
        routing = low(route_mask(target_ref[step], experts * padded))
        rows = column_sum(routing, rows_ref[step, 0])
        rows = low(rows.reshape(experts, padded, D))
        for copy in range(copies):
            out_ref[:, copy, step] = rows


def attention_kernel(experts, x_ref, target_ref, a_ref, *refs):
    out_refs = refs[:MB]
    qkv_ref, mixed_ref, middle_ref, probs_ref, score_ref, weight_ref = refs[MB:]
    copies, padded = out_refs[0].shape[1:3]
    inputs = wide(x_ref[0, 0])
    extra = a_ref[:, 4 * D :]
    vectors = wide(extra).T
    gains = [vectors[experts + i : experts + i + 1] for i in range(4)]
    normed, _ = norm_parts(inputs)
    normed_low = low(normed * gains[0] + gains[1])
    qkv_ref[0] = low(dot(normed_low, a_ref[:, : 3 * D]))
    lanes = lax.broadcasted_iota(jnp.int32, (SEQ, 2 * HEAD_DIM), 1)
    for head in range(HEADS):
        start = 2 * HEAD_DIM * (head // 2)
        query = qkv_ref[0, :, start : start + 2 * HEAD_DIM]
        keys = qkv_ref[0, :, D + start : D + start + 2 * HEAD_DIM]
        here = (lanes < HEAD_DIM) if head % 2 == 0 else (lanes >= HEAD_DIM)
        score_ref[head] = row_product(jnp.where(here, query, 0), keys) * HEAD_DIM ** (-0.5)
    weight_ref[...] = low(softmax_rows(score_ref[...]))
    for pair in range(HEADS // 2):
        start = 2 * HEAD_DIM * pair
        values = qkv_ref[0, :, 2 * D + start : 2 * D + start + 2 * HEAD_DIM]
        both = [dot(weight_ref[2 * pair + side], values) for side in range(2)]
        mixed_ref[0, :, start : start + 2 * HEAD_DIM] = low(
            jnp.where(lanes < HEAD_DIM, both[0], both[1])
        )
    middle = inputs + dot(mixed_ref[0], a_ref[:, 3 * D : 4 * D])
    middle_ref[0] = middle
    normed, _ = norm_parts(middle)
    moe_low = low(normed * gains[2] + gains[3])
    probs_ref[0] = masked_softmax(dot(moe_low, extra), experts)
    routing = low(route_mask(target_ref[0], experts * padded))
    rows = low(column_sum(routing, moe_low).reshape(experts, padded, D))
    for step, out_ref in enumerate(out_refs):

        @pl.when(pl.program_id(0) == step)
        def _(out_ref=out_ref):
            for copy in range(copies):
                out_ref[:, copy] = rows


def attention_backward_kernel(experts, skipped, *refs):
    refs = refs[skipped:]
    x_ref, up_ref, target_ref, back_ref, qkv_ref, mixed_ref, middle_ref, probs_ref, a_ref = refs[:9]
    score_ref, slope_ref, weight_ref, grad_score_ref = refs[-4:]
    out_ref, grad_ref, normed_ref, joined_ref, branch_ref, moe_ref, logit_ref, vector_ref = refs[
        -12:-4
    ]
    copies, padded = (back_ref.shape[1], back_ref.shape[3])
    slot_total = experts * padded
    extra = a_ref[:, 4 * D :]
    vectors = wide(extra).T
    gains = [vectors[experts + i : experts + i + 1] for i in range(4)]
    inputs = wide(x_ref[0, 0])
    upstream_low = up_ref[0, 0]
    upstream = wide(upstream_low)
    middle = middle_ref[0]
    probs = probs_ref[0]

    def collected(kind):
        total = wide(back_ref[:, 0, kind])
        for copy in range(1, copies):
            total = total + wide(back_ref[:, copy, kind])
        return low(total.reshape(slot_total, D))

    coming = collected(0)
    grad_coming = collected(1)
    routing = route_mask(target_ref[0], slot_total)
    member = jnp.where(
        lax.broadcasted_iota(jnp.int32, (probs.shape[1], slot_total), 1) // padded
        == lax.broadcasted_iota(jnp.int32, (probs.shape[1], slot_total), 0),
        1.0,
        0.0,
    )
    member_low = low(member)
    probs_high = low(probs)
    slot_gate = routing * (dot(probs_high, member_low) + dot(low(probs - wide(probs_high)), member_low))
    gate_high = low(slot_gate)
    final = middle + dot(gate_high, coming) + dot(low(slot_gate - wide(gate_high)), coming)
    out_ref[0, 0] = low(final)
    slot_grads = routing * row_product(upstream_low, coming)
    slot_high = low(slot_grads)
    prob_grads = row_product(slot_high, member_low) + row_product(
        low(slot_grads - wide(slot_high)), member_low
    )
    logit_low = low(
        probs * (prob_grads - jnp.sum(prob_grads * probs, axis=-1, keepdims=True))
    )
    logit_ref[...] = logit_low
    moe_grad = dot(low(routing), grad_coming) + row_product(logit_low, extra)
    normed, scale = norm_parts(middle)
    moe_ref[...] = low(normed * gains[2] + gains[3])
    vector_ref[2:3] = jnp.sum(moe_grad * normed, axis=0, keepdims=True)
    vector_ref[3:4] = jnp.sum(moe_grad, axis=0, keepdims=True)
    grad_middle = upstream + norm_backward(moe_grad, normed, scale, gains[2])
    branch_low = low(grad_middle)
    branch_ref[...] = branch_low
    grad_mixed = low(row_product(branch_low, a_ref[:, 3 * D : 4 * D]))
    lanes = lax.broadcasted_iota(jnp.int32, (SEQ, 2 * HEAD_DIM), 1)
    for head in range(HEADS):
        start = 2 * HEAD_DIM * (head // 2)
        stop = start + 2 * HEAD_DIM
        query = qkv_ref[0, :, start:stop]
        keys = qkv_ref[0, :, D + start : D + stop]
        values = qkv_ref[0, :, 2 * D + start : 2 * D + stop]
        here = (lanes < HEAD_DIM) if head % 2 == 0 else (lanes >= HEAD_DIM)
        score_ref[head] = row_product(jnp.where(here, query, 0), keys) * HEAD_DIM ** (-0.5)
        slope_ref[head] = row_product(jnp.where(here, grad_mixed[:, start:stop], 0), values)
    weights = softmax_rows(score_ref[...])
    weight_ref[...] = low(weights)
    slopes = slope_ref[...]
    grad_score_ref[...] = low(
        weights * (slopes - jnp.sum(slopes * weights, axis=-1, keepdims=True))
    )
    for pair in range(HEADS // 2):
        start = 2 * HEAD_DIM * pair
        stop = start + 2 * HEAD_DIM
        query = qkv_ref[0, :, start:stop]
        keys = qkv_ref[0, :, D + start : D + stop]
        grad_here = grad_mixed[:, start:stop]
        results = []
        for side in range(2):
            grad_scores = grad_score_ref[2 * pair + side]
            results.append(
                (
                    dot(grad_scores, keys) * HEAD_DIM ** (-0.5),
                    column_sum(grad_scores, query) * HEAD_DIM ** (-0.5),
                    column_sum(weight_ref[2 * pair + side], grad_here),
                )
            )
        for part in range(3):
            joined_ref[:, part * D + start : part * D + stop] = low(
                jnp.where(lanes < HEAD_DIM, results[0][part], results[1][part])
            )
    grad_normed = row_product(joined_ref[...], a_ref[:, : 3 * D])
    normed, scale = norm_parts(inputs)
    normed_ref[...] = low(normed * gains[0] + gains[1])
    vector_ref[4:8] = jnp.zeros((4, D), jnp.float32)
    vector_ref[0:1] = jnp.sum(grad_normed * normed, axis=0, keepdims=True)
    vector_ref[1:2] = jnp.sum(grad_normed, axis=0, keepdims=True)
    grad_ref[0, 0] = grad_middle + norm_backward(grad_normed, normed, scale, gains[0])


def weight_sums_kernel(experts, after_ref, core_ref, mixed_ref, *refs):
    own_ref, other_ref, token_ref = refs[-3:]
    token_ref[...] = jnp.zeros_like(token_ref)
    steps = [refs[6 * i : 6 * i + 6] for i in range(MB)]
    held, block, _ = own_ref.shape
    first_core = core_ref[0] == 0

    def write(total, start):
        stop = start + total.shape[1]
        pairs = total.reshape(held, 2, block, total.shape[1])
        even, odd = (pairs[:, 0], pairs[:, 1])
        own_ref[:, :, start:stop] = jnp.where(first_core, even, odd)
        other_ref[:, :, start:stop] = low(jnp.where(first_core, odd, even))

    for part in range(3):
        total = sum(column_sum(s[0][...], s[1][:, part * D : part * D + D]) for s in steps)
        write(total, part * D)
    write(sum(column_sum(mixed_ref[i], s[2][...]) for i, s in enumerate(steps)), 3 * D)
    vectors = sum(s[5][...] for s in steps)
    vectors = jnp.concatenate(
        [
            jnp.zeros((experts, D), jnp.float32),
            vectors,
            jnp.zeros((128 - experts - vectors.shape[0], D), jnp.float32),
        ],
        axis=0,
    )
    write(sum(column_sum(s[3][...], s[4][...]) for s in steps) + vectors.T, 4 * D)


def gelu_parts(values):
    raised = jnp.exp(-0.5 * values * values)
    root = 1.0 / (1.0 + (0.3275911 * 0.5**0.5) * jnp.abs(values))
    tail = 1.061405429 * root - 1.453152027
    tail = tail * root + 1.421413741
    tail = tail * root - 0.284496736
    tail = tail * root + 0.254829592
    tail = 0.5 * tail * root * raised
    return jnp.where(values >= 0.0, 1.0 - tail, tail), raised * 0.3989422804014327


def hidden_kernel(
    experts,
    expert_ref,
    rows_ref,
    up_ref,
    router_ref,
    weight_ref,
    bias_ref,
    hidden_ref,
    slope_ref,
    grad_ref,
    sum_ref,
):
    count, padded = rows_ref.shape[:2]
    units = weight_ref.shape[2]
    rows = low(wide(rows_ref[...]).reshape(count * padded, D))
    probs = masked_softmax(dot(rows, router_ref[...]), experts)
    lanes = lax.broadcasted_iota(jnp.int32, probs.shape, 1)
    gate = jnp.sum(jnp.where(lanes == expert_ref[0], probs, 0.0), axis=-1, keepdims=True)
    grad = low(gate * wide(up_ref[...]).reshape(count * padded, D))
    grad_ref[...] = grad

    @pl.when(pl.program_id(0) == 0)
    def _():
        sum_ref[...] = jnp.zeros_like(sum_ref)

    sum_ref[0:1] += jnp.sum(wide(grad), axis=0, keepdims=True)
    for side in range(2):
        values = dot(rows, weight_ref[side]) + bias_ref[:, side * units : (side + 1) * units]
        area, density = gelu_parts(values)
        hidden_ref[side] = low(values * area)
        slope_ref[side] = low(area + values * density)


def result_kernel(skipped, *refs):
    (
        hidden_ref,
        slope_ref,
        grad_ref,
        out_ref,
        in_ref,
        bias_ref,
        back_ref,
        pre_ref,
        sum_ref,
    ) = refs[skipped:]
    count, _, padded, _ = back_ref.shape
    units = in_ref.shape[2]

    @pl.when(pl.program_id(0) == 0)
    def _():
        sum_ref[...] = jnp.zeros_like(sum_ref)

    out_term = dot(hidden_ref[0], out_ref[0]) + dot(hidden_ref[1], out_ref[1]) + bias_ref[...]
    back_ref[:, 0] = low(out_term.reshape(count, padded, D))
    grad_term = None
    for side in range(2):
        pre = low(row_product(grad_ref[...], out_ref[side]) * wide(slope_ref[side]))
        pre_ref[side] = pre
        sum_ref[0:1, side * units : (side + 1) * units] += jnp.sum(
            wide(pre), axis=0, keepdims=True
        )
        term = row_product(pre, in_ref[side])
        grad_term = term if grad_term is None else grad_term + term
    back_ref[:, 1] = low(grad_term.reshape(count, padded, D))


def split(values):
    high = low(values)
    return high, low(values - wide(high))


def split_dot(left, right, dims):
    def one(a, b):
        return lax.dot_general(a, b, (dims, ((), ())), preferred_element_type=jnp.float32)

    return one(left[0], right[0]) + (one(left[0], right[1]) + one(left[1], right[0]))


def turn_kernel(along_rows, rate, skipped, *refs):
    refs = refs[skipped:]
    gradient_ref, weight_ref, first_ref, second_ref, stat_ref, basis_ref = refs[:6]
    first_out, second_out, weight_out, copy_out, stat_out, stretched_out = refs[-6:]
    gradient = gradient_ref[...]
    basis = basis_ref[0, 0]
    basis_parts = split(basis)
    if along_rows:
        turned = column_sum(basis_parts[0], gradient) + column_sum(basis_parts[1], gradient)
        outer = row_product(gradient, gradient)
    else:
        turned = dot(gradient, basis_parts[0]) + dot(gradient, basis_parts[1])
        outer = column_sum(gradient, gradient)
    first_new, second_new, step = moment_step(turned, first_ref[0], second_ref[0])
    first_out[0] = first_new
    second_out[0] = second_new
    step_parts = split(step)
    if along_rows:
        returned = split_dot(basis_parts, step_parts, ((1,), (0,)))
    else:
        returned = split_dot(step_parts, basis_parts, ((1,), (1,)))
    weight = weight_ref[0]
    weight_new = weight - rate * (returned + DECAY_RATE * weight)
    weight_out[0] = weight_new
    copy_out[0] = low(weight_new)
    stat_new = STAT_DECAY * stat_ref[0, 0] + (1.0 - STAT_DECAY) * outer
    stat_out[0, 0] = stat_new
    stretched_out[...] = mm(stat_new, basis)


def dense_update_kernel(kept_ref, received_ref, *refs):
    inputs, outputs = (refs[:9], refs[9:])
    gradient = kept_ref[...] + wide(received_ref[...])
    extra = gradient[:, 4 * D :]
    experts = inputs[3].shape[1]
    gradients = (gradient[:, : 4 * D], extra[:, :experts], extra.T[experts : experts + 4])
    rates = ((RATE_DENSE, DECAY_RATE), (RATE_DENSE, DECAY_RATE), (RATE_NORMS, 0.0))
    place = 0
    for kind in range(3):
        weight, first, second = (r[...] for r in inputs[3 * kind : 3 * kind + 3])
        first_new, second_new, weight_new = adam_update(
            weight, gradients[kind], first, second, *rates[kind]
        )
        outputs[place][...] = first_new
        outputs[place + 1][...] = second_new
        outputs[place + 2][...] = weight_new
        place += 3
        if kind < 2:
            outputs[place][...] = low(weight_new)
            place += 1


def row_sums_kernel(*refs):
    total = sum(column_sum(refs[i][...], refs[MB + i][...]) for i in range(MB))
    refs[-1][...] = low(total)


def swap(values, axis, distance):
    size = lax.axis_size(axis)
    return lax.ppermute(values, axis, [(i, i ^ distance) for i in range(size)])


def across(values):
    size = lax.axis_size(TENSOR)
    return lax.ppermute(values, TENSOR, [(i, (i + size // 2) % size) for i in range(size)])


def ordered(bit, mine, other):
    return jnp.where(bit == 0, jnp.stack([mine, other]), jnp.stack([other, mine]))


def gather_tensor(shard):
    tensors, tensor = (lax.axis_size(TENSOR), lax.axis_index(TENSOR))
    block = shard[None]
    distance = 1
    while distance < tensors:
        other = swap(block, TENSOR, distance)
        block = ordered((tensor // distance) % 2, block, other).reshape(-1, *shard.shape)
        distance *= 2
    return block


def gather_experts(block, beside, released, waiting):
    experts, tensors = (lax.axis_size(EXPERT), lax.axis_size(TENSOR))
    expert = lax.axis_index(EXPERT)
    columns = block.shape[-1]
    block = block[None]
    distance = 2
    while distance < experts // 4:
        other = swap(block, EXPERT, distance)
        block = ordered((expert // distance) % 2, block, other).reshape(-1, *block.shape[1:])
        distance *= 2
    near, far = (distance, 2 * distance)
    middle = tensors // 2
    from_near, from_far = (swap(block, EXPERT, near), swap(block, EXPERT, far))
    corner = jnp.concatenate(
        [swap(from_far[:, :middle], EXPERT, near), swap(from_near[:, middle:], EXPERT, far)],
        axis=1,
    )
    corner, beside, released, waiting = lax.optimization_barrier(
        (corner, beside, released, waiting)
    )
    pieces = (block, from_near, from_far, corner)
    crossed = [swap(piece, EXPERT, 1) for piece in pieces]
    near_bit, far_bit = ((expert // near) % 2, (expert // far) % 2)

    def arranged(four):
        return ordered(
            far_bit,
            ordered(near_bit, four[0], four[1]),
            ordered(near_bit, four[2], four[3]),
        ).reshape(-1, *block.shape[1:])

    whole = ordered(expert % 2, arranged(pieces), arranged(crossed))
    whole = jnp.moveaxis(whole, 0, 1)
    return whole.reshape(-1, columns), beside, across(released), waiting


def scatter_sums(held, sending):
    experts, tensors = (lax.axis_size(EXPERT), lax.axis_size(TENSOR))
    expert, tensor = (lax.axis_index(EXPERT), lax.axis_index(TENSOR))
    columns = held.shape[2]

    def pick(values, index, axis=0):
        return lax.dynamic_index_in_dim(values, index, axis, False)

    held = held + wide(swap(sending, EXPERT, 1))
    stages = [held]
    near, far = (experts // 4, experts // 2)
    near_bit, far_bit = ((expert // near) % 2, (expert // far) % 2)
    held = held.reshape(4, experts // 8, tensors, -1, columns)
    place = 2 * far_bit + near_bit
    own, to_near, to_far, to_corner = (
        pick(held, place),
        pick(held, place ^ 1),
        pick(held, place ^ 2),
        pick(held, place ^ 3),
    )
    middle = tensors // 2
    passed_near = swap(low(to_corner[:, :middle]), EXPERT, near)
    passed_far = swap(low(to_corner[:, middle:]), EXPERT, far)
    to_far = jnp.concatenate([to_far[:, :middle] + wide(passed_near), to_far[:, middle:]], axis=1)
    to_near = jnp.concatenate([to_near[:, :middle], to_near[:, middle:] + wide(passed_far)], axis=1)
    stages.append(to_near)
    held = (
        own
        + wide(swap(low(to_near), EXPERT, near))
        + wide(swap(low(to_far), EXPERT, far))
    )
    distance = experts // 8
    while distance >= 2:
        bit = (expert // distance) % 2
        halves = held.reshape(2, -1, *held.shape[1:])
        held = pick(halves, bit) + wide(swap(low(pick(halves, 1 - bit)), EXPERT, distance))
        distance //= 2
    stages.append(held)
    held = held.reshape(tensors, -1, columns)
    distance = tensors // 2
    while distance >= 1:
        bit = (tensor // distance) % 2
        halves = held.reshape(2, -1, *held.shape[1:])
        kept = pick(halves, bit)
        received = swap(low(pick(halves, 1 - bit)), TENSOR, distance)
        if distance > 1:
            held = kept + wide(received)
        distance //= 2
    stages.append(kept)
    return kept.reshape(-1, columns), received.reshape(-1, columns), stages


def soap_turn(along_rows, rate, at, token, gradient, state, statistics, earlier):
    weight, first, second = state
    statistic = statistics[0]
    f32 = jnp.float32
    if along_rows:
        deep = pl.BlockSpec((1, BLK, D), lambda i: (0, at, 0))
    else:
        deep = pl.BlockSpec((1, D, BLK), lambda i: (0, 0, at))
    square = pl.BlockSpec((1, 1, BLK, BLK), lambda i: (0, at, 0, 0))
    anywhere = pl.BlockSpec(memory_space=pl.ANY)
    return vmem_call(
        partial(turn_kernel, along_rows, rate, len(token)),
        8,
        grid=(1,),
        in_specs=[anywhere] * len(token)
        + [full_block(gradient.shape)]
        + [deep] * 3
        + [square] * 2
        + [anywhere] * len(earlier),
        out_specs=[deep] * 4 + [square, full_block((BLK, BLK))],
        out_shape=[jax.ShapeDtypeStruct(weight.shape, f32)] * 3
        + [
            jax.ShapeDtypeStruct(weight.shape, jnp.bfloat16),
            jax.ShapeDtypeStruct(statistic.shape, f32),
            jax.ShapeDtypeStruct((BLK, BLK), f32),
        ],
        input_output_aliases={6 + len(token) + i: i for i in range(len(earlier))},
    )(*token, gradient, *state, *statistics, *earlier)


def row_sums(left, right, at, left_paired):
    rows, width = left[0].shape[-2:]
    height, columns = (BLK, right[0].shape[-1]) if left_paired else (width, BLK)
    paired = pl.BlockSpec((None, rows, BLK), lambda i: (i, 0, at))
    plain = full_block((rows, columns if left_paired else width))
    return vmem_call(
        row_sums_kernel,
        5,
        grid=(2,),
        in_specs=[paired if left_paired else plain] * MB
        + [plain if left_paired else paired] * MB,
        out_specs=pl.BlockSpec((None, height, columns), lambda i: (i, 0, 0)),
        out_shape=jax.ShapeDtypeStruct((2, height, columns), jnp.bfloat16),
    )(*left, *right)


def per_device(
    patches,
    cotangent,
    expert_ids,
    slots,
    attn_weights,
    attn_first,
    attn_second,
    router_weights,
    router_first,
    router_second,
    norm_params,
    norm_first,
    norm_second,
    w_in,
    w_in_first,
    w_in_second,
    w_in_stat,
    w_in_basis,
    w_out,
    w_out_first,
    w_out_second,
    w_out_stat,
    w_out_basis,
    b_in,
    b_in_first,
    b_in_second,
    b_out,
    b_out_first,
    b_out_second,
):
    tokens_here = SEQ
    expert_total = router_weights.shape[1]
    capacity = (105 * TOPK * tokens_here + 100 * expert_total - 1) // (100 * expert_total)
    padded = 8 * ((capacity + 7) // 8)
    experts, tensors = (lax.axis_size(EXPERT), lax.axis_size(TENSOR))
    expert, tensor = (lax.axis_index(EXPERT), lax.axis_index(TENSOR))
    half = tensors // 2
    members = expert_total * half
    units = w_in.shape[2]
    shard_columns = b_out.shape[1]
    columns = 4 * D + 128
    bf16, f32 = (jnp.bfloat16, jnp.float32)
    shape = jax.ShapeDtypeStruct
    pairs = [[i, i + half] for i in range(half)]
    groups = [
        [e * tensors + z for e in range(experts) for z in range(h * half, (h + 1) * half)]
        for h in range(2)
    ]

    def exchange(values):
        return lax.all_to_all(values, BOTH, 0, 0, axis_index_groups=groups, tiled=True)

    packed = jnp.concatenate(
        [
            low(attn_weights),
            low(router_weights),
            low(norm_params).T,
            jnp.zeros((attn_weights.shape[0], 128 - expert_total - 4), bf16),
        ],
        axis=1,
    )
    in_own, out_own = (low(w_in[0]), low(w_out[0]))
    b_in_low, b_out_low = (low(b_in), low(b_out))
    peer_bias = across(jnp.concatenate([b_in_low, b_out_low], axis=1))
    chosen = expert_ids.reshape(MB, tokens_here, TOPK)
    placed = slots.reshape(MB, tokens_here, TOPK)
    target = jnp.where(placed < capacity, chosen * padded + placed, -1)
    up_sent = vmem_call(
        dispatch_kernel,
        4,
        grid=(1,),
        in_specs=[full_block(target.shape), full_block(cotangent.shape)],
        out_specs=full_block((expert_total, half, MB, padded, D)),
        out_shape=shape((expert_total, half, MB, padded, D), bf16),
    )(target, cotangent)
    first_stage, peer_bias, sent_first = lax.optimization_barrier(
        (gather_tensor(packed), peer_bias, in_own[: D // 2])
    )
    out_pair = lax.all_gather(out_own, TENSOR, axis_index_groups=pairs)
    gathered, in_first, in_second, up_sent = gather_experts(
        first_stage, across(sent_first), in_own[D // 2 :], up_sent
    )
    up_all = exchange(up_sent.reshape(members, MB, padded, D))
    upper = tensor >= half
    peer_in = peer_bias[:, :units]
    bias_in = wide(
        jnp.where(
            upper,
            jnp.concatenate([peer_in, b_in_low], axis=1),
            jnp.concatenate([b_in_low, peer_in], axis=1),
        )
    )
    bias_out = jnp.zeros((1, D), f32)
    own_place = tensor * shard_columns
    peer_place = ((tensor + half) % tensors) * shard_columns
    bias_out = lax.dynamic_update_slice(bias_out, wide(b_out_low), (0, own_place))
    bias_out = lax.dynamic_update_slice(bias_out, wide(peer_bias[:, units:]), (0, peer_place))
    image = pl.BlockSpec((1, 1, SEQ, D), lambda i: (i, 0, 0, 0))

    def per_step(*tail):
        return pl.BlockSpec((1, *tail), lambda i: (i,) + (0,) * len(tail))

    *sent, qkv, mixed, middle, probs = vmem_call(
        partial(attention_kernel, expert_total),
        11,
        grid=(MB,),
        in_specs=[image, per_step(SEQ, TOPK), full_block((D, columns))],
        out_specs=[
            *[full_block((expert_total, half, padded, D))] * MB,
            per_step(SEQ, 3 * D),
            per_step(SEQ, D),
            per_step(SEQ, D),
            per_step(SEQ, 128),
        ],
        out_shape=[
            *[shape((expert_total, half, padded, D), bf16)] * MB,
            shape((MB, SEQ, 3 * D), bf16),
            shape((MB, SEQ, D), bf16),
            shape((MB, SEQ, D), f32),
            shape((MB, SEQ, 128), f32),
        ],
        scratch_shapes=[pltpu.VMEM((HEADS, SEQ, SEQ), f32), pltpu.VMEM((HEADS, SEQ, SEQ), bf16)],
    )(patches, target, gathered)
    earlier, up_all, in_second = lax.optimization_barrier((sent[0], up_all, in_second))
    in_peer = jnp.concatenate([in_first, in_second], axis=0)
    in_pair = jnp.where(upper, jnp.stack([in_peer, in_own]), jnp.stack([in_own, in_peer]))
    arrived = [exchange(earlier.reshape(members, padded, D))]
    later, arrived[0] = lax.optimization_barrier((sent[1], arrived[0]))
    arrived.append(exchange(later.reshape(members, padded, D)))
    count = max(
        n
        for n in range(1, members + 1)
        if members % n == 0 and n * padded <= ROW_TILE and (n * padded) % 16 == 0
    )
    tile = count * padded
    total_rows = members * padded
    tiles = members // count

    def rows_of(width):
        return pl.BlockSpec((tile, width), lambda i: (i, 0))

    expert_scalar = jnp.reshape(expert, (1,)).astype(jnp.int32)
    in_smem = pl.BlockSpec(memory_space=pltpu.SMEM)
    anywhere = pl.BlockSpec(memory_space=pl.ANY)
    both_rows = pl.BlockSpec((2, tile, units), lambda i: (0, i, 0))
    both_shape = shape((2, total_rows, units), bf16)
    hidden = []
    for step in range(MB):
        hidden.append(
            vmem_call(
                partial(hidden_kernel, expert_total),
                12,
                grid=(tiles,),
                in_specs=[
                    in_smem,
                    pl.BlockSpec((count, padded, D), lambda i: (i, 0, 0)),
                    pl.BlockSpec((count, None, padded, D), lambda i, step=step: (i, step, 0, 0)),
                    pl.BlockSpec((D, 128), lambda i: (0, 4 * D // 128)),
                    full_block((2, D, units)),
                    full_block((1, 2 * units)),
                ],
                out_specs=[both_rows] * 2 + [rows_of(D), full_block((8, D))],
                out_shape=[both_shape] * 2
                + [shape((total_rows, D), bf16), shape((8, D), f32)],
            )(expert_scalar, arrived[step], up_all, gathered, in_pair, bias_in)
        )
    blocks = units // BLK
    row_grads = [h[2] for h in hidden]
    sum_out = [row_sums([h[0] for h in hidden], row_grads, at, True) for at in range(blocks)]
    results = []
    for step in range(MB):
        before = [] if step == 0 else sum_out
        results.append(
            vmem_call(
                partial(result_kernel, len(before)),
                12,
                grid=(tiles,),
                in_specs=[anywhere] * len(before)
                + [both_rows] * 2
                + [
                    rows_of(D),
                    full_block((2, units, D)),
                    full_block((2, D, units)),
                    full_block((1, D)),
                ],
                out_specs=[
                    pl.BlockSpec((count, 2, padded, D), lambda i: (i, 0, 0, 0)),
                    both_rows,
                    full_block((8, 2 * units)),
                ],
                out_shape=[
                    shape((members, 2, padded, D), bf16),
                    both_shape,
                    shape((8, 2 * units), f32),
                ],
            )(*before, *hidden[step][:3], out_pair, in_pair, bias_out)
        )
    flat_rows = [rows.reshape(total_rows, D) for rows in arrived]
    sum_in = [row_sums(flat_rows, [r[1] for r in results], at, False) for at in range(blocks)]

    def shared(sums):
        return lax.psum_scatter(sums, TENSOR, axis_index_groups=pairs)

    grads_out = [shared(sums) for sums in sum_out]
    grads_in = [shared(sums) for sums in sum_in]
    returned = [exchange(r[0]) for r in results]
    sum_bin = sum(r[2][:1] for r in results)
    sum_bout = sum(h[3][:1] for h in hidden)
    bias_sums = jnp.concatenate(
        [
            jnp.where(upper, sum_bin[:, :units], sum_bin[:, units:]),
            lax.dynamic_slice_in_dim(sum_bout, peer_place, shard_columns, 1),
        ],
        axis=1,
    )
    bias_other = across(bias_sums)
    backward = []
    tokens = [sum_in]
    for step in range(MB):
        first = step == 0
        here = pl.BlockSpec((1, 1, SEQ, D), lambda i, step=step: (step, 0, 0, 0))

        def of_step(*tail, step=step):
            return pl.BlockSpec((1, *tail), lambda i: (step,) + (0,) * len(tail))

        back = returned[step].reshape(expert_total, half, 2, padded, D)
        outs = [
            (shape(patches.shape, bf16), here),
            (shape(patches.shape, f32), here),
            (shape((SEQ, D), bf16), full_block((SEQ, D))),
            (shape((SEQ, 3 * D), bf16), full_block((SEQ, 3 * D))),
            (shape((SEQ, D), bf16), full_block((SEQ, D))),
            (shape((SEQ, D), bf16), full_block((SEQ, D))),
            (shape((SEQ, 128), bf16), full_block((SEQ, 128))),
            (shape((8, D), f32), full_block((8, D))),
        ]
        earlier = [] if first else list(backward[-1][:2])
        backward.append(
            vmem_call(
                partial(attention_backward_kernel, expert_total, len(tokens[step])),
        15,
                grid=(1,),
                in_specs=[anywhere] * len(tokens[step])
                + [
                    here,
                    here,
                    of_step(SEQ, TOPK),
                    full_block(back.shape),
                    of_step(SEQ, 3 * D),
                    of_step(SEQ, D),
                    of_step(SEQ, D),
                    of_step(SEQ, 128),
                    full_block((D, columns)),
                ]
                + [pl.BlockSpec(memory_space=pl.ANY)] * len(earlier),
                out_specs=[o[1] for o in outs],
                out_shape=[o[0] for o in outs],
                scratch_shapes=[pltpu.VMEM((HEADS, SEQ, SEQ), f32)] * 2
                + [pltpu.VMEM((HEADS, SEQ, SEQ), bf16)] * 2,
                input_output_aliases={}
                if first
                else {9 + len(tokens[step]): 0, 10 + len(tokens[step]): 1},
            )(
                *tokens[step],
                patches,
                cotangent,
                target,
                back,
                qkv,
                mixed,
                middle,
                probs,
                gathered,
                *earlier,
            )
        )
        if first:
            out_turned = [
                soap_turn(
                    True,
                    RATE_OUTPUT,
                    0,
                    [backward[0][6]],
                    grads_out[0],
                    (w_out, w_out_first, w_out_second),
                    (w_out_stat, w_out_basis),
                    [],
                )
            ]
            tokens.append([out_turned[0][5]])
    core_scalar = jnp.reshape(expert % 2, (1,)).astype(jnp.int32)
    block_rows = tensors * attn_weights.shape[0]
    flat_steps = [value for b in backward for value in b[2:]]
    core_shape = (experts // 2, block_rows, columns)
    held, sending, token = vmem_call(
        partial(weight_sums_kernel, expert_total),
        8,
        grid=(1,),
        in_specs=[anywhere, in_smem] + [full_block(v.shape) for v in (mixed, *flat_steps)],
        out_specs=[full_block(core_shape)] * 2 + [full_block((8, 128))],
        out_shape=[shape(core_shape, f32), shape(core_shape, bf16), shape((8, 128), f32)],
    )(b_in_low, core_scalar, mixed, *flat_steps)
    kept, received, stages = scatter_sums(held, sending)
    dense = [shape(attn_weights.shape, f32)] * 3 + [shape(attn_weights.shape, bf16)]
    routers = [shape(router_weights.shape, f32)] * 3 + [shape(router_weights.shape, bf16)]
    norms = [shape(norm_params.shape, f32)] * 3
    states = (
        kept,
        received,
        attn_weights,
        attn_first,
        attn_second,
        router_weights,
        router_first,
        router_second,
        norm_params,
        norm_first,
        norm_second,
    )
    updated_shapes = dense + routers + norms
    updated = vmem_call(
        dense_update_kernel,
        3,
        grid=(1,),
        in_specs=[full_block(v.shape) for v in states],
        out_specs=[full_block(v.shape) for v in updated_shapes],
        out_shape=updated_shapes,
    )(*states)
    for at in range(1, blocks):
        out_turned.append(
            soap_turn(
                True,
                RATE_OUTPUT,
                at,
                [token],
                grads_out[at],
                (w_out, w_out_first, w_out_second),
                (w_out_stat, w_out_basis),
                out_turned[-1][:5],
            )
        )
    w_out_basis_new = renew(stages[:1], [turned[5] for turned in out_turned])
    in_turned = []
    for at in range(blocks):
        in_turned.append(
            soap_turn(
                False,
                RATE_INPUT,
                at,
                [w_out_basis_new, stages[1]] if at == 0 else [in_turned[-1][5], stages[2]],
                grads_in[at],
                (w_in, w_in_first, w_in_second),
                (w_in_stat, w_in_basis),
                in_turned[-1][:5] if at > 0 else [],
            )
        )
    w_in_basis_new = renew(stages[3:], [turned[5] for turned in in_turned])
    bias_other, w_in_basis_new = lax.optimization_barrier((bias_other, w_in_basis_new))
    w_in_results = (*in_turned[-1][:5], w_in_basis_new)
    w_out_results = (*out_turned[-1][:5], w_out_basis_new)
    own_bin = jnp.where(upper, sum_bin[:, units:], sum_bin[:, :units])
    grad_bin = own_bin + bias_other[:, :units]
    grad_bout = (
        lax.dynamic_slice_in_dim(sum_bout, own_place, shard_columns, 1) + bias_other[:, units:]
    )
    bin_first_new, bin_second_new, bin_new = adam_update(
        b_in, grad_bin, b_in_first, b_in_second, RATE_BIASES, 0.0
    )
    bout_first_new, bout_second_new, bout_new = adam_update(
        b_out, grad_bout, b_out_first, b_out_second, RATE_OFFSETS, 0.0
    )
    return (
        *backward[-1][:2],
        *updated,
        *w_in_results,
        *w_out_results,
        bin_first_new,
        bin_second_new,
        bin_new,
        bout_first_new,
        bout_second_new,
        bout_new,
    )


def solution(mesh):
    tokens = P(None, BOTH, None, None)
    rows = P(BOTH, None)
    columns = P(None, BOTH)
    first_layer = P(EXPERT, None, TENSOR)
    second_layer = P(EXPERT, TENSOR, None)
    blocks = P(EXPERT, TENSOR, None, None)
    biases = P(EXPERT, TENSOR)
    in_specs = (
        (tokens,) * 4
        + (rows,) * 6
        + (columns,) * 3
        + (first_layer,) * 3
        + (blocks,) * 2
        + (second_layer,) * 3
        + (blocks,) * 2
        + (biases,) * 6
    )
    out_specs = (
        (tokens,) * 2
        + (rows,) * 8
        + (columns,) * 3
        + (first_layer,) * 4
        + (blocks,) * 2
        + (second_layer,) * 4
        + (blocks,) * 2
        + (biases,) * 6
    )
    return jax.shard_map(
        per_device, mesh=mesh, in_specs=in_specs, out_specs=out_specs, check_vma=False
    )
```

```python
from functools import partial

import jax
import jax.numpy as jnp
from jax import lax
from jax.experimental import pallas as pl
from jax.experimental.pallas import tpu as pltpu
from jax.sharding import PartitionSpec as P

D = 768
HEADS = 12
HEAD_DIM = 64
SEQ = 196
TOPK = 2
MB = 2
STEP = 10
BLK = 384


MATMUL_ACCURACY = lax.Precision.HIGHEST
NORM_EPS = 1e-06
BETA_FIRST = 0.5
BETA_SECOND = 0.5
STAT_DECAY = 0.5
ADAM_EPS = 1e-08
DECAY_RATE = 0.1
RATE_DENSE = 0.05
RATE_NORMS = 0.4
RATE_INPUT = 0.04
RATE_OUTPUT = 0.4
RATE_BIASES = 0.05
RATE_OFFSETS = 1.0


def column_sum(left_side, right_side):
    return lax.dot_general(
        left_side, right_side, (((0,), (0,)), ((), ())), preferred_element_type=jnp.float32
    )


def row_product(left_side, right_side):
    return lax.dot_general(
        left_side, right_side, (((1,), (1,)), ((), ())), preferred_element_type=jnp.float32
    )


def moment_step(gradient, first_moment, second_moment):
    first_new = BETA_FIRST * first_moment + (1.0 - BETA_FIRST) * gradient
    second_new = BETA_SECOND * second_moment + (1.0 - BETA_SECOND) * gradient * gradient
    normed_step = (
        first_new
        / (1.0 - BETA_FIRST**STEP)
        / (jnp.sqrt(second_new / (1.0 - BETA_SECOND**STEP)) + ADAM_EPS)
    )
    return (first_new, second_new, normed_step)


def adam_update(weight, gradient, first_moment, second_moment, step_rate, weight_decay):
    first_new, second_new, normed_step = moment_step(gradient, first_moment, second_moment)
    return (first_new, second_new, weight - step_rate * (normed_step + weight_decay * weight))


EXPERT = "expert"
TENSOR = "tensor"
BOTH = (EXPERT, TENSOR)
VMEM_LIMIT = 56 * 2**20
FLOPS_PER_US = 1.1e9
ROW_TILE = 512
SUB = 64


def mm(left, right):
    return jnp.dot(left, right, preferred_element_type=jnp.float32, precision=MATMUL_ACCURACY)


def mt(left, right):
    return lax.dot_general(
        left,
        right,
        (((1,), (1,)), ((), ())),
        preferred_element_type=jnp.float32,
        precision=MATMUL_ACCURACY,
    )


def tm(left, right):
    return lax.dot_general(
        left,
        right,
        (((0,), (0,)), ((), ())),
        preferred_element_type=jnp.float32,
        precision=MATMUL_ACCURACY,
    )


def factor_inverse(mats):
    n=SUB; B=jnp.broadcast_to; w=(8,2*n)
    lane=lax.broadcasted_iota(jnp.int32,w,1); sub=lax.broadcasted_iota(jnp.int32,w,0)
    X=[]
    for m in mats:
        tiles=[]
        for i in range(n//8):
            eye=jnp.where(lane==sub+8*i+n,1.0,0.0)
            tiles.append(jnp.concatenate([m[8*i:8*i+8,:],eye[:,n:]],axis=1))
        X.append(tiles)
    outs=[[] for _ in mats]
    for r in range(n//8):
        for m,tiles in enumerate(X):
            T=tiles[r]
            cols=[[B(tiles[t][:,8*r+k:8*r+k+1],w) for k in range(8)] for t in range(r,n//8)]
            a=[[B(cols[0][j][i:i+1,:],w) for j in range(i+1)] for i in range(8)]
            rows=[B(T[i:i+1,:],w) for i in range(8)]
            inv=[None]*8; l=[[None]*8 for _ in range(8)]
            for k in range(8):
                inv[k]=1.0/a[k][k]
                for i in range(k+1,8): l[i][k]=a[i][k]*inv[k]
                for i in range(k+1,8):
                    for j in range(k+1,i+1):
                        a[i][j]=a[i][j]-l[i][k]*a[j][k]
                for i in range(k+1,8): rows[i]=rows[i]-l[i][k]*rows[k]
            o=jnp.zeros(w,jnp.float32)
            for k in range(8): o=jnp.where(sub==k,rows[k]*lax.rsqrt(a[k][k]),o)
            outs[m].append(o[:,n:])
            if r+1<n//8:
                wv=[rows[k]*inv[k] for k in range(8)]
                for k in range(6,-1,-1):
                    for j in range(k+1,8): wv[k]=wv[k]-l[j][k]*wv[j]
                for t in range(r+1,n//8):
                    c=cols[t-r]
                    acc=c[0]*wv[0]
                    for k in range(1,8): acc=acc+c[k]*wv[k]
                    tiles[t]=tiles[t]-acc
    return [jnp.concatenate(o,axis=0) for o in outs]
def renew_kernel(skipped, *refs):
    refs=refs[skipped:]
    m_ref=refs[-1]
    zs=refs[:-2]
    nb=len(zs)
    qs=[refs[-2].at[0,i] for i in range(nb)]
    n=BLK; kb=n//128; h=SUB
    for b in range(nb):
        z=zs[b][...]
        m_ref[b]=tm(z,z)
    for k in range(kb):
        o=128*k; sl=slice(o,o+128)
        d11=[m_ref[b,o:o+h,o:o+h] for b in range(nb)]
        i1=factor_inverse(d11)
        l21=[mt(m_ref[b,o+h:o+128,o:o+h],i1[b]) for b in range(nb)]
        d22=[m_ref[b,o+h:o+128,o+h:o+128]-mt(l21[b],l21[b]) for b in range(nb)]
        i2=factor_inverse(d22)
        inv=[]
        for b in range(nb):
            low=-mm(mm(i2[b],l21[b]),i1[b])
            inv.append(jnp.concatenate([jnp.concatenate([i1[b],jnp.zeros((h,h),jnp.float32)],1),jnp.concatenate([low,i2[b]],1)],0))
        for b in range(nb):
            q=zs[b][:,sl]
            for j in range(k):
                q=q-mt(qs[b][:,128*j:128*j+128],m_ref[b,sl,128*j:128*j+128])
            qs[b][:,sl]=mt(q,inv[b])
            if k+1<kb:
                p=mt(m_ref[b,o+128:,sl],inv[b])
                m_ref[b,o+128:,sl]=p
                m_ref[b,o+128:,o+128:]=m_ref[b,o+128:,o+128:]-mt(p,p)
def renew(tokens, stretched):
    count=len(stretched)
    return vmem_call(
        partial(renew_kernel, len(tokens)),
        30,
        grid=(1,),
        out_shape=jax.ShapeDtypeStruct((1, count, BLK, BLK), jnp.float32),
        in_specs=[pl.BlockSpec(memory_space=pl.ANY)] * len(tokens)
        + [full_block((BLK, BLK))] * count,
        out_specs=full_block((1, count, BLK, BLK)),
        scratch_shapes=[pltpu.VMEM((count, BLK, BLK), jnp.float32)],
    )(*tokens, *stretched)


def low(values):
    return values.astype(jnp.bfloat16)


def wide(values):
    return values.astype(jnp.float32)


def dot(left, right):
    return jnp.dot(left, right, preferred_element_type=jnp.float32)


def vmem_call(kernel, microseconds, **options):
    cost = pl.CostEstimate(
        flops=int(microseconds * FLOPS_PER_US), bytes_accessed=0, transcendentals=0
    )
    return pl.pallas_call(
        kernel,
        compiler_params=pltpu.CompilerParams(vmem_limit_bytes=VMEM_LIMIT),
        cost_estimate=cost,
        **options,
    )


def full_block(shape):
    return pl.BlockSpec(shape, lambda *_: (0,) * len(shape))


def norm_parts(values):
    centred = values - jnp.mean(values, axis=-1, keepdims=True)
    scale = lax.rsqrt(jnp.mean(centred * centred, axis=-1, keepdims=True) + NORM_EPS)
    return centred * scale, scale


def norm_backward(grads, normed, scale, gain):
    inner = grads * gain
    return scale * (
        inner
        - jnp.mean(inner, axis=-1, keepdims=True)
        - normed * jnp.mean(inner * normed, axis=-1, keepdims=True)
    )


def route_mask(target, slot_total):
    slot_index = lax.broadcasted_iota(jnp.int32, (target.shape[0], slot_total), 1)
    hit = (slot_index == target[:, :1]) | (slot_index == target[:, 1:2])
    return jnp.where(hit, 1.0, 0.0)


def masked_softmax(logits, count):
    lanes = lax.broadcasted_iota(jnp.int32, logits.shape, 1)
    inside = lanes < count
    peak = jnp.max(jnp.where(inside, logits, -jnp.inf), axis=-1, keepdims=True)
    raised = jnp.where(inside, jnp.exp(jnp.where(inside, logits - peak, 0.0)), 0.0)
    return raised / jnp.sum(raised, axis=-1, keepdims=True)


def softmax_rows(scores):
    raised = jnp.exp(scores - jnp.max(scores, axis=-1, keepdims=True))
    return raised / jnp.sum(raised, axis=-1, keepdims=True)


def dispatch_kernel(target_ref, rows_ref, out_ref):
    experts, copies, steps, padded, _ = out_ref.shape
    for step in range(steps):
        routing = low(route_mask(target_ref[step], experts * padded))
        rows = column_sum(routing, rows_ref[step, 0])
        rows = low(rows.reshape(experts, padded, D))
        for copy in range(copies):
            out_ref[:, copy, step] = rows


def attention_kernel(experts, x_ref, target_ref, a_ref, *refs):
    out_refs = refs[:MB]
    qkv_ref, mixed_ref, middle_ref, probs_ref, score_ref, weight_ref = refs[MB:]
    copies, padded = out_refs[0].shape[1:3]
    inputs = wide(x_ref[0, 0])
    extra = a_ref[:, 4 * D :]
    vectors = wide(extra).T
    gains = [vectors[experts + i : experts + i + 1] for i in range(4)]
    normed, _ = norm_parts(inputs)
    normed_low = low(normed * gains[0] + gains[1])
    qkv_ref[0] = low(dot(normed_low, a_ref[:, : 3 * D]))
    lanes = lax.broadcasted_iota(jnp.int32, (SEQ, 2 * HEAD_DIM), 1)
    for head in range(HEADS):
        start = 2 * HEAD_DIM * (head // 2)
        query = qkv_ref[0, :, start : start + 2 * HEAD_DIM]
        keys = qkv_ref[0, :, D + start : D + start + 2 * HEAD_DIM]
        here = (lanes < HEAD_DIM) if head % 2 == 0 else (lanes >= HEAD_DIM)
        score_ref[head] = row_product(jnp.where(here, query, 0), keys) * HEAD_DIM ** (-0.5)
    weight_ref[...] = low(softmax_rows(score_ref[...]))
    for pair in range(HEADS // 2):
        start = 2 * HEAD_DIM * pair
        values = qkv_ref[0, :, 2 * D + start : 2 * D + start + 2 * HEAD_DIM]
        both = [dot(weight_ref[2 * pair + side], values) for side in range(2)]
        mixed_ref[0, :, start : start + 2 * HEAD_DIM] = low(
            jnp.where(lanes < HEAD_DIM, both[0], both[1])
        )
    middle = inputs + dot(mixed_ref[0], a_ref[:, 3 * D : 4 * D])
    middle_ref[0] = middle
    normed, _ = norm_parts(middle)
    moe_low = low(normed * gains[2] + gains[3])
    probs_ref[0] = masked_softmax(dot(moe_low, extra), experts)
    routing = low(route_mask(target_ref[0], experts * padded))
    rows = low(column_sum(routing, moe_low).reshape(experts, padded, D))
    for step, out_ref in enumerate(out_refs):

        @pl.when(pl.program_id(0) == step)
        def _(out_ref=out_ref):
            for copy in range(copies):
                out_ref[:, copy] = rows


def attention_backward_kernel(experts, skipped, *refs):
    refs = refs[skipped:]
    x_ref, up_ref, target_ref, back_ref, qkv_ref, mixed_ref, middle_ref, probs_ref, a_ref = refs[:9]
    score_ref, slope_ref, weight_ref, grad_score_ref = refs[-4:]
    out_ref, grad_ref, normed_ref, joined_ref, branch_ref, moe_ref, logit_ref, vector_ref = refs[
        -12:-4
    ]
    copies, padded = (back_ref.shape[1], back_ref.shape[3])
    slot_total = experts * padded
    extra = a_ref[:, 4 * D :]
    vectors = wide(extra).T
    gains = [vectors[experts + i : experts + i + 1] for i in range(4)]
    inputs = wide(x_ref[0, 0])
    upstream_low = up_ref[0, 0]
    upstream = wide(upstream_low)
    middle = middle_ref[0]
    probs = probs_ref[0]

    def collected(kind):
        total = wide(back_ref[:, 0, kind])
        for copy in range(1, copies):
            total = total + wide(back_ref[:, copy, kind])
        return low(total.reshape(slot_total, D))

    coming = collected(0)
    grad_coming = collected(1)
    routing = route_mask(target_ref[0], slot_total)
    member = jnp.where(
        lax.broadcasted_iota(jnp.int32, (probs.shape[1], slot_total), 1) // padded
        == lax.broadcasted_iota(jnp.int32, (probs.shape[1], slot_total), 0),
        1.0,
        0.0,
    )
    member_low = low(member)
    probs_high = low(probs)
    slot_gate = routing * (dot(probs_high, member_low) + dot(low(probs - wide(probs_high)), member_low))
    gate_high = low(slot_gate)
    final = middle + dot(gate_high, coming) + dot(low(slot_gate - wide(gate_high)), coming)
    out_ref[0, 0] = low(final)
    slot_grads = routing * row_product(upstream_low, coming)
    slot_high = low(slot_grads)
    prob_grads = row_product(slot_high, member_low) + row_product(
        low(slot_grads - wide(slot_high)), member_low
    )
    logit_low = low(
        probs * (prob_grads - jnp.sum(prob_grads * probs, axis=-1, keepdims=True))
    )
    logit_ref[...] = logit_low
    moe_grad = dot(low(routing), grad_coming) + row_product(logit_low, extra)
    normed, scale = norm_parts(middle)
    moe_ref[...] = low(normed * gains[2] + gains[3])
    vector_ref[2:3] = jnp.sum(moe_grad * normed, axis=0, keepdims=True)
    vector_ref[3:4] = jnp.sum(moe_grad, axis=0, keepdims=True)
    grad_middle = upstream + norm_backward(moe_grad, normed, scale, gains[2])
    branch_low = low(grad_middle)
    branch_ref[...] = branch_low
    grad_mixed = low(row_product(branch_low, a_ref[:, 3 * D : 4 * D]))
    lanes = lax.broadcasted_iota(jnp.int32, (SEQ, 2 * HEAD_DIM), 1)
    for head in range(HEADS):
        start = 2 * HEAD_DIM * (head // 2)
        stop = start + 2 * HEAD_DIM
        query = qkv_ref[0, :, start:stop]
        keys = qkv_ref[0, :, D + start : D + stop]
        values = qkv_ref[0, :, 2 * D + start : 2 * D + stop]
        here = (lanes < HEAD_DIM) if head % 2 == 0 else (lanes >= HEAD_DIM)
        score_ref[head] = row_product(jnp.where(here, query, 0), keys) * HEAD_DIM ** (-0.5)
        slope_ref[head] = row_product(jnp.where(here, grad_mixed[:, start:stop], 0), values)
    weights = softmax_rows(score_ref[...])
    weight_ref[...] = low(weights)
    slopes = slope_ref[...]
    grad_score_ref[...] = low(
        weights * (slopes - jnp.sum(slopes * weights, axis=-1, keepdims=True))
    )
    for pair in range(HEADS // 2):
        start = 2 * HEAD_DIM * pair
        stop = start + 2 * HEAD_DIM
        query = qkv_ref[0, :, start:stop]
        keys = qkv_ref[0, :, D + start : D + stop]
        grad_here = grad_mixed[:, start:stop]
        results = []
        for side in range(2):
            grad_scores = grad_score_ref[2 * pair + side]
            results.append(
                (
                    dot(grad_scores, keys) * HEAD_DIM ** (-0.5),
                    column_sum(grad_scores, query) * HEAD_DIM ** (-0.5),
                    column_sum(weight_ref[2 * pair + side], grad_here),
                )
            )
        for part in range(3):
            joined_ref[:, part * D + start : part * D + stop] = low(
                jnp.where(lanes < HEAD_DIM, results[0][part], results[1][part])
            )
    grad_normed = row_product(joined_ref[...], a_ref[:, : 3 * D])
    normed, scale = norm_parts(inputs)
    normed_ref[...] = low(normed * gains[0] + gains[1])
    vector_ref[4:8] = jnp.zeros((4, D), jnp.float32)
    vector_ref[0:1] = jnp.sum(grad_normed * normed, axis=0, keepdims=True)
    vector_ref[1:2] = jnp.sum(grad_normed, axis=0, keepdims=True)
    grad_ref[0, 0] = grad_middle + norm_backward(grad_normed, normed, scale, gains[0])


def weight_sums_kernel(experts, after_ref, core_ref, mixed_ref, *refs):
    own_ref, other_ref, token_ref = refs[-3:]
    token_ref[...] = jnp.zeros_like(token_ref)
    steps = [refs[6 * i : 6 * i + 6] for i in range(MB)]
    held, block, _ = own_ref.shape
    first_core = core_ref[0] == 0

    def write(total, start):
        stop = start + total.shape[1]
        pairs = total.reshape(held, 2, block, total.shape[1])
        even, odd = (pairs[:, 0], pairs[:, 1])
        own_ref[:, :, start:stop] = jnp.where(first_core, even, odd)
        other_ref[:, :, start:stop] = low(jnp.where(first_core, odd, even))

    for part in range(3):
        total = sum(column_sum(s[0][...], s[1][:, part * D : part * D + D]) for s in steps)
        write(total, part * D)
    write(sum(column_sum(mixed_ref[i], s[2][...]) for i, s in enumerate(steps)), 3 * D)
    vectors = sum(s[5][...] for s in steps)
    vectors = jnp.concatenate(
        [
            jnp.zeros((experts, D), jnp.float32),
            vectors,
            jnp.zeros((128 - experts - vectors.shape[0], D), jnp.float32),
        ],
        axis=0,
    )
    write(sum(column_sum(s[3][...], s[4][...]) for s in steps) + vectors.T, 4 * D)


def gelu_parts(values):
    raised = jnp.exp(-0.5 * values * values)
    root = 1.0 / (1.0 + (0.3275911 * 0.5**0.5) * jnp.abs(values))
    tail = 1.061405429 * root - 1.453152027
    tail = tail * root + 1.421413741
    tail = tail * root - 0.284496736
    tail = tail * root + 0.254829592
    tail = 0.5 * tail * root * raised
    return jnp.where(values >= 0.0, 1.0 - tail, tail), raised * 0.3989422804014327


def hidden_kernel(
    experts,
    expert_ref,
    rows_ref,
    up_ref,
    router_ref,
    weight_ref,
    bias_ref,
    hidden_ref,
    slope_ref,
    grad_ref,
    sum_ref,
):
    count, padded = rows_ref.shape[:2]
    units = weight_ref.shape[2]
    rows = low(wide(rows_ref[...]).reshape(count * padded, D))
    probs = masked_softmax(dot(rows, router_ref[...]), experts)
    lanes = lax.broadcasted_iota(jnp.int32, probs.shape, 1)
    gate = jnp.sum(jnp.where(lanes == expert_ref[0], probs, 0.0), axis=-1, keepdims=True)
    grad = low(gate * wide(up_ref[...]).reshape(count * padded, D))
    grad_ref[...] = grad

    @pl.when(pl.program_id(0) == 0)
    def _():
        sum_ref[...] = jnp.zeros_like(sum_ref)

    sum_ref[0:1] += jnp.sum(wide(grad), axis=0, keepdims=True)
    for side in range(2):
        values = dot(rows, weight_ref[side]) + bias_ref[:, side * units : (side + 1) * units]
        area, density = gelu_parts(values)
        hidden_ref[side] = low(values * area)
        slope_ref[side] = low(area + values * density)


def result_kernel(skipped, *refs):
    (
        hidden_ref,
        slope_ref,
        grad_ref,
        out_ref,
        in_ref,
        bias_ref,
        back_ref,
        pre_ref,
        sum_ref,
    ) = refs[skipped:]
    count, _, padded, _ = back_ref.shape
    units = in_ref.shape[2]

    @pl.when(pl.program_id(0) == 0)
    def _():
        sum_ref[...] = jnp.zeros_like(sum_ref)

    out_term = dot(hidden_ref[0], out_ref[0]) + dot(hidden_ref[1], out_ref[1]) + bias_ref[...]
    back_ref[:, 0] = low(out_term.reshape(count, padded, D))
    grad_term = None
    for side in range(2):
        pre = low(row_product(grad_ref[...], out_ref[side]) * wide(slope_ref[side]))
        pre_ref[side] = pre
        sum_ref[0:1, side * units : (side + 1) * units] += jnp.sum(
            wide(pre), axis=0, keepdims=True
        )
        term = row_product(pre, in_ref[side])
        grad_term = term if grad_term is None else grad_term + term
    back_ref[:, 1] = low(grad_term.reshape(count, padded, D))


def split(values):
    high = low(values)
    return high, low(values - wide(high))


def split_dot(left, right, dims):
    def one(a, b):
        return lax.dot_general(a, b, (dims, ((), ())), preferred_element_type=jnp.float32)

    return one(left[0], right[0]) + (one(left[0], right[1]) + one(left[1], right[0]))


def turn_kernel(along_rows, rate, skipped, *refs):
    refs = refs[skipped:]
    gradient_ref, weight_ref, first_ref, second_ref, stat_ref, basis_ref = refs[:6]
    first_out, second_out, weight_out, copy_out, stat_out, stretched_out = refs[-6:]
    gradient = gradient_ref[...]
    basis = basis_ref[0, 0]
    basis_parts = split(basis)
    if along_rows:
        turned = column_sum(basis_parts[0], gradient) + column_sum(basis_parts[1], gradient)
        outer = row_product(gradient, gradient)
    else:
        turned = dot(gradient, basis_parts[0]) + dot(gradient, basis_parts[1])
        outer = column_sum(gradient, gradient)
    first_new, second_new, step = moment_step(turned, first_ref[0], second_ref[0])
    first_out[0] = first_new
    second_out[0] = second_new
    step_parts = split(step)
    if along_rows:
        returned = split_dot(basis_parts, step_parts, ((1,), (0,)))
    else:
        returned = split_dot(step_parts, basis_parts, ((1,), (1,)))
    weight = weight_ref[0]
    weight_new = weight - rate * (returned + DECAY_RATE * weight)
    weight_out[0] = weight_new
    copy_out[0] = low(weight_new)
    stat_new = STAT_DECAY * stat_ref[0, 0] + (1.0 - STAT_DECAY) * outer
    stat_out[0, 0] = stat_new
    stretched_out[...] = mm(stat_new, basis)


def dense_update_kernel(kept_ref, received_ref, *refs):
    inputs, outputs = (refs[:9], refs[9:])
    gradient = kept_ref[...] + wide(received_ref[...])
    extra = gradient[:, 4 * D :].T
    experts = inputs[3].shape[0]
    gradients = (gradient[:, : 4 * D], extra[:experts], extra[experts : experts + 4])
    rates = ((RATE_DENSE, DECAY_RATE), (RATE_DENSE, DECAY_RATE), (RATE_NORMS, 0.0))
    place = 0
    for kind in range(3):
        weight, first, second = (r[...] for r in inputs[3 * kind : 3 * kind + 3])
        first_new, second_new, weight_new = adam_update(
            weight, gradients[kind], first, second, *rates[kind]
        )
        outputs[place][...] = first_new
        outputs[place + 1][...] = second_new
        outputs[place + 2][...] = weight_new
        place += 3
        if kind < 2:
            outputs[place][...] = low(weight_new)
            place += 1


def row_sums_kernel(*refs):
    total = sum(column_sum(refs[i][...], refs[MB + i][...]) for i in range(MB))
    refs[-1][...] = low(total)


def swap(values, axis, distance):
    size = lax.axis_size(axis)
    return lax.ppermute(values, axis, [(i, i ^ distance) for i in range(size)])


def across(values):
    size = lax.axis_size(TENSOR)
    return lax.ppermute(values, TENSOR, [(i, (i + size // 2) % size) for i in range(size)])


def ordered(bit, mine, other):
    return jnp.where(bit == 0, jnp.stack([mine, other]), jnp.stack([other, mine]))


def gather_tensor(shard):
    tensors, tensor = (lax.axis_size(TENSOR), lax.axis_index(TENSOR))
    block = shard[None]
    distance = 1
    while distance < tensors:
        other = swap(block, TENSOR, distance)
        block = ordered((tensor // distance) % 2, block, other).reshape(-1, *shard.shape)
        distance *= 2
    return block


def gather_experts(block, beside, released):
    experts, tensors = (lax.axis_size(EXPERT), lax.axis_size(TENSOR))
    expert = lax.axis_index(EXPERT)
    columns = block.shape[-1]
    block = block[None]
    distance = 2
    while distance < experts // 4:
        other = swap(block, EXPERT, distance)
        block = ordered((expert // distance) % 2, block, other).reshape(-1, *block.shape[1:])
        distance *= 2
    near, far = (distance, 2 * distance)
    middle = tensors // 2
    from_near, from_far = (swap(block, EXPERT, near), swap(block, EXPERT, far))
    corner = jnp.concatenate(
        [swap(from_far[:, :middle], EXPERT, near), swap(from_near[:, middle:], EXPERT, far)],
        axis=1,
    )
    corner, beside, released = lax.optimization_barrier((corner, beside, released))
    pieces = (block, from_near, from_far, corner)
    crossed = [swap(piece, EXPERT, 1) for piece in pieces]
    near_bit, far_bit = ((expert // near) % 2, (expert // far) % 2)

    def arranged(four):
        return ordered(
            far_bit,
            ordered(near_bit, four[0], four[1]),
            ordered(near_bit, four[2], four[3]),
        ).reshape(-1, *block.shape[1:])

    whole = ordered(expert % 2, arranged(pieces), arranged(crossed))
    whole = jnp.moveaxis(whole, 0, 1)
    return whole.reshape(-1, columns), beside, across(released)


def scatter_sums(held, sending):
    experts, tensors = (lax.axis_size(EXPERT), lax.axis_size(TENSOR))
    expert, tensor = (lax.axis_index(EXPERT), lax.axis_index(TENSOR))
    columns = held.shape[2]

    def pick(values, index, axis=0):
        return lax.dynamic_index_in_dim(values, index, axis, False)

    held = held + wide(swap(sending, EXPERT, 1))
    stages = [held]
    near, far = (experts // 4, experts // 2)
    near_bit, far_bit = ((expert // near) % 2, (expert // far) % 2)
    held = held.reshape(4, experts // 8, tensors, -1, columns)
    place = 2 * far_bit + near_bit
    own, to_near, to_far, to_corner = (
        pick(held, place),
        pick(held, place ^ 1),
        pick(held, place ^ 2),
        pick(held, place ^ 3),
    )
    middle = tensors // 2
    passed_near = swap(low(to_corner[:, :middle]), EXPERT, near)
    passed_far = swap(low(to_corner[:, middle:]), EXPERT, far)
    to_far = jnp.concatenate([to_far[:, :middle] + wide(passed_near), to_far[:, middle:]], axis=1)
    to_near = jnp.concatenate([to_near[:, :middle], to_near[:, middle:] + wide(passed_far)], axis=1)
    stages.append(to_near)
    held = (
        own
        + wide(swap(low(to_near), EXPERT, near))
        + wide(swap(low(to_far), EXPERT, far))
    )
    distance = experts // 8
    while distance >= 2:
        bit = (expert // distance) % 2
        halves = held.reshape(2, -1, *held.shape[1:])
        held = pick(halves, bit) + wide(swap(low(pick(halves, 1 - bit)), EXPERT, distance))
        distance //= 2
    stages.append(held)
    held = held.reshape(tensors, -1, columns)
    distance = tensors // 2
    while distance >= 1:
        bit = (tensor // distance) % 2
        halves = held.reshape(2, -1, *held.shape[1:])
        kept = pick(halves, bit)
        received = swap(low(pick(halves, 1 - bit)), TENSOR, distance)
        if distance > 1:
            held = kept + wide(received)
        distance //= 2
    stages.append(kept)
    return kept.reshape(-1, columns), received.reshape(-1, columns), stages


def soap_turn(along_rows, rate, at, token, gradient, state, statistics, earlier):
    weight, first, second = state
    statistic = statistics[0]
    f32 = jnp.float32
    if along_rows:
        deep = pl.BlockSpec((1, BLK, D), lambda i: (0, at, 0))
    else:
        deep = pl.BlockSpec((1, D, BLK), lambda i: (0, 0, at))
    square = pl.BlockSpec((1, 1, BLK, BLK), lambda i: (0, at, 0, 0))
    anywhere = pl.BlockSpec(memory_space=pl.ANY)
    return vmem_call(
        partial(turn_kernel, along_rows, rate, len(token)),
        8,
        grid=(1,),
        in_specs=[anywhere] * len(token)
        + [full_block(gradient.shape)]
        + [deep] * 3
        + [square] * 2
        + [anywhere] * len(earlier),
        out_specs=[deep] * 4 + [square, full_block((BLK, BLK))],
        out_shape=[jax.ShapeDtypeStruct(weight.shape, f32)] * 3
        + [
            jax.ShapeDtypeStruct(weight.shape, jnp.bfloat16),
            jax.ShapeDtypeStruct(statistic.shape, f32),
            jax.ShapeDtypeStruct((BLK, BLK), f32),
        ],
        input_output_aliases={6 + len(token) + i: i for i in range(len(earlier))},
    )(*token, gradient, *state, *statistics, *earlier)


def row_sums(left, right, at, left_paired):
    rows, width = left[0].shape[-2:]
    height, columns = (BLK, right[0].shape[-1]) if left_paired else (width, BLK)
    paired = pl.BlockSpec((None, rows, BLK), lambda i: (i, 0, at))
    plain = full_block((rows, columns if left_paired else width))
    return vmem_call(
        row_sums_kernel,
        5,
        grid=(2,),
        in_specs=[paired if left_paired else plain] * MB
        + [plain if left_paired else paired] * MB,
        out_specs=pl.BlockSpec((None, height, columns), lambda i: (i, 0, 0)),
        out_shape=jax.ShapeDtypeStruct((2, height, columns), jnp.bfloat16),
    )(*left, *right)


def per_device(
    patches,
    cotangent,
    expert_ids,
    slots,
    attn_weights,
    attn_first,
    attn_second,
    router_weights,
    router_first,
    router_second,
    norm_params,
    norm_first,
    norm_second,
    w_in,
    w_in_first,
    w_in_second,
    w_in_stat,
    w_in_basis,
    w_out,
    w_out_first,
    w_out_second,
    w_out_stat,
    w_out_basis,
    b_in,
    b_in_first,
    b_in_second,
    b_out,
    b_out_first,
    b_out_second,
):
    tokens_here = SEQ
    expert_total = router_weights.shape[1]
    capacity = (105 * TOPK * tokens_here + 100 * expert_total - 1) // (100 * expert_total)
    padded = 8 * ((capacity + 7) // 8)
    experts, tensors = (lax.axis_size(EXPERT), lax.axis_size(TENSOR))
    expert, tensor = (lax.axis_index(EXPERT), lax.axis_index(TENSOR))
    half = tensors // 2
    members = expert_total * half
    units = w_in.shape[2]
    shard_columns = b_out.shape[1]
    columns = 4 * D + 128
    bf16, f32 = (jnp.bfloat16, jnp.float32)
    shape = jax.ShapeDtypeStruct
    pairs = [[i, i + half] for i in range(half)]
    groups = [
        [e * tensors + z for e in range(experts) for z in range(h * half, (h + 1) * half)]
        for h in range(2)
    ]

    def exchange(values):
        return lax.all_to_all(values, BOTH, 0, 0, axis_index_groups=groups, tiled=True)

    packed = jnp.concatenate(
        [
            low(attn_weights),
            low(router_weights),
            low(norm_params).T,
            jnp.zeros((attn_weights.shape[0], 128 - expert_total - 4), bf16),
        ],
        axis=1,
    )
    in_own, out_own = (low(w_in[0]), low(w_out[0]))
    b_in_low, b_out_low = (low(b_in), low(b_out))
    peer_bias = across(jnp.concatenate([b_in_low, b_out_low], axis=1))
    chosen = expert_ids.reshape(MB, tokens_here, TOPK)
    placed = slots.reshape(MB, tokens_here, TOPK)
    target = jnp.where(placed < capacity, chosen * padded + placed, -1)
    up_sent = vmem_call(
        dispatch_kernel,
        4,
        grid=(1,),
        in_specs=[full_block(target.shape), full_block(cotangent.shape)],
        out_specs=full_block((expert_total, half, MB, padded, D)),
        out_shape=shape((expert_total, half, MB, padded, D), bf16),
    )(target, cotangent)
    first_stage, peer_bias, sent_first = lax.optimization_barrier(
        (gather_tensor(packed), peer_bias, in_own[: D // 2])
    )
    out_first = lax.all_gather(out_own[: units // 2], TENSOR, axis_index_groups=pairs)
    up_all = exchange(up_sent.reshape(members, MB, padded, D))
    gathered, in_first, in_second = gather_experts(
        first_stage, across(sent_first), in_own[D // 2 :]
    )
    upper = tensor >= half
    peer_in = peer_bias[:, :units]
    bias_in = wide(
        jnp.where(
            upper,
            jnp.concatenate([peer_in, b_in_low], axis=1),
            jnp.concatenate([b_in_low, peer_in], axis=1),
        )
    )
    bias_out = jnp.zeros((1, D), f32)
    own_place = tensor * shard_columns
    peer_place = ((tensor + half) % tensors) * shard_columns
    bias_out = lax.dynamic_update_slice(bias_out, wide(b_out_low), (0, own_place))
    bias_out = lax.dynamic_update_slice(bias_out, wide(peer_bias[:, units:]), (0, peer_place))
    image = pl.BlockSpec((1, 1, SEQ, D), lambda i: (i, 0, 0, 0))

    def per_step(*tail):
        return pl.BlockSpec((1, *tail), lambda i: (i,) + (0,) * len(tail))

    *sent, qkv, mixed, middle, probs = vmem_call(
        partial(attention_kernel, expert_total),
        11,
        grid=(MB,),
        in_specs=[image, per_step(SEQ, TOPK), full_block((D, columns))],
        out_specs=[
            *[full_block((expert_total, half, padded, D))] * MB,
            per_step(SEQ, 3 * D),
            per_step(SEQ, D),
            per_step(SEQ, D),
            per_step(SEQ, 128),
        ],
        out_shape=[
            *[shape((expert_total, half, padded, D), bf16)] * MB,
            shape((MB, SEQ, 3 * D), bf16),
            shape((MB, SEQ, D), bf16),
            shape((MB, SEQ, D), f32),
            shape((MB, SEQ, 128), f32),
        ],
        scratch_shapes=[pltpu.VMEM((HEADS, SEQ, SEQ), f32), pltpu.VMEM((HEADS, SEQ, SEQ), bf16)],
    )(patches, target, gathered)
    earlier, up_all, in_second = lax.optimization_barrier((sent[0], up_all, in_second))
    in_peer = jnp.concatenate([in_first, in_second], axis=0)
    in_pair = jnp.where(upper, jnp.stack([in_peer, in_own]), jnp.stack([in_own, in_peer]))
    arrived = [exchange(earlier.reshape(members, padded, D))]
    later, arrived[0], out_first = lax.optimization_barrier((sent[1], arrived[0], out_first))
    arrived.append(exchange(later.reshape(members, padded, D)))
    count = max(
        n
        for n in range(1, members + 1)
        if members % n == 0 and n * padded <= ROW_TILE and (n * padded) % 16 == 0
    )
    tile = count * padded
    total_rows = members * padded
    tiles = members // count

    def rows_of(width):
        return pl.BlockSpec((tile, width), lambda i: (i, 0))

    expert_scalar = jnp.reshape(expert, (1,)).astype(jnp.int32)
    in_smem = pl.BlockSpec(memory_space=pltpu.SMEM)
    anywhere = pl.BlockSpec(memory_space=pl.ANY)
    both_rows = pl.BlockSpec((2, tile, units), lambda i: (0, i, 0))
    both_shape = shape((2, total_rows, units), bf16)
    hidden = []
    for step in range(MB):
        hidden.append(
            vmem_call(
                partial(hidden_kernel, expert_total),
                12,
                grid=(tiles,),
                in_specs=[
                    in_smem,
                    pl.BlockSpec((count, padded, D), lambda i: (i, 0, 0)),
                    pl.BlockSpec((count, None, padded, D), lambda i, step=step: (i, step, 0, 0)),
                    pl.BlockSpec((D, 128), lambda i: (0, 4 * D // 128)),
                    full_block((2, D, units)),
                    full_block((1, 2 * units)),
                ],
                out_specs=[both_rows] * 2 + [rows_of(D), full_block((8, D))],
                out_shape=[both_shape] * 2
                + [shape((total_rows, D), bf16), shape((8, D), f32)],
            )(expert_scalar, arrived[step], up_all, gathered, in_pair, bias_in)
        )
    sent_second, hidden_last = lax.optimization_barrier((out_own[units // 2 :], hidden[-1][2]))
    hidden[-1] = (*hidden[-1][:2], hidden_last, *hidden[-1][3:])
    out_second = lax.all_gather(sent_second, TENSOR, axis_index_groups=pairs)
    out_pair = jnp.concatenate([out_first, out_second], axis=1)
    blocks = units // BLK
    row_grads = [h[2] for h in hidden]
    sum_out = [row_sums([h[0] for h in hidden], row_grads, at, True) for at in range(blocks)]
    results = []
    for step in range(MB):
        before = sum_out if step == 0 else []
        results.append(
            vmem_call(
                partial(result_kernel, len(before)),
                12,
                grid=(tiles,),
                in_specs=[anywhere] * len(before)
                + [both_rows] * 2
                + [
                    rows_of(D),
                    full_block((2, units, D)),
                    full_block((2, D, units)),
                    full_block((1, D)),
                ],
                out_specs=[
                    pl.BlockSpec((count, 2, padded, D), lambda i: (i, 0, 0, 0)),
                    both_rows,
                    full_block((8, 2 * units)),
                ],
                out_shape=[
                    shape((members, 2, padded, D), bf16),
                    both_shape,
                    shape((8, 2 * units), f32),
                ],
            )(*before, *hidden[step][:3], out_pair, in_pair, bias_out)
        )
    flat_rows = [rows.reshape(total_rows, D) for rows in arrived]
    sum_in = [row_sums(flat_rows, [r[1] for r in results], at, False) for at in range(blocks)]

    def shared(sums):
        return lax.psum_scatter(sums, TENSOR, axis_index_groups=pairs)

    grads_out = [shared(sums) for sums in sum_out]
    grads_in = [shared(sums) for sums in sum_in]
    returned = [exchange(r[0]) for r in results]
    sum_bin = sum(r[2][:1] for r in results)
    sum_bout = sum(h[3][:1] for h in hidden)
    bias_sums = jnp.concatenate(
        [
            jnp.where(upper, sum_bin[:, :units], sum_bin[:, units:]),
            lax.dynamic_slice_in_dim(sum_bout, peer_place, shard_columns, 1),
        ],
        axis=1,
    )
    bias_other = across(bias_sums)
    backward = []
    tokens = [sum_in]
    for step in range(MB):
        first = step == 0
        here = pl.BlockSpec((1, 1, SEQ, D), lambda i, step=step: (step, 0, 0, 0))

        def of_step(*tail, step=step):
            return pl.BlockSpec((1, *tail), lambda i: (step,) + (0,) * len(tail))

        back = returned[step].reshape(expert_total, half, 2, padded, D)
        outs = [
            (shape(patches.shape, bf16), here),
            (shape(patches.shape, f32), here),
            (shape((SEQ, D), bf16), full_block((SEQ, D))),
            (shape((SEQ, 3 * D), bf16), full_block((SEQ, 3 * D))),
            (shape((SEQ, D), bf16), full_block((SEQ, D))),
            (shape((SEQ, D), bf16), full_block((SEQ, D))),
            (shape((SEQ, 128), bf16), full_block((SEQ, 128))),
            (shape((8, D), f32), full_block((8, D))),
        ]
        earlier = [] if first else list(backward[-1][:2])
        backward.append(
            vmem_call(
                partial(attention_backward_kernel, expert_total, len(tokens[step])),
        15,
                grid=(1,),
                in_specs=[anywhere] * len(tokens[step])
                + [
                    here,
                    here,
                    of_step(SEQ, TOPK),
                    full_block(back.shape),
                    of_step(SEQ, 3 * D),
                    of_step(SEQ, D),
                    of_step(SEQ, D),
                    of_step(SEQ, 128),
                    full_block((D, columns)),
                ]
                + [pl.BlockSpec(memory_space=pl.ANY)] * len(earlier),
                out_specs=[o[1] for o in outs],
                out_shape=[o[0] for o in outs],
                scratch_shapes=[pltpu.VMEM((HEADS, SEQ, SEQ), f32)] * 2
                + [pltpu.VMEM((HEADS, SEQ, SEQ), bf16)] * 2,
                input_output_aliases={}
                if first
                else {9 + len(tokens[step]): 0, 10 + len(tokens[step]): 1},
            )(
                *tokens[step],
                patches,
                cotangent,
                target,
                back,
                qkv,
                mixed,
                middle,
                probs,
                gathered,
                *earlier,
            )
        )
        if first:
            out_turned = [
                soap_turn(
                    True,
                    RATE_OUTPUT,
                    0,
                    [backward[0][6]],
                    grads_out[0],
                    (w_out, w_out_first, w_out_second),
                    (w_out_stat, w_out_basis),
                    [],
                )
            ]
            tokens.append([out_turned[0][5]])
    core_scalar = jnp.reshape(expert % 2, (1,)).astype(jnp.int32)
    block_rows = tensors * attn_weights.shape[0]
    flat_steps = [value for b in backward for value in b[2:]]
    core_shape = (experts // 2, block_rows, columns)
    held, sending, token = vmem_call(
        partial(weight_sums_kernel, expert_total),
        8,
        grid=(1,),
        in_specs=[anywhere, in_smem] + [full_block(v.shape) for v in (mixed, *flat_steps)],
        out_specs=[full_block(core_shape)] * 2 + [full_block((8, 128))],
        out_shape=[shape(core_shape, f32), shape(core_shape, bf16), shape((8, 128), f32)],
    )(b_in_low, core_scalar, mixed, *flat_steps)
    kept, received, stages = scatter_sums(held, sending)
    dense = [shape(attn_weights.shape, f32)] * 3 + [shape(attn_weights.shape, bf16)]
    turned_shape = router_weights.shape[::-1]
    routers = [shape(turned_shape, f32)] * 3 + [shape(turned_shape, bf16)]
    norms = [shape(norm_params.shape, f32)] * 3
    states = (
        kept,
        received,
        attn_weights,
        attn_first,
        attn_second,
        router_weights.T,
        router_first.T,
        router_second.T,
        norm_params,
        norm_first,
        norm_second,
    )
    updated_shapes = dense + routers + norms
    updated = vmem_call(
        dense_update_kernel,
        3,
        grid=(1,),
        in_specs=[full_block(v.shape) for v in states],
        out_specs=[full_block(v.shape) for v in updated_shapes],
        out_shape=updated_shapes,
    )(*states)
    for at in range(1, blocks):
        out_turned.append(
            soap_turn(
                True,
                RATE_OUTPUT,
                at,
                [token],
                grads_out[at],
                (w_out, w_out_first, w_out_second),
                (w_out_stat, w_out_basis),
                out_turned[-1][:5],
            )
        )
    w_out_basis_new = renew(stages[:1], [turned[5] for turned in out_turned])
    in_turned = []
    for at in range(blocks):
        in_turned.append(
            soap_turn(
                False,
                RATE_INPUT,
                at,
                [w_out_basis_new, stages[1]] if at == 0 else [in_turned[-1][5], stages[2]],
                grads_in[at],
                (w_in, w_in_first, w_in_second),
                (w_in_stat, w_in_basis),
                in_turned[-1][:5] if at > 0 else [],
            )
        )
    w_in_basis_new = renew(stages[3:], [turned[5] for turned in in_turned])
    bias_other, w_in_basis_new = lax.optimization_barrier((bias_other, w_in_basis_new))
    w_in_results = (*in_turned[-1][:5], w_in_basis_new)
    w_out_results = (*out_turned[-1][:5], w_out_basis_new)
    own_bin = jnp.where(upper, sum_bin[:, units:], sum_bin[:, :units])
    grad_bin = own_bin + bias_other[:, :units]
    grad_bout = (
        lax.dynamic_slice_in_dim(sum_bout, own_place, shard_columns, 1) + bias_other[:, units:]
    )
    bin_first_new, bin_second_new, bin_new = adam_update(
        b_in, grad_bin, b_in_first, b_in_second, RATE_BIASES, 0.0
    )
    bout_first_new, bout_second_new, bout_new = adam_update(
        b_out, grad_bout, b_out_first, b_out_second, RATE_OFFSETS, 0.0
    )
    return (
        *backward[-1][:2],
        *updated[:4],
        *(value.T for value in updated[4:8]),
        *updated[8:],
        *w_in_results,
        *w_out_results,
        bin_first_new,
        bin_second_new,
        bin_new,
        bout_first_new,
        bout_second_new,
        bout_new,
    )


def solution(mesh):
    tokens = P(None, BOTH, None, None)
    rows = P(BOTH, None)
    columns = P(None, BOTH)
    first_layer = P(EXPERT, None, TENSOR)
    second_layer = P(EXPERT, TENSOR, None)
    blocks = P(EXPERT, TENSOR, None, None)
    biases = P(EXPERT, TENSOR)
    in_specs = (
        (tokens,) * 4
        + (rows,) * 6
        + (columns,) * 3
        + (first_layer,) * 3
        + (blocks,) * 2
        + (second_layer,) * 3
        + (blocks,) * 2
        + (biases,) * 6
    )
    out_specs = (
        (tokens,) * 2
        + (rows,) * 8
        + (columns,) * 3
        + (first_layer,) * 4
        + (blocks,) * 2
        + (second_layer,) * 4
        + (blocks,) * 2
        + (biases,) * 6
    )
    return jax.shard_map(
        per_device, mesh=mesh, in_specs=in_specs, out_specs=out_specs, check_vma=False
    )
```

```python
from functools import partial

import jax
import jax.numpy as jnp
from jax import lax
from jax.experimental import pallas as pl
from jax.experimental.pallas import tpu as pltpu
from jax.sharding import PartitionSpec as P

D = 768
HEADS = 12
HEAD_DIM = 64
SEQ = 196
TOPK = 2
MB = 2
STEP = 10
BLK = 384


MATMUL_ACCURACY = lax.Precision.HIGHEST
NORM_EPS = 1e-06
BETA_FIRST = 0.5
BETA_SECOND = 0.5
STAT_DECAY = 0.5
ADAM_EPS = 1e-08
DECAY_RATE = 0.1
RATE_DENSE = 0.05
RATE_NORMS = 0.4
RATE_INPUT = 0.04
RATE_OUTPUT = 0.4
RATE_BIASES = 0.05
RATE_OFFSETS = 1.0


def column_sum(left_side, right_side):
    return lax.dot_general(
        left_side, right_side, (((0,), (0,)), ((), ())), preferred_element_type=jnp.float32
    )


def row_product(left_side, right_side):
    return lax.dot_general(
        left_side, right_side, (((1,), (1,)), ((), ())), preferred_element_type=jnp.float32
    )


def moment_step(gradient, first_moment, second_moment):
    first_new = BETA_FIRST * first_moment + (1.0 - BETA_FIRST) * gradient
    second_new = BETA_SECOND * second_moment + (1.0 - BETA_SECOND) * gradient * gradient
    normed_step = (
        first_new
        / (1.0 - BETA_FIRST**STEP)
        / (jnp.sqrt(second_new / (1.0 - BETA_SECOND**STEP)) + ADAM_EPS)
    )
    return (first_new, second_new, normed_step)


def adam_update(weight, gradient, first_moment, second_moment, step_rate, weight_decay):
    first_new, second_new, normed_step = moment_step(gradient, first_moment, second_moment)
    return (first_new, second_new, weight - step_rate * (normed_step + weight_decay * weight))


EXPERT = "expert"
TENSOR = "tensor"
BOTH = (EXPERT, TENSOR)
VMEM_LIMIT = 56 * 2**20
FLOPS_PER_US = 1.1e9
ROW_TILE = 512
SUB = 64


def mm(left, right):
    return jnp.dot(left, right, preferred_element_type=jnp.float32, precision=MATMUL_ACCURACY)


def mt(left, right):
    return lax.dot_general(
        left,
        right,
        (((1,), (1,)), ((), ())),
        preferred_element_type=jnp.float32,
        precision=MATMUL_ACCURACY,
    )


def tm(left, right):
    return lax.dot_general(
        left,
        right,
        (((0,), (0,)), ((), ())),
        preferred_element_type=jnp.float32,
        precision=MATMUL_ACCURACY,
    )


def factor_inverse(mats):
    n=SUB; B=jnp.broadcast_to; w=(8,2*n)
    lane=lax.broadcasted_iota(jnp.int32,w,1); sub=lax.broadcasted_iota(jnp.int32,w,0)
    X=[]
    for m in mats:
        tiles=[]
        for i in range(n//8):
            eye=jnp.where(lane==sub+8*i+n,1.0,0.0)
            tiles.append(jnp.concatenate([m[8*i:8*i+8,:],eye[:,n:]],axis=1))
        X.append(tiles)
    outs=[[] for _ in mats]
    for r in range(n//8):
        for m,tiles in enumerate(X):
            T=tiles[r]
            cols=[[B(tiles[t][:,8*r+k:8*r+k+1],w) for k in range(8)] for t in range(r,n//8)]
            a=[[B(cols[0][j][i:i+1,:],w) for j in range(i+1)] for i in range(8)]
            rows=[B(T[i:i+1,:],w) for i in range(8)]
            inv=[None]*8; l=[[None]*8 for _ in range(8)]
            for k in range(8):
                inv[k]=1.0/a[k][k]
                for i in range(k+1,8): l[i][k]=a[i][k]*inv[k]
                for i in range(k+1,8):
                    for j in range(k+1,i+1):
                        a[i][j]=a[i][j]-l[i][k]*a[j][k]
                for i in range(k+1,8): rows[i]=rows[i]-l[i][k]*rows[k]
            o=jnp.zeros(w,jnp.float32)
            for k in range(8): o=jnp.where(sub==k,rows[k]*lax.rsqrt(a[k][k]),o)
            outs[m].append(o[:,n:])
            if r+1<n//8:
                wv=[rows[k]*inv[k] for k in range(8)]
                for k in range(6,-1,-1):
                    for j in range(k+1,8): wv[k]=wv[k]-l[j][k]*wv[j]
                for t in range(r+1,n//8):
                    c=cols[t-r]
                    acc=c[0]*wv[0]
                    for k in range(1,8): acc=acc+c[k]*wv[k]
                    tiles[t]=tiles[t]-acc
    return [jnp.concatenate(o,axis=0) for o in outs]
def renew_kernel(skipped, *refs):
    refs=refs[skipped:]
    m_ref=refs[-1]
    zs=refs[:-3]
    nb=len(zs)
    qs=[r.at[0,i] for r in refs[-3:-1] for i in range(r.shape[1])]
    n=BLK; kb=n//128; h=SUB
    for b in range(nb):
        z=zs[b][...]
        m_ref[b]=tm(z,z)
    for k in range(kb):
        o=128*k; sl=slice(o,o+128)
        d11=[m_ref[b,o:o+h,o:o+h] for b in range(nb)]
        i1=factor_inverse(d11)
        l21=[mt(m_ref[b,o+h:o+128,o:o+h],i1[b]) for b in range(nb)]
        d22=[m_ref[b,o+h:o+128,o+h:o+128]-mt(l21[b],l21[b]) for b in range(nb)]
        i2=factor_inverse(d22)
        inv=[]
        for b in range(nb):
            low=-mm(mm(i2[b],l21[b]),i1[b])
            inv.append(jnp.concatenate([jnp.concatenate([i1[b],jnp.zeros((h,h),jnp.float32)],1),jnp.concatenate([low,i2[b]],1)],0))
        for b in range(nb):
            q=zs[b][:,sl]
            for j in range(k):
                q=q-mt(qs[b][:,128*j:128*j+128],m_ref[b,sl,128*j:128*j+128])
            qs[b][:,sl]=mt(q,inv[b])
            if k+1<kb:
                p=mt(m_ref[b,o+128:,sl],inv[b])
                m_ref[b,o+128:,sl]=p
                m_ref[b,o+128:,o+128:]=m_ref[b,o+128:,o+128:]-mt(p,p)
def renew(tokens, first, second):
    shapes=[(1, len(group), BLK, BLK) for group in (first, second)]
    count=len(first)+len(second)
    return vmem_call(
        partial(renew_kernel, len(tokens)),
        40,
        grid=(1,),
        out_shape=[jax.ShapeDtypeStruct(s, jnp.float32) for s in shapes],
        in_specs=[pl.BlockSpec(memory_space=pl.ANY)] * len(tokens)
        + [full_block((BLK, BLK))] * count,
        out_specs=[full_block(s) for s in shapes],
        scratch_shapes=[pltpu.VMEM((count, BLK, BLK), jnp.float32)],
    )(*tokens, *first, *second)


def low(values):
    return values.astype(jnp.bfloat16)


def wide(values):
    return values.astype(jnp.float32)


def dot(left, right):
    return jnp.dot(left, right, preferred_element_type=jnp.float32)


def vmem_call(kernel, microseconds, **options):
    cost = pl.CostEstimate(
        flops=int(microseconds * FLOPS_PER_US), bytes_accessed=0, transcendentals=0
    )
    return pl.pallas_call(
        kernel,
        compiler_params=pltpu.CompilerParams(vmem_limit_bytes=VMEM_LIMIT),
        cost_estimate=cost,
        **options,
    )


def full_block(shape):
    return pl.BlockSpec(shape, lambda *_: (0,) * len(shape))


def norm_parts(values):
    centred = values - jnp.mean(values, axis=-1, keepdims=True)
    scale = lax.rsqrt(jnp.mean(centred * centred, axis=-1, keepdims=True) + NORM_EPS)
    return centred * scale, scale


def norm_backward(grads, normed, scale, gain):
    inner = grads * gain
    return scale * (
        inner
        - jnp.mean(inner, axis=-1, keepdims=True)
        - normed * jnp.mean(inner * normed, axis=-1, keepdims=True)
    )


def route_mask(target, slot_total):
    slot_index = lax.broadcasted_iota(jnp.int32, (target.shape[0], slot_total), 1)
    hit = (slot_index == target[:, :1]) | (slot_index == target[:, 1:2])
    return jnp.where(hit, 1.0, 0.0)


def masked_softmax(logits, count):
    lanes = lax.broadcasted_iota(jnp.int32, logits.shape, 1)
    inside = lanes < count
    peak = jnp.max(jnp.where(inside, logits, -jnp.inf), axis=-1, keepdims=True)
    raised = jnp.where(inside, jnp.exp(jnp.where(inside, logits - peak, 0.0)), 0.0)
    return raised / jnp.sum(raised, axis=-1, keepdims=True)


def softmax_rows(scores):
    raised = jnp.exp(scores - jnp.max(scores, axis=-1, keepdims=True))
    return raised / jnp.sum(raised, axis=-1, keepdims=True)


def dispatch_kernel(target_ref, rows_ref, out_ref):
    experts, copies, steps, padded, _ = out_ref.shape
    for step in range(steps):
        routing = low(route_mask(target_ref[step], experts * padded))
        rows = column_sum(routing, rows_ref[step, 0])
        rows = low(rows.reshape(experts, padded, D))
        for copy in range(copies):
            out_ref[:, copy, step] = rows


def attention_kernel(experts, x_ref, target_ref, a_ref, *refs):
    out_refs = refs[:MB]
    qkv_ref, mixed_ref, middle_ref, probs_ref, score_ref, weight_ref = refs[MB:]
    copies, padded = out_refs[0].shape[1:3]
    inputs = wide(x_ref[0, 0])
    extra = a_ref[:, 4 * D :]
    vectors = wide(extra).T
    gains = [vectors[experts + i : experts + i + 1] for i in range(4)]
    normed, _ = norm_parts(inputs)
    normed_low = low(normed * gains[0] + gains[1])
    qkv_ref[0] = low(dot(normed_low, a_ref[:, : 3 * D]))
    lanes = lax.broadcasted_iota(jnp.int32, (SEQ, 2 * HEAD_DIM), 1)
    for head in range(HEADS):
        start = 2 * HEAD_DIM * (head // 2)
        query = qkv_ref[0, :, start : start + 2 * HEAD_DIM]
        keys = qkv_ref[0, :, D + start : D + start + 2 * HEAD_DIM]
        here = (lanes < HEAD_DIM) if head % 2 == 0 else (lanes >= HEAD_DIM)
        score_ref[head] = row_product(jnp.where(here, query, 0), keys) * HEAD_DIM ** (-0.5)
    weight_ref[...] = low(softmax_rows(score_ref[...]))
    for pair in range(HEADS // 2):
        start = 2 * HEAD_DIM * pair
        values = qkv_ref[0, :, 2 * D + start : 2 * D + start + 2 * HEAD_DIM]
        both = [dot(weight_ref[2 * pair + side], values) for side in range(2)]
        mixed_ref[0, :, start : start + 2 * HEAD_DIM] = low(
            jnp.where(lanes < HEAD_DIM, both[0], both[1])
        )
    middle = inputs + dot(mixed_ref[0], a_ref[:, 3 * D : 4 * D])
    middle_ref[0] = middle
    normed, _ = norm_parts(middle)
    moe_low = low(normed * gains[2] + gains[3])
    probs_ref[0] = masked_softmax(dot(moe_low, extra), experts)
    routing = low(route_mask(target_ref[0], experts * padded))
    rows = low(column_sum(routing, moe_low).reshape(experts, padded, D))
    for step, out_ref in enumerate(out_refs):

        @pl.when(pl.program_id(0) == step)
        def _(out_ref=out_ref):
            for copy in range(copies):
                out_ref[:, copy] = rows


def attention_backward_kernel(experts, skipped, *refs):
    refs = refs[skipped:]
    x_ref, up_ref, target_ref, back_ref, qkv_ref, mixed_ref, middle_ref, probs_ref, a_ref = refs[:9]
    score_ref, slope_ref, weight_ref, grad_score_ref = refs[-4:]
    out_ref, grad_ref, normed_ref, joined_ref, branch_ref, moe_ref, logit_ref, vector_ref = refs[
        -12:-4
    ]
    copies, padded = (back_ref.shape[1], back_ref.shape[3])
    slot_total = experts * padded
    extra = a_ref[:, 4 * D :]
    vectors = wide(extra).T
    gains = [vectors[experts + i : experts + i + 1] for i in range(4)]
    inputs = wide(x_ref[0, 0])
    upstream_low = up_ref[0, 0]
    upstream = wide(upstream_low)
    middle = middle_ref[0]
    probs = probs_ref[0]

    def collected(kind):
        total = wide(back_ref[:, 0, kind])
        for copy in range(1, copies):
            total = total + wide(back_ref[:, copy, kind])
        return low(total.reshape(slot_total, D))

    coming = collected(0)
    grad_coming = collected(1)
    routing = route_mask(target_ref[0], slot_total)
    member = jnp.where(
        lax.broadcasted_iota(jnp.int32, (probs.shape[1], slot_total), 1) // padded
        == lax.broadcasted_iota(jnp.int32, (probs.shape[1], slot_total), 0),
        1.0,
        0.0,
    )
    member_low = low(member)
    probs_high = low(probs)
    slot_gate = routing * (dot(probs_high, member_low) + dot(low(probs - wide(probs_high)), member_low))
    gate_high = low(slot_gate)
    final = middle + dot(gate_high, coming) + dot(low(slot_gate - wide(gate_high)), coming)
    out_ref[0, 0] = low(final)
    slot_grads = routing * row_product(upstream_low, coming)
    slot_high = low(slot_grads)
    prob_grads = row_product(slot_high, member_low) + row_product(
        low(slot_grads - wide(slot_high)), member_low
    )
    logit_low = low(
        probs * (prob_grads - jnp.sum(prob_grads * probs, axis=-1, keepdims=True))
    )
    logit_ref[...] = logit_low
    moe_grad = dot(low(routing), grad_coming) + row_product(logit_low, extra)
    normed, scale = norm_parts(middle)
    moe_ref[...] = low(normed * gains[2] + gains[3])
    vector_ref[2:3] = jnp.sum(moe_grad * normed, axis=0, keepdims=True)
    vector_ref[3:4] = jnp.sum(moe_grad, axis=0, keepdims=True)
    grad_middle = upstream + norm_backward(moe_grad, normed, scale, gains[2])
    branch_low = low(grad_middle)
    branch_ref[...] = branch_low
    grad_mixed = low(row_product(branch_low, a_ref[:, 3 * D : 4 * D]))
    lanes = lax.broadcasted_iota(jnp.int32, (SEQ, 2 * HEAD_DIM), 1)
    for head in range(HEADS):
        start = 2 * HEAD_DIM * (head // 2)
        stop = start + 2 * HEAD_DIM
        query = qkv_ref[0, :, start:stop]
        keys = qkv_ref[0, :, D + start : D + stop]
        values = qkv_ref[0, :, 2 * D + start : 2 * D + stop]
        here = (lanes < HEAD_DIM) if head % 2 == 0 else (lanes >= HEAD_DIM)
        score_ref[head] = row_product(jnp.where(here, query, 0), keys) * HEAD_DIM ** (-0.5)
        slope_ref[head] = row_product(jnp.where(here, grad_mixed[:, start:stop], 0), values)
    weights = softmax_rows(score_ref[...])
    weight_ref[...] = low(weights)
    slopes = slope_ref[...]
    grad_score_ref[...] = low(
        weights * (slopes - jnp.sum(slopes * weights, axis=-1, keepdims=True))
    )
    for pair in range(HEADS // 2):
        start = 2 * HEAD_DIM * pair
        stop = start + 2 * HEAD_DIM
        query = qkv_ref[0, :, start:stop]
        keys = qkv_ref[0, :, D + start : D + stop]
        grad_here = grad_mixed[:, start:stop]
        results = []
        for side in range(2):
            grad_scores = grad_score_ref[2 * pair + side]
            results.append(
                (
                    dot(grad_scores, keys) * HEAD_DIM ** (-0.5),
                    column_sum(grad_scores, query) * HEAD_DIM ** (-0.5),
                    column_sum(weight_ref[2 * pair + side], grad_here),
                )
            )
        for part in range(3):
            joined_ref[:, part * D + start : part * D + stop] = low(
                jnp.where(lanes < HEAD_DIM, results[0][part], results[1][part])
            )
    grad_normed = row_product(joined_ref[...], a_ref[:, : 3 * D])
    normed, scale = norm_parts(inputs)
    normed_ref[...] = low(normed * gains[0] + gains[1])
    vector_ref[4:8] = jnp.zeros((4, D), jnp.float32)
    vector_ref[0:1] = jnp.sum(grad_normed * normed, axis=0, keepdims=True)
    vector_ref[1:2] = jnp.sum(grad_normed, axis=0, keepdims=True)
    grad_ref[0, 0] = grad_middle + norm_backward(grad_normed, normed, scale, gains[0])


def weight_sums_kernel(experts, after_ref, core_ref, mixed_ref, *refs):
    own_ref, other_ref, token_ref = refs[-3:]
    token_ref[...] = jnp.zeros_like(token_ref)
    steps = [refs[6 * i : 6 * i + 6] for i in range(MB)]
    held, block, _ = own_ref.shape
    first_core = core_ref[0] == 0

    def write(total, start):
        stop = start + total.shape[1]
        pairs = total.reshape(held, 2, block, total.shape[1])
        even, odd = (pairs[:, 0], pairs[:, 1])
        own_ref[:, :, start:stop] = jnp.where(first_core, even, odd)
        other_ref[:, :, start:stop] = low(jnp.where(first_core, odd, even))

    for part in range(3):
        total = sum(column_sum(s[0][...], s[1][:, part * D : part * D + D]) for s in steps)
        write(total, part * D)
    write(sum(column_sum(mixed_ref[i], s[2][...]) for i, s in enumerate(steps)), 3 * D)
    vectors = sum(s[5][...] for s in steps)
    vectors = jnp.concatenate(
        [
            jnp.zeros((experts, D), jnp.float32),
            vectors,
            jnp.zeros((128 - experts - vectors.shape[0], D), jnp.float32),
        ],
        axis=0,
    )
    write(sum(column_sum(s[3][...], s[4][...]) for s in steps) + vectors.T, 4 * D)


def gelu_parts(values):
    raised = jnp.exp(-0.5 * values * values)
    root = 1.0 / (1.0 + (0.3275911 * 0.5**0.5) * jnp.abs(values))
    tail = 1.061405429 * root - 1.453152027
    tail = tail * root + 1.421413741
    tail = tail * root - 0.284496736
    tail = tail * root + 0.254829592
    tail = 0.5 * tail * root * raised
    return jnp.where(values >= 0.0, 1.0 - tail, tail), raised * 0.3989422804014327


def hidden_kernel(
    experts,
    expert_ref,
    rows_ref,
    up_ref,
    router_ref,
    weight_ref,
    bias_ref,
    hidden_ref,
    slope_ref,
    grad_ref,
    sum_ref,
):
    count, padded = rows_ref.shape[:2]
    units = weight_ref.shape[2]
    rows = low(wide(rows_ref[...]).reshape(count * padded, D))
    probs = masked_softmax(dot(rows, router_ref[...]), experts)
    lanes = lax.broadcasted_iota(jnp.int32, probs.shape, 1)
    gate = jnp.sum(jnp.where(lanes == expert_ref[0], probs, 0.0), axis=-1, keepdims=True)
    grad = low(gate * wide(up_ref[...]).reshape(count * padded, D))
    grad_ref[...] = grad

    @pl.when(pl.program_id(0) == 0)
    def _():
        sum_ref[...] = jnp.zeros_like(sum_ref)

    sum_ref[0:1] += jnp.sum(wide(grad), axis=0, keepdims=True)
    for side in range(2):
        values = dot(rows, weight_ref[side]) + bias_ref[:, side * units : (side + 1) * units]
        area, density = gelu_parts(values)
        hidden_ref[side] = low(values * area)
        slope_ref[side] = low(area + values * density)


def result_kernel(skipped, *refs):
    (
        hidden_ref,
        slope_ref,
        grad_ref,
        out_ref,
        in_ref,
        bias_ref,
        back_ref,
        pre_ref,
        sum_ref,
    ) = refs[skipped:]
    count, _, padded, _ = back_ref.shape
    units = in_ref.shape[2]

    @pl.when(pl.program_id(0) == 0)
    def _():
        sum_ref[...] = jnp.zeros_like(sum_ref)

    out_term = dot(hidden_ref[0], out_ref[0]) + dot(hidden_ref[1], out_ref[1]) + bias_ref[...]
    back_ref[:, 0] = low(out_term.reshape(count, padded, D))
    grad_term = None
    for side in range(2):
        pre = low(row_product(grad_ref[...], out_ref[side]) * wide(slope_ref[side]))
        pre_ref[side] = pre
        sum_ref[0:1, side * units : (side + 1) * units] += jnp.sum(
            wide(pre), axis=0, keepdims=True
        )
        term = row_product(pre, in_ref[side])
        grad_term = term if grad_term is None else grad_term + term
    back_ref[:, 1] = low(grad_term.reshape(count, padded, D))


def split(values):
    high = low(values)
    return high, low(values - wide(high))


def split_dot(left, right, dims):
    def one(a, b):
        return lax.dot_general(a, b, (dims, ((), ())), preferred_element_type=jnp.float32)

    return one(left[0], right[0]) + (one(left[0], right[1]) + one(left[1], right[0]))


def turn_kernel(along_rows, rate, skipped, *refs):
    refs = refs[skipped:]
    gradient_ref, weight_ref, first_ref, second_ref, stat_ref, basis_ref = refs[:6]
    first_out, second_out, weight_out, copy_out, stat_out, stretched_out = refs[-6:]
    gradient = gradient_ref[...]
    basis = basis_ref[0, 0]
    basis_parts = split(basis)
    if along_rows:
        turned = column_sum(basis_parts[0], gradient) + column_sum(basis_parts[1], gradient)
        outer = row_product(gradient, gradient)
    else:
        turned = dot(gradient, basis_parts[0]) + dot(gradient, basis_parts[1])
        outer = column_sum(gradient, gradient)
    first_new, second_new, step = moment_step(turned, first_ref[0], second_ref[0])
    first_out[0] = first_new
    second_out[0] = second_new
    step_parts = split(step)
    if along_rows:
        returned = split_dot(basis_parts, step_parts, ((1,), (0,)))
    else:
        returned = split_dot(step_parts, basis_parts, ((1,), (1,)))
    weight = weight_ref[0]
    weight_new = weight - rate * (returned + DECAY_RATE * weight)
    weight_out[0] = weight_new
    copy_out[0] = low(weight_new)
    stat_new = STAT_DECAY * stat_ref[0, 0] + (1.0 - STAT_DECAY) * outer
    stat_out[0, 0] = stat_new
    stretched_out[...] = mm(stat_new, basis)


def dense_update_kernel(kept_ref, received_ref, *refs):
    inputs, outputs = (refs[:9], refs[9:])
    gradient = kept_ref[...] + wide(received_ref[...])
    extra = gradient[:, 4 * D :].T
    experts = inputs[3].shape[0]
    gradients = (gradient[:, : 4 * D], extra[:experts], extra[experts : experts + 4])
    rates = ((RATE_DENSE, DECAY_RATE), (RATE_DENSE, DECAY_RATE), (RATE_NORMS, 0.0))
    place = 0
    for kind in range(3):
        weight, first, second = (r[...] for r in inputs[3 * kind : 3 * kind + 3])
        first_new, second_new, weight_new = adam_update(
            weight, gradients[kind], first, second, *rates[kind]
        )
        outputs[place][...] = first_new
        outputs[place + 1][...] = second_new
        outputs[place + 2][...] = weight_new
        place += 3
        if kind < 2:
            outputs[place][...] = low(weight_new)
            place += 1


def row_sums_kernel(*refs):
    total = sum(column_sum(refs[i][...], refs[MB + i][...]) for i in range(MB))
    refs[-1][...] = low(total)


def swap(values, axis, distance):
    size = lax.axis_size(axis)
    return lax.ppermute(values, axis, [(i, i ^ distance) for i in range(size)])


def across(values):
    size = lax.axis_size(TENSOR)
    return lax.ppermute(values, TENSOR, [(i, (i + size // 2) % size) for i in range(size)])


def ordered(bit, mine, other):
    return jnp.where(bit == 0, jnp.stack([mine, other]), jnp.stack([other, mine]))


def gather_tensor(shard):
    tensors, tensor = (lax.axis_size(TENSOR), lax.axis_index(TENSOR))
    block = shard[None]
    distance = 1
    while distance < tensors:
        other = swap(block, TENSOR, distance)
        block = ordered((tensor // distance) % 2, block, other).reshape(-1, *shard.shape)
        distance *= 2
    return block


def gather_experts(block, beside, released, waiting):
    experts, tensors = (lax.axis_size(EXPERT), lax.axis_size(TENSOR))
    expert = lax.axis_index(EXPERT)
    columns = block.shape[-1]
    block = block[None]
    distance = 2
    while distance < experts // 4:
        other = swap(block, EXPERT, distance)
        block = ordered((expert // distance) % 2, block, other).reshape(-1, *block.shape[1:])
        distance *= 2
    near, far = (distance, 2 * distance)
    middle = tensors // 2
    from_near, from_far = (swap(block, EXPERT, near), swap(block, EXPERT, far))
    corner = jnp.concatenate(
        [swap(from_far[:, :middle], EXPERT, near), swap(from_near[:, middle:], EXPERT, far)],
        axis=1,
    )
    corner, beside, released, waiting = lax.optimization_barrier(
        (corner, beside, released, waiting)
    )
    pieces = (block, from_near, from_far, corner)
    crossed = [swap(piece, EXPERT, 1) for piece in pieces]
    near_bit, far_bit = ((expert // near) % 2, (expert // far) % 2)

    def arranged(four):
        return ordered(
            far_bit,
            ordered(near_bit, four[0], four[1]),
            ordered(near_bit, four[2], four[3]),
        ).reshape(-1, *block.shape[1:])

    whole = ordered(expert % 2, arranged(pieces), arranged(crossed))
    whole = jnp.moveaxis(whole, 0, 1)
    return whole.reshape(-1, columns), beside, across(released), waiting


def scatter_sums(held, sending):
    experts, tensors = (lax.axis_size(EXPERT), lax.axis_size(TENSOR))
    expert, tensor = (lax.axis_index(EXPERT), lax.axis_index(TENSOR))
    columns = held.shape[2]

    def pick(values, index, axis=0):
        return lax.dynamic_index_in_dim(values, index, axis, False)

    held = held + wide(swap(sending, EXPERT, 1))
    stages = [held]
    near, far = (experts // 4, experts // 2)
    near_bit, far_bit = ((expert // near) % 2, (expert // far) % 2)
    held = held.reshape(4, experts // 8, tensors, -1, columns)
    place = 2 * far_bit + near_bit
    own, to_near, to_far, to_corner = (
        pick(held, place),
        pick(held, place ^ 1),
        pick(held, place ^ 2),
        pick(held, place ^ 3),
    )
    middle = tensors // 2
    passed_near = swap(low(to_corner[:, :middle]), EXPERT, near)
    passed_far = swap(low(to_corner[:, middle:]), EXPERT, far)
    to_far = jnp.concatenate([to_far[:, :middle] + wide(passed_near), to_far[:, middle:]], axis=1)
    to_near = jnp.concatenate([to_near[:, :middle], to_near[:, middle:] + wide(passed_far)], axis=1)
    stages.append(to_near)
    held = (
        own
        + wide(swap(low(to_near), EXPERT, near))
        + wide(swap(low(to_far), EXPERT, far))
    )
    distance = experts // 8
    while distance >= 2:
        bit = (expert // distance) % 2
        halves = held.reshape(2, -1, *held.shape[1:])
        held = pick(halves, bit) + wide(swap(low(pick(halves, 1 - bit)), EXPERT, distance))
        distance //= 2
    stages.append(held)
    held = held.reshape(tensors, -1, columns)
    distance = tensors // 2
    while distance >= 1:
        bit = (tensor // distance) % 2
        halves = held.reshape(2, -1, *held.shape[1:])
        kept = pick(halves, bit)
        received = swap(low(pick(halves, 1 - bit)), TENSOR, distance)
        if distance > 1:
            held = kept + wide(received)
        distance //= 2
    stages.append(kept)
    return kept.reshape(-1, columns), received.reshape(-1, columns), stages


def soap_turn(along_rows, rate, at, token, gradient, state, statistics, earlier):
    weight, first, second = state
    statistic = statistics[0]
    f32 = jnp.float32
    if along_rows:
        deep = pl.BlockSpec((1, BLK, D), lambda i: (0, at, 0))
    else:
        deep = pl.BlockSpec((1, D, BLK), lambda i: (0, 0, at))
    square = pl.BlockSpec((1, 1, BLK, BLK), lambda i: (0, at, 0, 0))
    anywhere = pl.BlockSpec(memory_space=pl.ANY)
    return vmem_call(
        partial(turn_kernel, along_rows, rate, len(token)),
        8,
        grid=(1,),
        in_specs=[anywhere] * len(token)
        + [full_block(gradient.shape)]
        + [deep] * 3
        + [square] * 2
        + [anywhere] * len(earlier),
        out_specs=[deep] * 4 + [square, full_block((BLK, BLK))],
        out_shape=[jax.ShapeDtypeStruct(weight.shape, f32)] * 3
        + [
            jax.ShapeDtypeStruct(weight.shape, jnp.bfloat16),
            jax.ShapeDtypeStruct(statistic.shape, f32),
            jax.ShapeDtypeStruct((BLK, BLK), f32),
        ],
        input_output_aliases={6 + len(token) + i: i for i in range(len(earlier))},
    )(*token, gradient, *state, *statistics, *earlier)


def row_sums(left, right, at, left_paired):
    rows, width = left[0].shape[-2:]
    height, columns = (BLK, right[0].shape[-1]) if left_paired else (width, BLK)
    paired = pl.BlockSpec((None, rows, BLK), lambda i: (i, 0, at))
    plain = full_block((rows, columns if left_paired else width))
    return vmem_call(
        row_sums_kernel,
        5,
        grid=(2,),
        in_specs=[paired if left_paired else plain] * MB
        + [plain if left_paired else paired] * MB,
        out_specs=pl.BlockSpec((None, height, columns), lambda i: (i, 0, 0)),
        out_shape=jax.ShapeDtypeStruct((2, height, columns), jnp.bfloat16),
    )(*left, *right)


def per_device(
    patches,
    cotangent,
    expert_ids,
    slots,
    attn_weights,
    attn_first,
    attn_second,
    router_weights,
    router_first,
    router_second,
    norm_params,
    norm_first,
    norm_second,
    w_in,
    w_in_first,
    w_in_second,
    w_in_stat,
    w_in_basis,
    w_out,
    w_out_first,
    w_out_second,
    w_out_stat,
    w_out_basis,
    b_in,
    b_in_first,
    b_in_second,
    b_out,
    b_out_first,
    b_out_second,
):
    tokens_here = SEQ
    expert_total = router_weights.shape[1]
    capacity = (105 * TOPK * tokens_here + 100 * expert_total - 1) // (100 * expert_total)
    padded = 8 * ((capacity + 7) // 8)
    experts, tensors = (lax.axis_size(EXPERT), lax.axis_size(TENSOR))
    expert, tensor = (lax.axis_index(EXPERT), lax.axis_index(TENSOR))
    half = tensors // 2
    members = expert_total * half
    units = w_in.shape[2]
    shard_columns = b_out.shape[1]
    columns = 4 * D + 128
    bf16, f32 = (jnp.bfloat16, jnp.float32)
    shape = jax.ShapeDtypeStruct
    pairs = [[i, i + half] for i in range(half)]
    groups = [
        [e * tensors + z for e in range(experts) for z in range(h * half, (h + 1) * half)]
        for h in range(2)
    ]

    def exchange(values):
        return lax.all_to_all(values, BOTH, 0, 0, axis_index_groups=groups, tiled=True)

    packed = jnp.concatenate(
        [
            low(attn_weights),
            low(router_weights),
            low(norm_params).T,
            jnp.zeros((attn_weights.shape[0], 128 - expert_total - 4), bf16),
        ],
        axis=1,
    )
    in_own, out_own = (low(w_in[0]), low(w_out[0]))
    b_in_low, b_out_low = (low(b_in), low(b_out))
    peer_bias = across(jnp.concatenate([b_in_low, b_out_low], axis=1))
    chosen = expert_ids.reshape(MB, tokens_here, TOPK)
    placed = slots.reshape(MB, tokens_here, TOPK)
    target = jnp.where(placed < capacity, chosen * padded + placed, -1)
    up_sent = vmem_call(
        dispatch_kernel,
        4,
        grid=(1,),
        in_specs=[full_block(target.shape), full_block(cotangent.shape)],
        out_specs=full_block((expert_total, half, MB, padded, D)),
        out_shape=shape((expert_total, half, MB, padded, D), bf16),
    )(target, cotangent)
    first_stage, peer_bias, sent_first = lax.optimization_barrier(
        (gather_tensor(packed), peer_bias, in_own[: D // 2])
    )
    out_pair = lax.all_gather(out_own, TENSOR, axis_index_groups=pairs)
    gathered, in_first, in_second, up_sent = gather_experts(
        first_stage, across(sent_first), in_own[D // 2 :], up_sent
    )
    up_all = exchange(up_sent.reshape(members, MB, padded, D))
    upper = tensor >= half
    peer_in = peer_bias[:, :units]
    bias_in = wide(
        jnp.where(
            upper,
            jnp.concatenate([peer_in, b_in_low], axis=1),
            jnp.concatenate([b_in_low, peer_in], axis=1),
        )
    )
    bias_out = jnp.zeros((1, D), f32)
    own_place = tensor * shard_columns
    peer_place = ((tensor + half) % tensors) * shard_columns
    bias_out = lax.dynamic_update_slice(bias_out, wide(b_out_low), (0, own_place))
    bias_out = lax.dynamic_update_slice(bias_out, wide(peer_bias[:, units:]), (0, peer_place))
    image = pl.BlockSpec((1, 1, SEQ, D), lambda i: (i, 0, 0, 0))

    def per_step(*tail):
        return pl.BlockSpec((1, *tail), lambda i: (i,) + (0,) * len(tail))

    *sent, qkv, mixed, middle, probs = vmem_call(
        partial(attention_kernel, expert_total),
        11,
        grid=(MB,),
        in_specs=[image, per_step(SEQ, TOPK), full_block((D, columns))],
        out_specs=[
            *[full_block((expert_total, half, padded, D))] * MB,
            per_step(SEQ, 3 * D),
            per_step(SEQ, D),
            per_step(SEQ, D),
            per_step(SEQ, 128),
        ],
        out_shape=[
            *[shape((expert_total, half, padded, D), bf16)] * MB,
            shape((MB, SEQ, 3 * D), bf16),
            shape((MB, SEQ, D), bf16),
            shape((MB, SEQ, D), f32),
            shape((MB, SEQ, 128), f32),
        ],
        scratch_shapes=[pltpu.VMEM((HEADS, SEQ, SEQ), f32), pltpu.VMEM((HEADS, SEQ, SEQ), bf16)],
    )(patches, target, gathered)
    earlier, up_all, in_second = lax.optimization_barrier((sent[0], up_all, in_second))
    in_peer = jnp.concatenate([in_first, in_second], axis=0)
    in_pair = jnp.where(upper, jnp.stack([in_peer, in_own]), jnp.stack([in_own, in_peer]))
    arrived = [exchange(earlier.reshape(members, padded, D))]
    later, arrived[0] = lax.optimization_barrier((sent[1], arrived[0]))
    arrived.append(exchange(later.reshape(members, padded, D)))
    count = max(
        n
        for n in range(1, members + 1)
        if members % n == 0 and n * padded <= ROW_TILE and (n * padded) % 16 == 0
    )
    tile = count * padded
    total_rows = members * padded
    tiles = members // count

    def rows_of(width):
        return pl.BlockSpec((tile, width), lambda i: (i, 0))

    expert_scalar = jnp.reshape(expert, (1,)).astype(jnp.int32)
    in_smem = pl.BlockSpec(memory_space=pltpu.SMEM)
    anywhere = pl.BlockSpec(memory_space=pl.ANY)
    both_rows = pl.BlockSpec((2, tile, units), lambda i: (0, i, 0))
    both_shape = shape((2, total_rows, units), bf16)
    hidden = []
    for step in range(MB):
        hidden.append(
            vmem_call(
                partial(hidden_kernel, expert_total),
                12,
                grid=(tiles,),
                in_specs=[
                    in_smem,
                    pl.BlockSpec((count, padded, D), lambda i: (i, 0, 0)),
                    pl.BlockSpec((count, None, padded, D), lambda i, step=step: (i, step, 0, 0)),
                    pl.BlockSpec((D, 128), lambda i: (0, 4 * D // 128)),
                    full_block((2, D, units)),
                    full_block((1, 2 * units)),
                ],
                out_specs=[both_rows] * 2 + [rows_of(D), full_block((8, D))],
                out_shape=[both_shape] * 2
                + [shape((total_rows, D), bf16), shape((8, D), f32)],
            )(expert_scalar, arrived[step], up_all, gathered, in_pair, bias_in)
        )
    blocks = units // BLK
    row_grads = [h[2] for h in hidden]
    sum_out = [row_sums([h[0] for h in hidden], row_grads, at, True) for at in range(blocks)]
    results = []
    for step in range(MB):
        before = [] if step == 0 else sum_out
        results.append(
            vmem_call(
                partial(result_kernel, len(before)),
                12,
                grid=(tiles,),
                in_specs=[anywhere] * len(before)
                + [both_rows] * 2
                + [
                    rows_of(D),
                    full_block((2, units, D)),
                    full_block((2, D, units)),
                    full_block((1, D)),
                ],
                out_specs=[
                    pl.BlockSpec((count, 2, padded, D), lambda i: (i, 0, 0, 0)),
                    both_rows,
                    full_block((8, 2 * units)),
                ],
                out_shape=[
                    shape((members, 2, padded, D), bf16),
                    both_shape,
                    shape((8, 2 * units), f32),
                ],
            )(*before, *hidden[step][:3], out_pair, in_pair, bias_out)
        )
    flat_rows = [rows.reshape(total_rows, D) for rows in arrived]
    sum_in = [row_sums(flat_rows, [r[1] for r in results], at, False) for at in range(blocks)]

    def shared(sums):
        return lax.psum_scatter(sums, TENSOR, axis_index_groups=pairs)

    grads_out = [shared(sums) for sums in sum_out]
    grads_in = [shared(sums) for sums in sum_in]
    returned = [exchange(r[0]) for r in results]
    sum_bin = sum(r[2][:1] for r in results)
    sum_bout = sum(h[3][:1] for h in hidden)
    bias_sums = jnp.concatenate(
        [
            jnp.where(upper, sum_bin[:, :units], sum_bin[:, units:]),
            lax.dynamic_slice_in_dim(sum_bout, peer_place, shard_columns, 1),
        ],
        axis=1,
    )
    bias_other = across(bias_sums)
    backward = []
    tokens = [sum_in]
    for step in range(MB):
        first = step == 0
        here = pl.BlockSpec((1, 1, SEQ, D), lambda i, step=step: (step, 0, 0, 0))

        def of_step(*tail, step=step):
            return pl.BlockSpec((1, *tail), lambda i: (step,) + (0,) * len(tail))

        back = returned[step].reshape(expert_total, half, 2, padded, D)
        outs = [
            (shape(patches.shape, bf16), here),
            (shape(patches.shape, f32), here),
            (shape((SEQ, D), bf16), full_block((SEQ, D))),
            (shape((SEQ, 3 * D), bf16), full_block((SEQ, 3 * D))),
            (shape((SEQ, D), bf16), full_block((SEQ, D))),
            (shape((SEQ, D), bf16), full_block((SEQ, D))),
            (shape((SEQ, 128), bf16), full_block((SEQ, 128))),
            (shape((8, D), f32), full_block((8, D))),
        ]
        earlier = [] if first else list(backward[-1][:2])
        backward.append(
            vmem_call(
                partial(attention_backward_kernel, expert_total, len(tokens[step])),
        15,
                grid=(1,),
                in_specs=[anywhere] * len(tokens[step])
                + [
                    here,
                    here,
                    of_step(SEQ, TOPK),
                    full_block(back.shape),
                    of_step(SEQ, 3 * D),
                    of_step(SEQ, D),
                    of_step(SEQ, D),
                    of_step(SEQ, 128),
                    full_block((D, columns)),
                ]
                + [pl.BlockSpec(memory_space=pl.ANY)] * len(earlier),
                out_specs=[o[1] for o in outs],
                out_shape=[o[0] for o in outs],
                scratch_shapes=[pltpu.VMEM((HEADS, SEQ, SEQ), f32)] * 2
                + [pltpu.VMEM((HEADS, SEQ, SEQ), bf16)] * 2,
                input_output_aliases={}
                if first
                else {9 + len(tokens[step]): 0, 10 + len(tokens[step]): 1},
            )(
                *tokens[step],
                patches,
                cotangent,
                target,
                back,
                qkv,
                mixed,
                middle,
                probs,
                gathered,
                *earlier,
            )
        )
        if first:
            out_turned = [
                soap_turn(
                    True,
                    RATE_OUTPUT,
                    0,
                    [backward[0][6]],
                    grads_out[0],
                    (w_out, w_out_first, w_out_second),
                    (w_out_stat, w_out_basis),
                    [],
                )
            ]
            tokens.append([out_turned[0][5]])
    core_scalar = jnp.reshape(expert % 2, (1,)).astype(jnp.int32)
    block_rows = tensors * attn_weights.shape[0]
    flat_steps = [value for b in backward for value in b[2:]]
    core_shape = (experts // 2, block_rows, columns)
    held, sending, token = vmem_call(
        partial(weight_sums_kernel, expert_total),
        8,
        grid=(1,),
        in_specs=[anywhere, in_smem] + [full_block(v.shape) for v in (mixed, *flat_steps)],
        out_specs=[full_block(core_shape)] * 2 + [full_block((8, 128))],
        out_shape=[shape(core_shape, f32), shape(core_shape, bf16), shape((8, 128), f32)],
    )(b_in_low, core_scalar, mixed, *flat_steps)
    kept, received, stages = scatter_sums(held, sending)
    dense = [shape(attn_weights.shape, f32)] * 3 + [shape(attn_weights.shape, bf16)]
    turned_shape = router_weights.shape[::-1]
    routers = [shape(turned_shape, f32)] * 3 + [shape(turned_shape, bf16)]
    norms = [shape(norm_params.shape, f32)] * 3
    states = (
        kept,
        received,
        attn_weights,
        attn_first,
        attn_second,
        router_weights.T,
        router_first.T,
        router_second.T,
        norm_params,
        norm_first,
        norm_second,
    )
    updated_shapes = dense + routers + norms
    updated = vmem_call(
        dense_update_kernel,
        3,
        grid=(1,),
        in_specs=[full_block(v.shape) for v in states],
        out_specs=[full_block(v.shape) for v in updated_shapes],
        out_shape=updated_shapes,
    )(*states)
    for at in range(1, blocks):
        out_turned.append(
            soap_turn(
                True,
                RATE_OUTPUT,
                at,
                [token],
                grads_out[at],
                (w_out, w_out_first, w_out_second),
                (w_out_stat, w_out_basis),
                out_turned[-1][:5],
            )
        )
    in_turned = []
    for at in range(blocks):
        in_turned.append(
            soap_turn(
                False,
                RATE_INPUT,
                at,
                [out_turned[-1][5], stages[0]] if at == 0 else [in_turned[-1][5], stages[2]],
                grads_in[at],
                (w_in, w_in_first, w_in_second),
                (w_in_stat, w_in_basis),
                in_turned[-1][:5] if at > 0 else [],
            )
        )
    w_out_basis_new, w_in_basis_new = renew(
        stages[3:], [turned[5] for turned in out_turned], [turned[5] for turned in in_turned]
    )
    bias_other, w_in_basis_new = lax.optimization_barrier((bias_other, w_in_basis_new))
    w_in_results = (*in_turned[-1][:5], w_in_basis_new)
    w_out_results = (*out_turned[-1][:5], w_out_basis_new)
    own_bin = jnp.where(upper, sum_bin[:, units:], sum_bin[:, :units])
    grad_bin = own_bin + bias_other[:, :units]
    grad_bout = (
        lax.dynamic_slice_in_dim(sum_bout, own_place, shard_columns, 1) + bias_other[:, units:]
    )
    bin_first_new, bin_second_new, bin_new = adam_update(
        b_in, grad_bin, b_in_first, b_in_second, RATE_BIASES, 0.0
    )
    bout_first_new, bout_second_new, bout_new = adam_update(
        b_out, grad_bout, b_out_first, b_out_second, RATE_OFFSETS, 0.0
    )
    return (
        *backward[-1][:2],
        *updated[:4],
        *(value.T for value in updated[4:8]),
        *updated[8:],
        *w_in_results,
        *w_out_results,
        bin_first_new,
        bin_second_new,
        bin_new,
        bout_first_new,
        bout_second_new,
        bout_new,
    )


def solution(mesh):
    tokens = P(None, BOTH, None, None)
    rows = P(BOTH, None)
    columns = P(None, BOTH)
    first_layer = P(EXPERT, None, TENSOR)
    second_layer = P(EXPERT, TENSOR, None)
    blocks = P(EXPERT, TENSOR, None, None)
    biases = P(EXPERT, TENSOR)
    in_specs = (
        (tokens,) * 4
        + (rows,) * 6
        + (columns,) * 3
        + (first_layer,) * 3
        + (blocks,) * 2
        + (second_layer,) * 3
        + (blocks,) * 2
        + (biases,) * 6
    )
    out_specs = (
        (tokens,) * 2
        + (rows,) * 8
        + (columns,) * 3
        + (first_layer,) * 4
        + (blocks,) * 2
        + (second_layer,) * 4
        + (blocks,) * 2
        + (biases,) * 6
    )
    return jax.shard_map(
        per_device, mesh=mesh, in_specs=in_specs, out_specs=out_specs, check_vma=False
    )
```

```python
from functools import partial

import jax
import jax.numpy as jnp
from jax import lax
from jax.experimental import pallas as pl
from jax.experimental.pallas import tpu as pltpu
from jax.sharding import PartitionSpec as P

D = 768
HEADS = 12
HEAD_DIM = 64
SEQ = 196
TOPK = 2
MB = 2
STEP = 10
BLK = 384


MATMUL_ACCURACY = lax.Precision.HIGHEST
NORM_EPS = 1e-06
BETA_FIRST = 0.5
BETA_SECOND = 0.5
STAT_DECAY = 0.5
ADAM_EPS = 1e-08
DECAY_RATE = 0.1
RATE_DENSE = 0.05
RATE_NORMS = 0.4
RATE_INPUT = 0.04
RATE_OUTPUT = 0.4
RATE_BIASES = 0.05
RATE_OFFSETS = 1.0


def column_sum(left_side, right_side):
    return lax.dot_general(
        left_side, right_side, (((0,), (0,)), ((), ())), preferred_element_type=jnp.float32
    )


def row_product(left_side, right_side):
    return lax.dot_general(
        left_side, right_side, (((1,), (1,)), ((), ())), preferred_element_type=jnp.float32
    )


def moment_step(gradient, first_moment, second_moment):
    first_new = BETA_FIRST * first_moment + (1.0 - BETA_FIRST) * gradient
    second_new = BETA_SECOND * second_moment + (1.0 - BETA_SECOND) * gradient * gradient
    normed_step = (
        first_new
        / (1.0 - BETA_FIRST**STEP)
        / (jnp.sqrt(second_new / (1.0 - BETA_SECOND**STEP)) + ADAM_EPS)
    )
    return (first_new, second_new, normed_step)


def adam_update(weight, gradient, first_moment, second_moment, step_rate, weight_decay):
    first_new, second_new, normed_step = moment_step(gradient, first_moment, second_moment)
    return (first_new, second_new, weight - step_rate * (normed_step + weight_decay * weight))


EXPERT = "expert"
TENSOR = "tensor"
BOTH = (EXPERT, TENSOR)
VMEM_LIMIT = 56 * 2**20
FLOPS_PER_US = 1.1e9
ROW_TILE = 512
SUB = 64


def mm(left, right):
    return jnp.dot(left, right, preferred_element_type=jnp.float32, precision=MATMUL_ACCURACY)


def mt(left, right):
    return lax.dot_general(
        left,
        right,
        (((1,), (1,)), ((), ())),
        preferred_element_type=jnp.float32,
        precision=MATMUL_ACCURACY,
    )


def tm(left, right):
    return lax.dot_general(
        left,
        right,
        (((0,), (0,)), ((), ())),
        preferred_element_type=jnp.float32,
        precision=MATMUL_ACCURACY,
    )


def factor_inverse(mats):
    n=SUB; B=jnp.broadcast_to; w=(8,2*n)
    lane=lax.broadcasted_iota(jnp.int32,w,1); sub=lax.broadcasted_iota(jnp.int32,w,0)
    X=[]
    for m in mats:
        tiles=[]
        for i in range(n//8):
            eye=jnp.where(lane==sub+8*i+n,1.0,0.0)
            tiles.append(jnp.concatenate([m[8*i:8*i+8,:],eye[:,n:]],axis=1))
        X.append(tiles)
    outs=[[] for _ in mats]
    for r in range(n//8):
        for m,tiles in enumerate(X):
            T=tiles[r]
            cols=[[B(tiles[t][:,8*r+k:8*r+k+1],w) for k in range(8)] for t in range(r,n//8)]
            a=[[B(cols[0][j][i:i+1,:],w) for j in range(i+1)] for i in range(8)]
            rows=[B(T[i:i+1,:],w) for i in range(8)]
            inv=[None]*8; l=[[None]*8 for _ in range(8)]
            for k in range(8):
                inv[k]=1.0/a[k][k]
                for i in range(k+1,8): l[i][k]=a[i][k]*inv[k]
                for i in range(k+1,8):
                    for j in range(k+1,i+1):
                        a[i][j]=a[i][j]-l[i][k]*a[j][k]
                for i in range(k+1,8): rows[i]=rows[i]-l[i][k]*rows[k]
            o=jnp.zeros(w,jnp.float32)
            for k in range(8): o=jnp.where(sub==k,rows[k]*lax.rsqrt(a[k][k]),o)
            outs[m].append(o[:,n:])
            if r+1<n//8:
                wv=[rows[k]*inv[k] for k in range(8)]
                for k in range(6,-1,-1):
                    for j in range(k+1,8): wv[k]=wv[k]-l[j][k]*wv[j]
                for t in range(r+1,n//8):
                    c=cols[t-r]
                    acc=c[0]*wv[0]
                    for k in range(1,8): acc=acc+c[k]*wv[k]
                    tiles[t]=tiles[t]-acc
    return [jnp.concatenate(o,axis=0) for o in outs]
def renew_kernel(skipped, *refs):
    refs=refs[skipped:]
    m_ref=refs[-1]
    zs=refs[:-3]
    nb=len(zs)
    qs=[r.at[0,i] for r in refs[-3:-1] for i in range(r.shape[1])]
    n=BLK; kb=n//128; h=SUB
    for b in range(nb):
        z=zs[b][...]
        m_ref[b]=tm(z,z)
    for k in range(kb):
        o=128*k; sl=slice(o,o+128)
        d11=[m_ref[b,o:o+h,o:o+h] for b in range(nb)]
        i1=factor_inverse(d11)
        l21=[mt(m_ref[b,o+h:o+128,o:o+h],i1[b]) for b in range(nb)]
        d22=[m_ref[b,o+h:o+128,o+h:o+128]-mt(l21[b],l21[b]) for b in range(nb)]
        i2=factor_inverse(d22)
        inv=[]
        for b in range(nb):
            low=-mm(mm(i2[b],l21[b]),i1[b])
            inv.append(jnp.concatenate([jnp.concatenate([i1[b],jnp.zeros((h,h),jnp.float32)],1),jnp.concatenate([low,i2[b]],1)],0))
        for b in range(nb):
            q=zs[b][:,sl]
            for j in range(k):
                q=q-mt(qs[b][:,128*j:128*j+128],m_ref[b,sl,128*j:128*j+128])
            qs[b][:,sl]=mt(q,inv[b])
            if k+1<kb:
                p=mt(m_ref[b,o+128:,sl],inv[b])
                m_ref[b,o+128:,sl]=p
                m_ref[b,o+128:,o+128:]=m_ref[b,o+128:,o+128:]-mt(p,p)
def renew(tokens, first, second):
    shapes=[(1, len(group), BLK, BLK) for group in (first, second)]
    count=len(first)+len(second)
    return vmem_call(
        partial(renew_kernel, len(tokens)),
        40,
        grid=(1,),
        out_shape=[jax.ShapeDtypeStruct(s, jnp.float32) for s in shapes],
        in_specs=[pl.BlockSpec(memory_space=pl.ANY)] * len(tokens)
        + [full_block((BLK, BLK))] * count,
        out_specs=[full_block(s) for s in shapes],
        scratch_shapes=[pltpu.VMEM((count, BLK, BLK), jnp.float32)],
    )(*tokens, *first, *second)


def low(values):
    return values.astype(jnp.bfloat16)


def wide(values):
    return values.astype(jnp.float32)


def dot(left, right):
    return jnp.dot(left, right, preferred_element_type=jnp.float32)


def vmem_call(kernel, microseconds, **options):
    cost = pl.CostEstimate(
        flops=int(microseconds * FLOPS_PER_US), bytes_accessed=0, transcendentals=0
    )
    return pl.pallas_call(
        kernel,
        compiler_params=pltpu.CompilerParams(vmem_limit_bytes=VMEM_LIMIT),
        cost_estimate=cost,
        **options,
    )


def full_block(shape):
    return pl.BlockSpec(shape, lambda *_: (0,) * len(shape))


def norm_parts(values):
    centred = values - jnp.mean(values, axis=-1, keepdims=True)
    scale = lax.rsqrt(jnp.mean(centred * centred, axis=-1, keepdims=True) + NORM_EPS)
    return centred * scale, scale


def norm_backward(grads, normed, scale, gain):
    inner = grads * gain
    return scale * (
        inner
        - jnp.mean(inner, axis=-1, keepdims=True)
        - normed * jnp.mean(inner * normed, axis=-1, keepdims=True)
    )


def route_mask(target, slot_total):
    slot_index = lax.broadcasted_iota(jnp.int32, (target.shape[0], slot_total), 1)
    hit = (slot_index == target[:, :1]) | (slot_index == target[:, 1:2])
    return jnp.where(hit, 1.0, 0.0)


def masked_softmax(logits, count):
    lanes = lax.broadcasted_iota(jnp.int32, logits.shape, 1)
    inside = lanes < count
    peak = jnp.max(jnp.where(inside, logits, -jnp.inf), axis=-1, keepdims=True)
    raised = jnp.where(inside, jnp.exp(jnp.where(inside, logits - peak, 0.0)), 0.0)
    return raised / jnp.sum(raised, axis=-1, keepdims=True)


def softmax_rows(scores):
    raised = jnp.exp(scores - jnp.max(scores, axis=-1, keepdims=True))
    return raised / jnp.sum(raised, axis=-1, keepdims=True)


def dispatch_kernel(target_ref, rows_ref, out_ref):
    experts, copies, steps, padded, _ = out_ref.shape
    for step in range(steps):
        routing = low(route_mask(target_ref[step], experts * padded))
        rows = column_sum(routing, rows_ref[step, 0])
        rows = low(rows.reshape(experts, padded, D))
        for copy in range(copies):
            out_ref[:, copy, step] = rows


def attention_kernel(experts, x_ref, target_ref, a_ref, *refs):
    out_refs = refs[:MB]
    qkv_ref, mixed_ref, middle_ref, probs_ref, score_ref, weight_ref = refs[MB:]
    copies, padded = out_refs[0].shape[1:3]
    inputs = wide(x_ref[0, 0])
    extra = a_ref[:, 4 * D :]
    vectors = wide(extra).T
    gains = [vectors[experts + i : experts + i + 1] for i in range(4)]
    normed, _ = norm_parts(inputs)
    normed_low = low(normed * gains[0] + gains[1])
    qkv_ref[0] = low(dot(normed_low, a_ref[:, : 3 * D]))
    lanes = lax.broadcasted_iota(jnp.int32, (SEQ, 2 * HEAD_DIM), 1)
    for head in range(HEADS):
        start = 2 * HEAD_DIM * (head // 2)
        query = qkv_ref[0, :, start : start + 2 * HEAD_DIM]
        keys = qkv_ref[0, :, D + start : D + start + 2 * HEAD_DIM]
        here = (lanes < HEAD_DIM) if head % 2 == 0 else (lanes >= HEAD_DIM)
        score_ref[head] = row_product(jnp.where(here, query, 0), keys) * HEAD_DIM ** (-0.5)
    weight_ref[...] = low(softmax_rows(score_ref[...]))
    for pair in range(HEADS // 2):
        start = 2 * HEAD_DIM * pair
        values = qkv_ref[0, :, 2 * D + start : 2 * D + start + 2 * HEAD_DIM]
        both = [dot(weight_ref[2 * pair + side], values) for side in range(2)]
        mixed_ref[0, :, start : start + 2 * HEAD_DIM] = low(
            jnp.where(lanes < HEAD_DIM, both[0], both[1])
        )
    middle = inputs + dot(mixed_ref[0], a_ref[:, 3 * D : 4 * D])
    middle_ref[0] = middle
    normed, _ = norm_parts(middle)
    moe_low = low(normed * gains[2] + gains[3])
    probs_ref[0] = masked_softmax(dot(moe_low, extra), experts)
    routing = low(route_mask(target_ref[0], experts * padded))
    rows = low(column_sum(routing, moe_low).reshape(experts, padded, D))
    for step, out_ref in enumerate(out_refs):

        @pl.when(pl.program_id(0) == step)
        def _(out_ref=out_ref):
            for copy in range(copies):
                out_ref[:, copy] = rows


def attention_backward_kernel(experts, skipped, *refs):
    refs = refs[skipped:]
    x_ref, up_ref, target_ref, back_ref, qkv_ref, mixed_ref, middle_ref, probs_ref, a_ref = refs[:9]
    score_ref, slope_ref, weight_ref, grad_score_ref = refs[-4:]
    out_ref, grad_ref, normed_ref, joined_ref, branch_ref, moe_ref, logit_ref, vector_ref = refs[
        -12:-4
    ]
    copies, padded = (back_ref.shape[1], back_ref.shape[3])
    slot_total = experts * padded
    extra = a_ref[:, 4 * D :]
    vectors = wide(extra).T
    gains = [vectors[experts + i : experts + i + 1] for i in range(4)]
    inputs = wide(x_ref[0, 0])
    upstream_low = up_ref[0, 0]
    upstream = wide(upstream_low)
    middle = middle_ref[0]
    probs = probs_ref[0]

    def collected(kind):
        total = wide(back_ref[:, 0, kind])
        for copy in range(1, copies):
            total = total + wide(back_ref[:, copy, kind])
        return low(total.reshape(slot_total, D))

    coming = collected(0)
    grad_coming = collected(1)
    routing = route_mask(target_ref[0], slot_total)
    member = jnp.where(
        lax.broadcasted_iota(jnp.int32, (probs.shape[1], slot_total), 1) // padded
        == lax.broadcasted_iota(jnp.int32, (probs.shape[1], slot_total), 0),
        1.0,
        0.0,
    )
    member_low = low(member)
    probs_high = low(probs)
    slot_gate = routing * (dot(probs_high, member_low) + dot(low(probs - wide(probs_high)), member_low))
    gate_high = low(slot_gate)
    final = middle + dot(gate_high, coming) + dot(low(slot_gate - wide(gate_high)), coming)
    out_ref[0, 0] = low(final)
    slot_grads = routing * row_product(upstream_low, coming)
    slot_high = low(slot_grads)
    prob_grads = row_product(slot_high, member_low) + row_product(
        low(slot_grads - wide(slot_high)), member_low
    )
    logit_low = low(
        probs * (prob_grads - jnp.sum(prob_grads * probs, axis=-1, keepdims=True))
    )
    logit_ref[...] = logit_low
    moe_grad = dot(low(routing), grad_coming) + row_product(logit_low, extra)
    normed, scale = norm_parts(middle)
    moe_ref[...] = low(normed * gains[2] + gains[3])
    vector_ref[2:3] = jnp.sum(moe_grad * normed, axis=0, keepdims=True)
    vector_ref[3:4] = jnp.sum(moe_grad, axis=0, keepdims=True)
    grad_middle = upstream + norm_backward(moe_grad, normed, scale, gains[2])
    branch_low = low(grad_middle)
    branch_ref[...] = branch_low
    grad_mixed = low(row_product(branch_low, a_ref[:, 3 * D : 4 * D]))
    lanes = lax.broadcasted_iota(jnp.int32, (SEQ, 2 * HEAD_DIM), 1)
    for head in range(HEADS):
        start = 2 * HEAD_DIM * (head // 2)
        stop = start + 2 * HEAD_DIM
        query = qkv_ref[0, :, start:stop]
        keys = qkv_ref[0, :, D + start : D + stop]
        values = qkv_ref[0, :, 2 * D + start : 2 * D + stop]
        here = (lanes < HEAD_DIM) if head % 2 == 0 else (lanes >= HEAD_DIM)
        score_ref[head] = row_product(jnp.where(here, query, 0), keys) * HEAD_DIM ** (-0.5)
        slope_ref[head] = row_product(jnp.where(here, grad_mixed[:, start:stop], 0), values)
    weights = softmax_rows(score_ref[...])
    weight_ref[...] = low(weights)
    slopes = slope_ref[...]
    grad_score_ref[...] = low(
        weights * (slopes - jnp.sum(slopes * weights, axis=-1, keepdims=True))
    )
    for pair in range(HEADS // 2):
        start = 2 * HEAD_DIM * pair
        stop = start + 2 * HEAD_DIM
        query = qkv_ref[0, :, start:stop]
        keys = qkv_ref[0, :, D + start : D + stop]
        grad_here = grad_mixed[:, start:stop]
        results = []
        for side in range(2):
            grad_scores = grad_score_ref[2 * pair + side]
            results.append(
                (
                    dot(grad_scores, keys) * HEAD_DIM ** (-0.5),
                    column_sum(grad_scores, query) * HEAD_DIM ** (-0.5),
                    column_sum(weight_ref[2 * pair + side], grad_here),
                )
            )
        for part in range(3):
            joined_ref[:, part * D + start : part * D + stop] = low(
                jnp.where(lanes < HEAD_DIM, results[0][part], results[1][part])
            )
    grad_normed = row_product(joined_ref[...], a_ref[:, : 3 * D])
    normed, scale = norm_parts(inputs)
    normed_ref[...] = low(normed * gains[0] + gains[1])
    vector_ref[4:8] = jnp.zeros((4, D), jnp.float32)
    vector_ref[0:1] = jnp.sum(grad_normed * normed, axis=0, keepdims=True)
    vector_ref[1:2] = jnp.sum(grad_normed, axis=0, keepdims=True)
    grad_ref[0, 0] = grad_middle + norm_backward(grad_normed, normed, scale, gains[0])


def weight_sums_kernel(experts, after_ref, core_ref, mixed_ref, *refs):
    own_ref, other_ref, token_ref = refs[-3:]
    token_ref[...] = jnp.zeros_like(token_ref)
    steps = [refs[6 * i : 6 * i + 6] for i in range(MB)]
    held, block, _ = own_ref.shape
    first_core = core_ref[0] == 0

    def write(total, start):
        stop = start + total.shape[1]
        pairs = total.reshape(held, 2, block, total.shape[1])
        even, odd = (pairs[:, 0], pairs[:, 1])
        own_ref[:, :, start:stop] = jnp.where(first_core, even, odd)
        other_ref[:, :, start:stop] = low(jnp.where(first_core, odd, even))

    for part in range(3):
        total = sum(column_sum(s[0][...], s[1][:, part * D : part * D + D]) for s in steps)
        write(total, part * D)
    write(sum(column_sum(mixed_ref[i], s[2][...]) for i, s in enumerate(steps)), 3 * D)
    vectors = sum(s[5][...] for s in steps)
    vectors = jnp.concatenate(
        [
            jnp.zeros((experts, D), jnp.float32),
            vectors,
            jnp.zeros((128 - experts - vectors.shape[0], D), jnp.float32),
        ],
        axis=0,
    )
    write(sum(column_sum(s[3][...], s[4][...]) for s in steps) + vectors.T, 4 * D)


def gelu_parts(values):
    raised = jnp.exp(-0.5 * values * values)
    root = 1.0 / (1.0 + (0.3275911 * 0.5**0.5) * jnp.abs(values))
    tail = 1.061405429 * root - 1.453152027
    tail = tail * root + 1.421413741
    tail = tail * root - 0.284496736
    tail = tail * root + 0.254829592
    tail = 0.5 * tail * root * raised
    return jnp.where(values >= 0.0, 1.0 - tail, tail), raised * 0.3989422804014327


def hidden_kernel(
    experts,
    expert_ref,
    rows_ref,
    up_ref,
    router_ref,
    weight_ref,
    bias_ref,
    hidden_ref,
    slope_ref,
    grad_ref,
    sum_ref,
):
    count, padded = rows_ref.shape[:2]
    units = weight_ref.shape[2]
    rows = low(wide(rows_ref[...]).reshape(count * padded, D))
    probs = masked_softmax(dot(rows, router_ref[...]), experts)
    lanes = lax.broadcasted_iota(jnp.int32, probs.shape, 1)
    gate = jnp.sum(jnp.where(lanes == expert_ref[0], probs, 0.0), axis=-1, keepdims=True)
    grad = low(gate * wide(up_ref[...]).reshape(count * padded, D))
    grad_ref[...] = grad

    @pl.when(pl.program_id(0) == 0)
    def _():
        sum_ref[...] = jnp.zeros_like(sum_ref)

    sum_ref[0:1] += jnp.sum(wide(grad), axis=0, keepdims=True)
    for side in range(2):
        values = dot(rows, weight_ref[side]) + bias_ref[:, side * units : (side + 1) * units]
        area, density = gelu_parts(values)
        hidden_ref[side] = low(values * area)
        slope_ref[side] = low(area + values * density)


def result_kernel(skipped, *refs):
    (
        hidden_ref,
        slope_ref,
        grad_ref,
        out_ref,
        in_ref,
        bias_ref,
        back_ref,
        pre_ref,
        sum_ref,
    ) = refs[skipped:]
    count, _, padded, _ = back_ref.shape
    units = in_ref.shape[2]

    @pl.when(pl.program_id(0) == 0)
    def _():
        sum_ref[...] = jnp.zeros_like(sum_ref)

    out_term = dot(hidden_ref[0], out_ref[0]) + dot(hidden_ref[1], out_ref[1]) + bias_ref[...]
    back_ref[:, 0] = low(out_term.reshape(count, padded, D))
    grad_term = None
    for side in range(2):
        pre = low(row_product(grad_ref[...], out_ref[side]) * wide(slope_ref[side]))
        pre_ref[side] = pre
        sum_ref[0:1, side * units : (side + 1) * units] += jnp.sum(
            wide(pre), axis=0, keepdims=True
        )
        term = row_product(pre, in_ref[side])
        grad_term = term if grad_term is None else grad_term + term
    back_ref[:, 1] = low(grad_term.reshape(count, padded, D))


def split(values):
    high = low(values)
    return high, low(values - wide(high))


def split_dot(left, right, dims):
    def one(a, b):
        return lax.dot_general(a, b, (dims, ((), ())), preferred_element_type=jnp.float32)

    return one(left[0], right[0]) + (one(left[0], right[1]) + one(left[1], right[0]))


def turn_kernel(along_rows, rate, skipped, *refs):
    refs = refs[skipped:]
    gradient_ref, weight_ref, first_ref, second_ref, stat_ref, basis_ref = refs[:6]
    first_out, second_out, weight_out, copy_out, stat_out, stretched_out = refs[-6:]
    gradient = gradient_ref[...]
    basis = basis_ref[0, 0]
    basis_parts = split(basis)
    if along_rows:
        turned = column_sum(basis_parts[0], gradient) + column_sum(basis_parts[1], gradient)
        outer = row_product(gradient, gradient)
    else:
        turned = dot(gradient, basis_parts[0]) + dot(gradient, basis_parts[1])
        outer = column_sum(gradient, gradient)
    first_new, second_new, step = moment_step(turned, first_ref[0], second_ref[0])
    first_out[0] = first_new
    second_out[0] = second_new
    step_parts = split(step)
    if along_rows:
        returned = split_dot(basis_parts, step_parts, ((1,), (0,)))
    else:
        returned = split_dot(step_parts, basis_parts, ((1,), (1,)))
    weight = weight_ref[0]
    weight_new = weight - rate * (returned + DECAY_RATE * weight)
    weight_out[0] = weight_new
    copy_out[0] = low(weight_new)
    stat_new = STAT_DECAY * stat_ref[0, 0] + (1.0 - STAT_DECAY) * outer
    stat_out[0, 0] = stat_new
    stretched_out[...] = mm(stat_new, basis)


def dense_update_kernel(kept_ref, received_ref, *refs):
    inputs, outputs = (refs[:9], refs[9:])
    gradient = kept_ref[...] + wide(received_ref[...])
    extra = gradient[:, 4 * D :].T
    experts = inputs[3].shape[0]
    gradients = (gradient[:, : 4 * D], extra[:experts], extra[experts : experts + 4])
    rates = ((RATE_DENSE, DECAY_RATE), (RATE_DENSE, DECAY_RATE), (RATE_NORMS, 0.0))
    place = 0
    for kind in range(3):
        weight, first, second = (r[...] for r in inputs[3 * kind : 3 * kind + 3])
        first_new, second_new, weight_new = adam_update(
            weight, gradients[kind], first, second, *rates[kind]
        )
        outputs[place][...] = first_new
        outputs[place + 1][...] = second_new
        outputs[place + 2][...] = weight_new
        place += 3
        if kind < 2:
            outputs[place][...] = low(weight_new)
            place += 1


def row_sums_kernel(*refs):
    total = sum(column_sum(refs[i][...], refs[MB + i][...]) for i in range(MB))
    refs[-1][...] = low(total)


def swap(values, axis, distance):
    size = lax.axis_size(axis)
    return lax.ppermute(values, axis, [(i, i ^ distance) for i in range(size)])


def across(values):
    size = lax.axis_size(TENSOR)
    return lax.ppermute(values, TENSOR, [(i, (i + size // 2) % size) for i in range(size)])


def ordered(bit, mine, other):
    return jnp.where(bit == 0, jnp.stack([mine, other]), jnp.stack([other, mine]))


def gather_tensor(shard):
    tensors, tensor = (lax.axis_size(TENSOR), lax.axis_index(TENSOR))
    block = shard[None]
    distance = 1
    while distance < tensors:
        other = swap(block, TENSOR, distance)
        block = ordered((tensor // distance) % 2, block, other).reshape(-1, *shard.shape)
        distance *= 2
    return block


def gather_experts(block, beside, released, waiting):
    experts, tensors = (lax.axis_size(EXPERT), lax.axis_size(TENSOR))
    expert = lax.axis_index(EXPERT)
    columns = block.shape[-1]
    block = block[None]
    distance = 2
    while distance < experts // 4:
        other = swap(block, EXPERT, distance)
        block = ordered((expert // distance) % 2, block, other).reshape(-1, *block.shape[1:])
        distance *= 2
    near, far = (distance, 2 * distance)
    middle = tensors // 2
    from_near, from_far = (swap(block, EXPERT, near), swap(block, EXPERT, far))
    corner = jnp.concatenate(
        [swap(from_far[:, :middle], EXPERT, near), swap(from_near[:, middle:], EXPERT, far)],
        axis=1,
    )
    corner, beside, released, waiting = lax.optimization_barrier(
        (corner, beside, released, waiting)
    )
    pieces = (block, from_near, from_far, corner)
    crossed = [swap(piece, EXPERT, 1) for piece in pieces]
    near_bit, far_bit = ((expert // near) % 2, (expert // far) % 2)

    def arranged(four):
        return ordered(
            far_bit,
            ordered(near_bit, four[0], four[1]),
            ordered(near_bit, four[2], four[3]),
        ).reshape(-1, *block.shape[1:])

    whole = ordered(expert % 2, arranged(pieces), arranged(crossed))
    whole = jnp.moveaxis(whole, 0, 1)
    return whole.reshape(-1, columns), beside, across(released), waiting


def scatter_sums(held, sending):
    experts, tensors = (lax.axis_size(EXPERT), lax.axis_size(TENSOR))
    expert, tensor = (lax.axis_index(EXPERT), lax.axis_index(TENSOR))
    columns = held.shape[2]

    def pick(values, index, axis=0):
        return lax.dynamic_index_in_dim(values, index, axis, False)

    held = held + wide(swap(sending, EXPERT, 1))
    stages = [held]
    near, far = (experts // 4, experts // 2)
    near_bit, far_bit = ((expert // near) % 2, (expert // far) % 2)
    held = held.reshape(4, experts // 8, tensors, -1, columns)
    place = 2 * far_bit + near_bit
    own, to_near, to_far, to_corner = (
        pick(held, place),
        pick(held, place ^ 1),
        pick(held, place ^ 2),
        pick(held, place ^ 3),
    )
    middle = tensors // 2
    passed_near = swap(low(to_corner[:, :middle]), EXPERT, near)
    passed_far = swap(low(to_corner[:, middle:]), EXPERT, far)
    to_far = jnp.concatenate([to_far[:, :middle] + wide(passed_near), to_far[:, middle:]], axis=1)
    to_near = jnp.concatenate([to_near[:, :middle], to_near[:, middle:] + wide(passed_far)], axis=1)
    stages.append(to_near)
    held = (
        own
        + wide(swap(low(to_near), EXPERT, near))
        + wide(swap(low(to_far), EXPERT, far))
    )
    distance = experts // 8
    while distance >= 2:
        bit = (expert // distance) % 2
        halves = held.reshape(2, -1, *held.shape[1:])
        held = pick(halves, bit) + wide(swap(low(pick(halves, 1 - bit)), EXPERT, distance))
        distance //= 2
    stages.append(held)
    held = held.reshape(tensors, -1, columns)
    distance = tensors // 2
    while distance >= 1:
        bit = (tensor // distance) % 2
        halves = held.reshape(2, -1, *held.shape[1:])
        kept = pick(halves, bit)
        received = swap(low(pick(halves, 1 - bit)), TENSOR, distance)
        if distance > 1:
            held = kept + wide(received)
        distance //= 2
    stages.append(kept)
    return kept.reshape(-1, columns), received.reshape(-1, columns), stages


def soap_turn(along_rows, rate, at, token, gradient, state, statistics, earlier):
    weight, first, second = state
    statistic = statistics[0]
    f32 = jnp.float32
    if along_rows:
        deep = pl.BlockSpec((1, BLK, D), lambda i: (0, at, 0))
    else:
        deep = pl.BlockSpec((1, D, BLK), lambda i: (0, 0, at))
    square = pl.BlockSpec((1, 1, BLK, BLK), lambda i: (0, at, 0, 0))
    anywhere = pl.BlockSpec(memory_space=pl.ANY)
    return vmem_call(
        partial(turn_kernel, along_rows, rate, len(token)),
        8,
        grid=(1,),
        in_specs=[anywhere] * len(token)
        + [full_block(gradient.shape)]
        + [deep] * 3
        + [square] * 2
        + [anywhere] * len(earlier),
        out_specs=[deep] * 4 + [square, full_block((BLK, BLK))],
        out_shape=[jax.ShapeDtypeStruct(weight.shape, f32)] * 3
        + [
            jax.ShapeDtypeStruct(weight.shape, jnp.bfloat16),
            jax.ShapeDtypeStruct(statistic.shape, f32),
            jax.ShapeDtypeStruct((BLK, BLK), f32),
        ],
        input_output_aliases={6 + len(token) + i: i for i in range(len(earlier))},
    )(*token, gradient, *state, *statistics, *earlier)


def row_sums(left, right, at, left_paired):
    rows, width = left[0].shape[-2:]
    height, columns = (BLK, right[0].shape[-1]) if left_paired else (width, BLK)
    paired = pl.BlockSpec((None, rows, BLK), lambda i: (i, 0, at))
    plain = full_block((rows, columns if left_paired else width))
    return vmem_call(
        row_sums_kernel,
        5,
        grid=(2,),
        in_specs=[paired if left_paired else plain] * MB
        + [plain if left_paired else paired] * MB,
        out_specs=pl.BlockSpec((None, height, columns), lambda i: (i, 0, 0)),
        out_shape=jax.ShapeDtypeStruct((2, height, columns), jnp.bfloat16),
    )(*left, *right)


def per_device(
    patches,
    cotangent,
    expert_ids,
    slots,
    attn_weights,
    attn_first,
    attn_second,
    router_weights,
    router_first,
    router_second,
    norm_params,
    norm_first,
    norm_second,
    w_in,
    w_in_first,
    w_in_second,
    w_in_stat,
    w_in_basis,
    w_out,
    w_out_first,
    w_out_second,
    w_out_stat,
    w_out_basis,
    b_in,
    b_in_first,
    b_in_second,
    b_out,
    b_out_first,
    b_out_second,
):
    tokens_here = SEQ
    expert_total = router_weights.shape[1]
    capacity = (105 * TOPK * tokens_here + 100 * expert_total - 1) // (100 * expert_total)
    padded = 8 * ((capacity + 7) // 8)
    experts, tensors = (lax.axis_size(EXPERT), lax.axis_size(TENSOR))
    expert, tensor = (lax.axis_index(EXPERT), lax.axis_index(TENSOR))
    half = tensors // 2
    members = expert_total * half
    units = w_in.shape[2]
    shard_columns = b_out.shape[1]
    columns = 4 * D + 128
    bf16, f32 = (jnp.bfloat16, jnp.float32)
    shape = jax.ShapeDtypeStruct
    pairs = [[i, i + half] for i in range(half)]
    groups = [
        [e * tensors + z for e in range(experts) for z in range(h * half, (h + 1) * half)]
        for h in range(2)
    ]

    def exchange(values):
        return lax.all_to_all(values, BOTH, 0, 0, axis_index_groups=groups, tiled=True)

    packed = jnp.concatenate(
        [
            low(attn_weights),
            low(router_weights),
            low(norm_params).T,
            jnp.zeros((attn_weights.shape[0], 128 - expert_total - 4), bf16),
        ],
        axis=1,
    )
    in_own, out_own = (low(w_in[0]), low(w_out[0]))
    b_in_low, b_out_low = (low(b_in), low(b_out))
    peer_bias = across(jnp.concatenate([b_in_low, b_out_low], axis=1))
    chosen = expert_ids.reshape(MB, tokens_here, TOPK)
    placed = slots.reshape(MB, tokens_here, TOPK)
    target = jnp.where(placed < capacity, chosen * padded + placed, -1)
    up_sent = vmem_call(
        dispatch_kernel,
        4,
        grid=(1,),
        in_specs=[full_block(target.shape), full_block(cotangent.shape)],
        out_specs=full_block((expert_total, half, MB, padded, D)),
        out_shape=shape((expert_total, half, MB, padded, D), bf16),
    )(target, cotangent)
    first_stage, peer_bias, sent_first = lax.optimization_barrier(
        (gather_tensor(packed), peer_bias, in_own[: 5 * D // 8])
    )
    out_pair = lax.all_gather(out_own, TENSOR, axis_index_groups=pairs)
    gathered, in_first, in_second, up_sent = gather_experts(
        first_stage, across(sent_first), in_own[5 * D // 8 :], up_sent
    )
    up_all = exchange(up_sent.reshape(members, MB, padded, D))
    upper = tensor >= half
    peer_in = peer_bias[:, :units]
    bias_in = wide(
        jnp.where(
            upper,
            jnp.concatenate([peer_in, b_in_low], axis=1),
            jnp.concatenate([b_in_low, peer_in], axis=1),
        )
    )
    bias_out = jnp.zeros((1, D), f32)
    own_place = tensor * shard_columns
    peer_place = ((tensor + half) % tensors) * shard_columns
    bias_out = lax.dynamic_update_slice(bias_out, wide(b_out_low), (0, own_place))
    bias_out = lax.dynamic_update_slice(bias_out, wide(peer_bias[:, units:]), (0, peer_place))
    image = pl.BlockSpec((1, 1, SEQ, D), lambda i: (i, 0, 0, 0))

    def per_step(*tail):
        return pl.BlockSpec((1, *tail), lambda i: (i,) + (0,) * len(tail))

    *sent, qkv, mixed, middle, probs = vmem_call(
        partial(attention_kernel, expert_total),
        11,
        grid=(MB,),
        in_specs=[image, per_step(SEQ, TOPK), full_block((D, columns))],
        out_specs=[
            *[full_block((expert_total, half, padded, D))] * MB,
            per_step(SEQ, 3 * D),
            per_step(SEQ, D),
            per_step(SEQ, D),
            per_step(SEQ, 128),
        ],
        out_shape=[
            *[shape((expert_total, half, padded, D), bf16)] * MB,
            shape((MB, SEQ, 3 * D), bf16),
            shape((MB, SEQ, D), bf16),
            shape((MB, SEQ, D), f32),
            shape((MB, SEQ, 128), f32),
        ],
        scratch_shapes=[pltpu.VMEM((HEADS, SEQ, SEQ), f32), pltpu.VMEM((HEADS, SEQ, SEQ), bf16)],
    )(patches, target, gathered)
    earlier, up_all, in_second = lax.optimization_barrier((sent[0], up_all, in_second))
    in_peer = jnp.concatenate([in_first, in_second], axis=0)
    in_pair = jnp.where(upper, jnp.stack([in_peer, in_own]), jnp.stack([in_own, in_peer]))
    arrived = [exchange(earlier.reshape(members, padded, D))]
    later, arrived[0] = lax.optimization_barrier((sent[1], arrived[0]))
    arrived.append(exchange(later.reshape(members, padded, D)))
    count = max(
        n
        for n in range(1, members + 1)
        if members % n == 0 and n * padded <= ROW_TILE and (n * padded) % 16 == 0
    )
    tile = count * padded
    total_rows = members * padded
    tiles = members // count

    def rows_of(width):
        return pl.BlockSpec((tile, width), lambda i: (i, 0))

    expert_scalar = jnp.reshape(expert, (1,)).astype(jnp.int32)
    in_smem = pl.BlockSpec(memory_space=pltpu.SMEM)
    anywhere = pl.BlockSpec(memory_space=pl.ANY)
    both_rows = pl.BlockSpec((2, tile, units), lambda i: (0, i, 0))
    both_shape = shape((2, total_rows, units), bf16)
    hidden = []
    for step in range(MB):
        hidden.append(
            vmem_call(
                partial(hidden_kernel, expert_total),
                12,
                grid=(tiles,),
                in_specs=[
                    in_smem,
                    pl.BlockSpec((count, padded, D), lambda i: (i, 0, 0)),
                    pl.BlockSpec((count, None, padded, D), lambda i, step=step: (i, step, 0, 0)),
                    pl.BlockSpec((D, 128), lambda i: (0, 4 * D // 128)),
                    full_block((2, D, units)),
                    full_block((1, 2 * units)),
                ],
                out_specs=[both_rows] * 2 + [rows_of(D), full_block((8, D))],
                out_shape=[both_shape] * 2
                + [shape((total_rows, D), bf16), shape((8, D), f32)],
            )(expert_scalar, arrived[step], up_all, gathered, in_pair, bias_in)
        )
    blocks = units // BLK
    row_grads = [h[2] for h in hidden]
    sum_out = [row_sums([h[0] for h in hidden], row_grads, at, True) for at in range(blocks)]
    results = []
    for step in range(MB):
        before = [] if step == 0 else sum_out
        results.append(
            vmem_call(
                partial(result_kernel, len(before)),
                12,
                grid=(tiles,),
                in_specs=[anywhere] * len(before)
                + [both_rows] * 2
                + [
                    rows_of(D),
                    full_block((2, units, D)),
                    full_block((2, D, units)),
                    full_block((1, D)),
                ],
                out_specs=[
                    pl.BlockSpec((count, 2, padded, D), lambda i: (i, 0, 0, 0)),
                    both_rows,
                    full_block((8, 2 * units)),
                ],
                out_shape=[
                    shape((members, 2, padded, D), bf16),
                    both_shape,
                    shape((8, 2 * units), f32),
                ],
            )(*before, *hidden[step][:3], out_pair, in_pair, bias_out)
        )
    flat_rows = [rows.reshape(total_rows, D) for rows in arrived]
    sum_in = [row_sums(flat_rows, [r[1] for r in results], at, False) for at in range(blocks)]

    def shared(sums):
        return lax.psum_scatter(sums, TENSOR, axis_index_groups=pairs)

    grads_out = [shared(sums) for sums in sum_out]
    grads_in = [shared(sums) for sums in sum_in]
    returned = [exchange(r[0]) for r in results]
    sum_bin = sum(r[2][:1] for r in results)
    sum_bout = sum(h[3][:1] for h in hidden)
    bias_sums = jnp.concatenate(
        [
            jnp.where(upper, sum_bin[:, :units], sum_bin[:, units:]),
            lax.dynamic_slice_in_dim(sum_bout, peer_place, shard_columns, 1),
        ],
        axis=1,
    )
    bias_other = across(bias_sums)
    backward = []
    tokens = [sum_in]
    for step in range(MB):
        first = step == 0
        here = pl.BlockSpec((1, 1, SEQ, D), lambda i, step=step: (step, 0, 0, 0))

        def of_step(*tail, step=step):
            return pl.BlockSpec((1, *tail), lambda i: (step,) + (0,) * len(tail))

        back = returned[step].reshape(expert_total, half, 2, padded, D)
        outs = [
            (shape(patches.shape, bf16), here),
            (shape(patches.shape, f32), here),
            (shape((SEQ, D), bf16), full_block((SEQ, D))),
            (shape((SEQ, 3 * D), bf16), full_block((SEQ, 3 * D))),
            (shape((SEQ, D), bf16), full_block((SEQ, D))),
            (shape((SEQ, D), bf16), full_block((SEQ, D))),
            (shape((SEQ, 128), bf16), full_block((SEQ, 128))),
            (shape((8, D), f32), full_block((8, D))),
        ]
        earlier = [] if first else list(backward[-1][:2])
        backward.append(
            vmem_call(
                partial(attention_backward_kernel, expert_total, len(tokens[step])),
        15,
                grid=(1,),
                in_specs=[anywhere] * len(tokens[step])
                + [
                    here,
                    here,
                    of_step(SEQ, TOPK),
                    full_block(back.shape),
                    of_step(SEQ, 3 * D),
                    of_step(SEQ, D),
                    of_step(SEQ, D),
                    of_step(SEQ, 128),
                    full_block((D, columns)),
                ]
                + [pl.BlockSpec(memory_space=pl.ANY)] * len(earlier),
                out_specs=[o[1] for o in outs],
                out_shape=[o[0] for o in outs],
                scratch_shapes=[pltpu.VMEM((HEADS, SEQ, SEQ), f32)] * 2
                + [pltpu.VMEM((HEADS, SEQ, SEQ), bf16)] * 2,
                input_output_aliases={}
                if first
                else {9 + len(tokens[step]): 0, 10 + len(tokens[step]): 1},
            )(
                *tokens[step],
                patches,
                cotangent,
                target,
                back,
                qkv,
                mixed,
                middle,
                probs,
                gathered,
                *earlier,
            )
        )
        if first:
            out_turned = [
                soap_turn(
                    True,
                    RATE_OUTPUT,
                    0,
                    [backward[0][6]],
                    grads_out[0],
                    (w_out, w_out_first, w_out_second),
                    (w_out_stat, w_out_basis),
                    [],
                )
            ]
            tokens.append([out_turned[0][5]])
    core_scalar = jnp.reshape(expert % 2, (1,)).astype(jnp.int32)
    block_rows = tensors * attn_weights.shape[0]
    flat_steps = [value for b in backward for value in b[2:]]
    core_shape = (experts // 2, block_rows, columns)
    held, sending, token = vmem_call(
        partial(weight_sums_kernel, expert_total),
        8,
        grid=(1,),
        in_specs=[anywhere, in_smem] + [full_block(v.shape) for v in (mixed, *flat_steps)],
        out_specs=[full_block(core_shape)] * 2 + [full_block((8, 128))],
        out_shape=[shape(core_shape, f32), shape(core_shape, bf16), shape((8, 128), f32)],
    )(b_in_low, core_scalar, mixed, *flat_steps)
    kept, received, stages = scatter_sums(held, sending)
    dense = [shape(attn_weights.shape, f32)] * 3 + [shape(attn_weights.shape, bf16)]
    turned_shape = router_weights.shape[::-1]
    routers = [shape(turned_shape, f32)] * 3 + [shape(turned_shape, bf16)]
    norms = [shape(norm_params.shape, f32)] * 3
    states = (
        kept,
        received,
        attn_weights,
        attn_first,
        attn_second,
        router_weights.T,
        router_first.T,
        router_second.T,
        norm_params,
        norm_first,
        norm_second,
    )
    updated_shapes = dense + routers + norms
    updated = vmem_call(
        dense_update_kernel,
        3,
        grid=(1,),
        in_specs=[full_block(v.shape) for v in states],
        out_specs=[full_block(v.shape) for v in updated_shapes],
        out_shape=updated_shapes,
    )(*states)
    for at in range(1, blocks):
        out_turned.append(
            soap_turn(
                True,
                RATE_OUTPUT,
                at,
                [token],
                grads_out[at],
                (w_out, w_out_first, w_out_second),
                (w_out_stat, w_out_basis),
                out_turned[-1][:5],
            )
        )
    in_turned = []
    for at in range(blocks):
        in_turned.append(
            soap_turn(
                False,
                RATE_INPUT,
                at,
                [out_turned[-1][5], stages[0]] if at == 0 else [in_turned[-1][5], stages[2]],
                grads_in[at],
                (w_in, w_in_first, w_in_second),
                (w_in_stat, w_in_basis),
                in_turned[-1][:5] if at > 0 else [],
            )
        )
    w_out_basis_new, w_in_basis_new = renew(
        stages[3:], [turned[5] for turned in out_turned], [turned[5] for turned in in_turned]
    )
    bias_other, w_in_basis_new = lax.optimization_barrier((bias_other, w_in_basis_new))
    w_in_results = (*in_turned[-1][:5], w_in_basis_new)
    w_out_results = (*out_turned[-1][:5], w_out_basis_new)
    own_bin = jnp.where(upper, sum_bin[:, units:], sum_bin[:, :units])
    grad_bin = own_bin + bias_other[:, :units]
    grad_bout = (
        lax.dynamic_slice_in_dim(sum_bout, own_place, shard_columns, 1) + bias_other[:, units:]
    )
    bin_first_new, bin_second_new, bin_new = adam_update(
        b_in, grad_bin, b_in_first, b_in_second, RATE_BIASES, 0.0
    )
    bout_first_new, bout_second_new, bout_new = adam_update(
        b_out, grad_bout, b_out_first, b_out_second, RATE_OFFSETS, 0.0
    )
    return (
        *backward[-1][:2],
        *updated[:4],
        *(value.T for value in updated[4:8]),
        *updated[8:],
        *w_in_results,
        *w_out_results,
        bin_first_new,
        bin_second_new,
        bin_new,
        bout_first_new,
        bout_second_new,
        bout_new,
    )


def solution(mesh):
    tokens = P(None, BOTH, None, None)
    rows = P(BOTH, None)
    columns = P(None, BOTH)
    first_layer = P(EXPERT, None, TENSOR)
    second_layer = P(EXPERT, TENSOR, None)
    blocks = P(EXPERT, TENSOR, None, None)
    biases = P(EXPERT, TENSOR)
    in_specs = (
        (tokens,) * 4
        + (rows,) * 6
        + (columns,) * 3
        + (first_layer,) * 3
        + (blocks,) * 2
        + (second_layer,) * 3
        + (blocks,) * 2
        + (biases,) * 6
    )
    out_specs = (
        (tokens,) * 2
        + (rows,) * 8
        + (columns,) * 3
        + (first_layer,) * 4
        + (blocks,) * 2
        + (second_layer,) * 4
        + (blocks,) * 2
        + (biases,) * 6
    )
    return jax.shard_map(
        per_device, mesh=mesh, in_specs=in_specs, out_specs=out_specs, check_vma=False
    )
```
